32 devices in a mesh: fsdp: 8 (over y, x, core), tp: 4 (over z).
Axes of the slice: x: 2, y: 2, z: 4, core: 2. Of those that a mesh axis runs over, the one named last changes fastest.
Arguments:
- hidden_in: bfloat16 [4096, 2048], P(('fsdp', 'tp')), may hold values from -6 to 6
- cotangent: bfloat16 [4096, 2048], P(('fsdp', 'tp')), may hold values from -6 to 6
- segment_ids: int32 [8, 512], P('fsdp'), may hold values from 0 to 3, never falling along the last dimension, each value on 1 to 256 neighbouring positions
- adapter_set: int32 [8], P('fsdp'), may hold values from 0 to 7
- qkv_weight: bfloat16 [3, 2048, 2048], P(None, 'fsdp', 'tp'), may hold values from -0.125 to 0.125
- qkv_bias: bfloat16 [2, 2048], P(None, 'tp'), may hold values from -3 to 3
- proj_weight: bfloat16 [2048, 2048], P('tp', 'fsdp'), may hold values from -1.5 to 1.5
- proj_bias: bfloat16 [2048], replicated, may hold values from -3 to 3
- up_weight: bfloat16 [2048, 8192], P('fsdp', 'tp'), may hold values from -0.125 to 0.125
- up_bias: bfloat16 [8192], P('tp'), may hold values from -3 to 3
- down_weight: bfloat16 [8192, 2048], P('tp', 'fsdp'), may hold values from -0.0625 to 0.0625
- down_bias: bfloat16 [2048], replicated, may hold values from -3 to 3
- norm_gain: bfloat16 [2, 2048], replicated, may hold values from 0.5 to 1.5
- norm_bias: bfloat16 [2, 2048], replicated, may hold values from -3 to 3
- qkv_adapt_in: bfloat16 [3, 8, 2048, 16], replicated, may hold values from -0.125 to 0.125
- qkv_adapt_out: bfloat16 [3, 8, 16, 2048], P(None, None, None, 'tp'), may hold values from -0.75 to 0.75
- attn_adapt_in: bfloat16 [8, 2048, 16], P(None, 'tp'), may hold values from -1.5 to 1.5
- attn_adapt_out: bfloat16 [8, 16, 2048], replicated, may hold values from -0.75 to 0.75
- up_adapt_in: bfloat16 [8, 2048, 16], replicated, may hold values from -0.125 to 0.125
- up_adapt_out: bfloat16 [8, 16, 8192], P(None, None, 'tp'), may hold values from -0.75 to 0.75
- down_adapt_in: bfloat16 [8, 8192, 16], P(None, 'tp'), may hold values from -0.0625 to 0.0625
- down_adapt_out: bfloat16 [8, 16, 2048], replicated, may hold values from -0.75 to 0.75
Outputs:
- layer_out: float32 [4096, 2048], P(('fsdp', 'tp'))
- grad_input: float32 [4096, 2048], P(('fsdp', 'tp'))
- grad_qkv_in: float32 [3, 8, 2048, 16], replicated
- grad_qkv_out: float32 [3, 8, 16, 2048], P(None, None, None, 'tp')
- grad_attn_in: float32 [8, 2048, 16], P(None, 'tp')
- grad_attn_out: float32 [8, 16, 2048], replicated
- grad_up_in: float32 [8, 2048, 16], replicated
- grad_up_out: float32 [8, 16, 8192], P(None, None, 'tp')
- grad_down_in: float32 [8, 8192, 16], P(None, 'tp')
- grad_down_out: float32 [8, 16, 2048], replicated
The draws below stay inside these ranges and needn't reach their ends.
Inputs may be any that keep to these rules, and one draw needn't show every extreme that they name: `segment_ids`: within a sequence the numbers never fall; each of the 4 documents holds 1 to 256 tokens and one holds exactly 256.
All inputs are finite; a program needn't handle non-finite values.
Results may differ from the reference program's by a relative error of at most 0.018.
Values may be sent and summed in bfloat16 or wider, within the bound.
A program may use at most 192 MiB of HBM per device.

```python
import math
import jax
import jax.numpy as jnp
import numpy as np
from jax import lax

D = 2048
HEADS = 16
HEAD = 128
FF = 8192
RANK = 16
SETS = 8
TOK_DEV = 512
DOCS = 4
DOC_MOST = 256
SEQS = 8
TOKENS = 4096


def set_ends(entries, own_key, low, top_value):
    spot = [jax.random.randint(jax.random.fold_in(own_key, axis), (), 0, length) for axis, length in enumerate(entries.shape)]
    longest = entries.shape.index(max(entries.shape))
    next_to = spot[:longest] + [(spot[longest] + 1) % entries.shape[longest]] + spot[longest + 1:]
    return entries.at[tuple(spot)].set(low).at[tuple(next_to)].set(top_value)


def block_levels(own_key, shape, shards, least, high):
    loudness, own = 1.0, jax.random.fold_in(own_key, 6)
    for dim, shards_of in shards:
        steps = jnp.exp(jax.random.uniform(jax.random.fold_in(own, dim), (shards_of,), jnp.float32, least / len(shards), high / len(shards)))
        loudness = loudness * jnp.repeat(steps, shape[dim] // shards_of).reshape([-1 if axis == dim else 1 for axis in range(len(shape))])
    return loudness


def length_profile(count, total, most, lean):
    portions = [(1 << 20) // math.isqrt(rank ** lean) + 1 for rank in range(2, count + 1)]
    rest, holding = total - most - (count - 1), [1] * (count - 1)
    while rest > 0:
        free = [i for i in range(count - 1) if holding[i] < most]
        mass, left = sum([portions[i] for i in free]), rest
        for i in free:
            addition = min(most - holding[i], max(1, left * portions[i] // mass), rest)
            holding[i] = holding[i] + addition
            rest = rest - addition
    return np.array([most] + holding)


def uneven_parts(stream_key, number_of, total, most, skew):
    if number_of == 2:
        one = jax.random.randint(stream_key, (), max(1, total - most), min(most, total - 1) + 1)
        return jnp.stack([one, total - one])
    lengths = jnp.asarray(length_profile(number_of, total, most, skew), jnp.int32)
    twos = (number_of - 1) // 2
    source_of, sink = lengths[1:1 + 2 * twos:2], lengths[2:2 + 2 * twos:2]
    slack = jnp.minimum(source_of - 1, most - sink)
    passed = jax.random.randint(jax.random.fold_in(stream_key, 1), (twos,), 0, 1 << 20) % (slack + 1)
    lengths = lengths.at[1:1 + 2 * twos:2].set(source_of - passed).at[2:2 + 2 * twos:2].set(sink + passed)
    return lengths[jax.random.permutation(jax.random.fold_in(stream_key, 2), number_of)]


def bell_draw(own_key, shape, scale, bound, cuts=(), kind=jnp.bfloat16):
    level = block_levels(own_key, shape, cuts, -0.22, 0.18) if cuts else 1.0
    array = jax.random.normal(own_key, shape, jnp.float32) * scale * level
    return jnp.minimum(jnp.maximum(array, -bound), bound).astype(kind)


def setup_inputs(seed: int = 0) -> dict:
    splits = jax.random.split(jax.random.key(seed), 23)
    hidden_in = bell_draw(splits[0], (TOKENS, D), 1.0, 6.0, ((0, 32),))
    cotangent = bell_draw(splits[1], (TOKENS, D), 1.0, 6.0, ((0, 32),))
    segment_ids = jax.vmap(lambda own: jnp.searchsorted(jnp.cumsum(uneven_parts(own, DOCS, TOK_DEV, DOC_MOST, 2)), jnp.arange(TOK_DEV), side="right"))(jax.random.split(splits[2], SEQS)).reshape((SEQS, TOK_DEV)).astype(jnp.int32)
    adapter_set = set_ends(jax.random.randint(splits[3], (SEQS,), 0, SETS), jax.random.fold_in(splits[3], 1), 0, SETS - 1).astype(jnp.int32)
    qkv_weight = bell_draw(splits[4], (3, D, D), D ** -0.5, 0.125, ((1, 8), (2, 4)))
    qkv_bias = bell_draw(splits[5], (2, D), 0.5, 3.0, ((1, 4),))
    proj_weight = bell_draw(splits[6], (D, D), (max(D // 128, 4)) ** -0.5, 1.5, ((0, 4), (1, 8)))
    proj_bias = bell_draw(splits[7], (D,), 0.5, 3.0)
    up_weight = bell_draw(splits[8], (D, FF), D ** -0.5, 0.125, ((0, 8), (1, 4)))
    up_bias = bell_draw(splits[9], (FF,), 0.5, 3.0, ((0, 4),))
    down_weight = bell_draw(splits[10], (FF, D), FF ** -0.5, 0.0625, ((0, 4), (1, 8)))
    down_bias = bell_draw(splits[11], (D,), 0.5, 3.0)
    norm_gain = jnp.clip(1.0 + 0.1 * jax.random.normal(splits[12], (2, D), jnp.float32), 0.5, 1.5).astype(jnp.bfloat16)
    norm_bias = bell_draw(splits[13], (2, D), 0.5, 3.0)
    qkv_adapt_in = bell_draw(splits[14], (3, SETS, D, RANK), D ** -0.5, 0.125)
    qkv_adapt_out = bell_draw(splits[15], (3, SETS, RANK, D), (4 * RANK) ** -0.5, 0.75, ((3, 4),))
    attn_adapt_in = bell_draw(splits[16], (SETS, D, RANK), (max(D // 128, 4)) ** -0.5, 1.5, ((1, 4),))
    attn_adapt_out = bell_draw(splits[17], (SETS, RANK, D), (4 * RANK) ** -0.5, 0.75)
    up_adapt_in = bell_draw(splits[18], (SETS, D, RANK), D ** -0.5, 0.125)
    up_adapt_out = bell_draw(splits[19], (SETS, RANK, FF), (4 * RANK) ** -0.5, 0.75, ((2, 4),))
    down_adapt_in = bell_draw(splits[20], (SETS, FF, RANK), FF ** -0.5, 0.0625, ((1, 4),))
    down_adapt_out = bell_draw(splits[21], (SETS, RANK, D), (4 * RANK) ** -0.5, 0.75)
    return dict(hidden_in=hidden_in, cotangent=cotangent, segment_ids=segment_ids, adapter_set=adapter_set, qkv_weight=qkv_weight, qkv_bias=qkv_bias, proj_weight=proj_weight, proj_bias=proj_bias, up_weight=up_weight, up_bias=up_bias, down_weight=down_weight, down_bias=down_bias, norm_gain=norm_gain, norm_bias=norm_bias, qkv_adapt_in=qkv_adapt_in, qkv_adapt_out=qkv_adapt_out, attn_adapt_in=attn_adapt_in, attn_adapt_out=attn_adapt_out, up_adapt_in=up_adapt_in, up_adapt_out=up_adapt_out, down_adapt_in=down_adapt_in, down_adapt_out=down_adapt_out)


@jax.custom_vjp
def low(v):
    return lax.optimization_barrier(v.astype(jnp.bfloat16)).astype(jnp.float32)

@jax.custom_vjp
def low_back(v):
    return v

def low_keep(v):
    return (low(v), None)

def low_pass(kept, grad):
    return (grad,)

def back_keep(v):
    return (v, None)

def back_low(kept, grad):
    return (low(grad),)
low.defvjp(low_keep, low_pass)
low_back.defvjp(back_keep, back_low)

def precise(left, right):
    return jnp.dot(left, right, precision=lax.Precision.HIGHEST)

def layer_norm(field_in, gain_row, shift_row):
    centre = lax.optimization_barrier(jnp.mean(field_in, axis=-1, keepdims=True))
    centred = field_in - centre
    spread = lax.optimization_barrier(jnp.mean(centred * centred, axis=-1, keepdims=True))
    return centred * lax.rsqrt(spread + 1e-05) * gain_row + shift_row

def choose_set(table, index, axis):
    return lax.dynamic_index_in_dim(table, index, axis, keepdims=False)

def attention(queries, keys, values, segments):
    seq_rows = queries.shape[0]
    block_rows = min(512, seq_rows)
    blocks = seq_rows // block_rows
    score_scale = 1.0 / math.sqrt(HEAD)
    query_blocks = queries.reshape(blocks, block_rows, HEADS, HEAD)
    seg_blocks = segments.reshape(blocks, block_rows)

    def one_block(inputs):
        query_rows, seg_rows = inputs
        raw_scores = jnp.einsum('bhe,she->hbs', query_rows, keys, precision=lax.Precision.HIGHEST) * score_scale
        raw_scores = low_back(raw_scores)
        same_doc = (seg_rows[:, None] == segments[None, :])[None]
        masked = jnp.where(same_doc, raw_scores, -1e+30)
        attn_probs = jax.nn.softmax(masked, axis=-1)
        return jnp.einsum('hbs,she->bhe', low(attn_probs), values, precision=lax.Precision.HIGHEST)
    mixed_rows = lax.map(jax.checkpoint(one_block), (query_blocks, seg_blocks))
    return mixed_rows.reshape(seq_rows, HEADS * HEAD)

def forward(hidden, qkv_in, qkv_out, attn_in, attn_out, up_in, up_out, down_in, down_out, frozen, segments, chosen):
    qkv_w, qkv_b, proj_w, proj_b, up_w, up_b, down_w, down_b, gains, shifts = frozen
    seq_rows = hidden.shape[0]
    first_q = choose_set(qkv_in, chosen, 1)
    second_q = choose_set(qkv_out, chosen, 1)
    biases = [qkv_b[0], jnp.zeros_like(qkv_b[0]), qkv_b[1]]
    projected = []
    for which in range(3):
        term = precise(hidden, qkv_w[which]) + precise(precise(hidden, first_q[which]), second_q[which]) + biases[which]
        projected.append(low_back(low(term)).reshape(seq_rows, HEADS, HEAD))
    attended = attention(projected[0], projected[1], projected[2], segments)
    attended = low_back(low(attended))
    branch = precise(attended, proj_w) + proj_b + precise(precise(attended, choose_set(attn_in, chosen, 0)), choose_set(attn_out, chosen, 0))
    branch = low_back(branch)
    normed = layer_norm(hidden + branch, gains[0], shifts[0])
    normed_low = low(normed)
    pre_act = precise(normed_low, up_w) + up_b + precise(precise(normed_low, choose_set(up_in, chosen, 0)), choose_set(up_out, chosen, 0))
    pre_act = low_back(pre_act)
    activated = low(jax.nn.gelu(pre_act, approximate=True))
    feed = precise(activated, down_w) + down_b + precise(precise(activated, choose_set(down_in, chosen, 0)), choose_set(down_out, chosen, 0))
    feed = low_back(feed)
    return layer_norm(normed + feed, gains[1], shifts[1])

def widen(array_in):
    return array_in.astype(jnp.float32)

def reference(hidden_in, cotangent, segment_ids, adapter_set, qkv_weight, qkv_bias, proj_weight, proj_bias, up_weight, up_bias, down_weight, down_bias, norm_gain, norm_bias, qkv_adapt_in, qkv_adapt_out, attn_adapt_in, attn_adapt_out, up_adapt_in, up_adapt_out, down_adapt_in, down_adapt_out):
    frozen = (widen(qkv_weight), widen(qkv_bias), widen(proj_weight), widen(proj_bias), widen(up_weight), widen(up_bias), widen(down_weight), widen(down_bias), widen(norm_gain), widen(norm_bias))
    adapters = (widen(qkv_adapt_in), widen(qkv_adapt_out), widen(attn_adapt_in), widen(attn_adapt_out), widen(up_adapt_in), widen(up_adapt_out), widen(down_adapt_in), widen(down_adapt_out))
    hidden_seq = widen(hidden_in).reshape(SEQS, TOK_DEV, D)
    grad_seq = widen(cotangent).reshape(SEQS, TOK_DEV, D)

    def one_seq(running, inputs):
        hidden, grad_out, segments, chosen = inputs

        def run_layer(hidden_arg, qkv_in, qkv_out, attn_in, attn_out, up_in, up_out, down_in, down_out):
            return forward(hidden_arg, qkv_in, qkv_out, attn_in, attn_out, up_in, up_out, down_in, down_out, frozen, segments, chosen)
        output, pullback = jax.vjp(run_layer, hidden, adapters[0], adapters[1], adapters[2], adapters[3], adapters[4], adapters[5], adapters[6], adapters[7])
        grads = pullback(grad_out)
        updated = tuple((older + fresh for older, fresh in zip(running, grads[1:])))
        return (updated, (output, grads[0]))
    zero_grads = tuple((jnp.zeros_like(factor) for factor in adapters))
    totals, outs = lax.scan(one_seq, zero_grads, (hidden_seq, grad_seq, segment_ids, adapter_set))
    outputs, grad_inputs = outs
    return (outputs.reshape(TOKENS, D), grad_inputs.reshape(TOKENS, D), totals[0], totals[1], totals[2], totals[3], totals[4], totals[5], totals[6], totals[7])
```

```python
import functools
import math

import jax
import jax.numpy as jnp
from jax import lax
from jax.experimental import pallas as pl
from jax.experimental.pallas import tpu as pltpu
from jax.sharding import PartitionSpec as P

HEAD = 128
RANK = 16
MESH = pl.DeviceIdType.MESH
F32 = jnp.float32
BF16 = jnp.bfloat16
ROOT = math.sqrt(2.0 / math.pi)


def layer_norm(field_in, gain_row, shift_row):
    centre = jnp.mean(field_in, axis=-1, keepdims=True)
    centred = field_in - centre
    spread = jnp.mean(centred * centred, axis=-1, keepdims=True)
    return centred * lax.rsqrt(spread + 1e-05) * gain_row + shift_row


def precise_dot(left, right):
    return jnp.dot(left, right, precision=lax.Precision.HIGHEST)


def mixed_dot(left, right):
    return jnp.dot(left, right, preferred_element_type=jnp.float32)


def choose_set(table, index, axis):
    return lax.dynamic_index_in_dim(table, index, axis, keepdims=False)


def place_set(grad, index, sets, axis):
    onehot = (jnp.arange(sets) == index).astype(jnp.float32)
    shape_list = [1] * (grad.ndim + 1)
    shape_list[axis] = sets
    return jnp.expand_dims(grad, axis) * onehot.reshape(shape_list)


def per_device(
    hidden_in,
    cotangent,
    segment_ids,
    adapter_set,
    qkv_weight,
    qkv_bias,
    proj_weight,
    proj_bias,
    up_weight,
    up_bias,
    down_weight,
    down_bias,
    norm_gain,
    norm_bias,
    qkv_adapt_in,
    qkv_adapt_out,
    attn_adapt_in,
    attn_adapt_out,
    up_adapt_in,
    up_adapt_out,
    down_adapt_in,
    down_adapt_out,
):
    width_local = qkv_weight.shape[2]
    heads_local = width_local // HEAD
    sets = qkv_adapt_in.shape[1]
    chosen = adapter_set[0]
    segments = segment_ids[0]
    seq_rows = segments.shape[0]
    block_rows = min(512, seq_rows)
    blocks = seq_rows // block_rows
    score_scale = 1.0 / math.sqrt(HEAD)
    gains = norm_gain.astype(jnp.float32)
    shifts = norm_bias.astype(jnp.float32)
    first_q = choose_set(qkv_adapt_in, chosen, 1)
    second_q = choose_set(qkv_adapt_out, chosen, 1)
    first_o = choose_set(attn_adapt_in, chosen, 0)
    second_o = choose_set(attn_adapt_out, chosen, 0)
    first_u = choose_set(up_adapt_in, chosen, 0)
    second_u = choose_set(up_adapt_out, chosen, 0)
    first_d = choose_set(down_adapt_in, chosen, 0)
    second_d = choose_set(down_adapt_out, chosen, 0)
    seq_hidden = lax.all_gather(hidden_in, "tp", axis=0, tiled=True)
    qkv_full, proj_full = (
        lax.all_gather(qkv_weight, "fsdp", axis=1, tiled=True),
        lax.all_gather(proj_weight, "fsdp", axis=1, tiled=True),
    )
    main_term = jnp.einsum("sd,jdc->jsc", seq_hidden, qkv_full, preferred_element_type=jnp.float32)
    low_in = jnp.einsum("sd,jdr->jsr", seq_hidden, first_q, preferred_element_type=jnp.float32)
    low_term = jnp.einsum(
        "jsr,jrc->jsc", low_in, second_q.astype(jnp.float32), precision=lax.Precision.HIGHEST
    )
    bias_rows = jnp.stack([qkv_bias[0], jnp.zeros_like(qkv_bias[0]), qkv_bias[1]]).astype(
        jnp.float32
    )[:, None, :]
    qkv_round = (main_term + low_term + bias_rows).astype(jnp.bfloat16)
    queries = qkv_round[0].reshape(seq_rows, heads_local, HEAD)
    keys = qkv_round[1].reshape(seq_rows, heads_local, HEAD)
    values = qkv_round[2].reshape(seq_rows, heads_local, HEAD)
    query_blocks = queries.reshape(blocks, block_rows, heads_local, HEAD)
    seg_blocks = segments.reshape(blocks, block_rows)

    def scores_of(query_rows, seg_rows):
        raw_scores = (
            jnp.einsum("bhe,she->hbs", query_rows, keys, preferred_element_type=jnp.float32)
            * score_scale
        )
        same_doc = (seg_rows[:, None] == segments[None, :])[None]
        return jnp.where(same_doc, raw_scores, -1e30)

    def forward_block(inputs):
        query_rows, seg_rows = inputs
        scores = scores_of(query_rows, seg_rows)
        row_top = jnp.max(scores, axis=-1, keepdims=True)
        weights = jnp.exp(scores - row_top)
        row_total = jnp.sum(weights, axis=-1, keepdims=True)
        attn_probs = (weights / row_total).astype(jnp.bfloat16)
        attn_mixed = jnp.einsum(
            "hbs,she->bhe", attn_probs, values, preferred_element_type=jnp.float32
        )
        return (attn_mixed, (row_top + jnp.log(row_total))[..., 0])

    attn_mixed, logsum = lax.map(forward_block, (query_blocks, seg_blocks))
    attended = attn_mixed.reshape(seq_rows, width_local).astype(jnp.bfloat16)
    low_attn = mixed_dot(attended, first_o)
    second_o_wide = second_o.astype(jnp.float32)
    row_part = attended
    low_part = low_attn
    attn_sum = lax.psum_scatter(
        mixed_dot(row_part, proj_full) + precise_dot(low_part, second_o_wide),
        "tp",
        scatter_dimension=0,
        tiled=True,
    )
    first_sum = hidden_in.astype(jnp.float32) + attn_sum + proj_bias.astype(jnp.float32)
    normed = layer_norm(first_sum, gains[0], shifts[0])
    normed_round = normed.astype(jnp.bfloat16)
    seq_normed = lax.all_gather(normed_round, "tp", axis=0, tiled=True)
    up_full, down_full = (
        lax.all_gather(up_weight, "fsdp", axis=0, tiled=True),
        lax.all_gather(down_weight, "fsdp", axis=1, tiled=True),
    )
    low_up = mixed_dot(seq_normed, first_u)
    pre_act = (
        mixed_dot(seq_normed, up_full)
        + precise_dot(low_up, second_u.astype(jnp.float32))
        + up_bias.astype(jnp.float32)
    )
    act_round = jax.nn.gelu(pre_act, approximate=True).astype(jnp.bfloat16)
    low_down = mixed_dot(act_round, first_d)
    second_d_wide = second_d.astype(jnp.float32)
    row_part = act_round
    low_part = low_down
    ffn_sum = lax.psum_scatter(
        mixed_dot(row_part, down_full) + precise_dot(low_part, second_d_wide),
        "tp",
        scatter_dimension=0,
        tiled=True,
    )
    second_sum = normed + ffn_sum + down_bias.astype(jnp.float32)
    layer_out = layer_norm(second_sum, gains[1], shifts[1])
    unused, norm_back = jax.vjp(
        lambda field_in: layer_norm(field_in, gains[1], shifts[1]), second_sum
    )
    grad_second = norm_back(cotangent.astype(jnp.float32))[0]
    grad_feed_round = grad_second.astype(jnp.bfloat16)
    seq_grad_feed = lax.all_gather(grad_feed_round, "tp", axis=0, tiled=True)
    up_back, down_back = (
        lax.all_gather(up_weight, "fsdp", axis=0, tiled=True),
        lax.all_gather(down_weight, "fsdp", axis=1, tiled=True),
    )
    grad_low_down = mixed_dot(seq_grad_feed, second_d.T)
    grad_act = jnp.einsum(
        "sd,fd->sf", seq_grad_feed, down_back, preferred_element_type=jnp.float32
    ) + precise_dot(grad_low_down, first_d.astype(jnp.float32).T)
    unused, gelu_back = jax.vjp(lambda field_in: jax.nn.gelu(field_in, approximate=True), pre_act)
    grad_pre_round = gelu_back(grad_act)[0].astype(jnp.bfloat16)
    grad_down_out_part = precise_dot(low_down.T, seq_grad_feed.astype(jnp.float32))
    grad_down_in_part = precise_dot(act_round.astype(jnp.float32).T, grad_low_down)
    grad_low_up = mixed_dot(grad_pre_round, second_u.T)
    grad_up_out_part = precise_dot(low_up.T, grad_pre_round.astype(jnp.float32))
    grad_up_in_part = precise_dot(seq_normed.astype(jnp.float32).T, grad_low_up)
    first_u_wide = first_u.astype(jnp.float32)
    row_part = grad_pre_round
    low_part = grad_low_up
    grad_normed = grad_second + lax.psum_scatter(
        jnp.einsum("sf,df->sd", row_part, up_back, preferred_element_type=jnp.float32)
        + precise_dot(low_part, first_u_wide.T),
        "tp",
        scatter_dimension=0,
        tiled=True,
    )
    unused, norm_front = jax.vjp(
        lambda field_in: layer_norm(field_in, gains[0], shifts[0]), first_sum
    )
    grad_first = norm_front(grad_normed)[0]
    grad_branch_round = grad_first.astype(jnp.bfloat16)
    seq_grad_branch = lax.all_gather(grad_branch_round, "tp", axis=0, tiled=True)
    qkv_back, proj_back = (
        lax.all_gather(qkv_weight, "fsdp", axis=1, tiled=True),
        lax.all_gather(proj_weight, "fsdp", axis=1, tiled=True),
    )
    grad_low_attn = mixed_dot(seq_grad_branch, second_o.T)
    grad_attended = jnp.einsum(
        "sd,cd->sc", seq_grad_branch, proj_back, preferred_element_type=jnp.float32
    ) + precise_dot(grad_low_attn, first_o.astype(jnp.float32).T)
    grad_attended_round = grad_attended.astype(jnp.bfloat16)
    grad_attn_out_part = precise_dot(low_attn.T, seq_grad_branch.astype(jnp.float32))
    grad_attn_in_part = precise_dot(attended.astype(jnp.float32).T, grad_low_attn)
    grad_blocks = grad_attended_round.reshape(blocks, block_rows, heads_local, HEAD)

    def backward_block(carry, inputs):
        grad_keys, grad_values = carry
        query_rows, seg_rows, lse_rows, grad_rows = inputs
        scores = scores_of(query_rows, seg_rows)
        attn_probs = jnp.exp(scores - lse_rows[..., None])
        grad_probs = jnp.einsum(
            "bhe,she->hbs", grad_rows, values, preferred_element_type=jnp.float32
        )
        centre = jnp.sum(grad_probs * attn_probs, axis=-1, keepdims=True)
        grad_scores = (attn_probs * (grad_probs - centre)).astype(jnp.bfloat16)
        grad_query = (
            jnp.einsum("hbs,she->bhe", grad_scores, keys, preferred_element_type=jnp.float32)
            * score_scale
        )
        grad_keys = (
            grad_keys
            + jnp.einsum(
                "hbs,bhe->she", grad_scores, query_rows, preferred_element_type=jnp.float32
            )
            * score_scale
        )
        grad_values = grad_values + jnp.einsum(
            "hbs,bhe->she",
            attn_probs.astype(jnp.bfloat16),
            grad_rows,
            preferred_element_type=jnp.float32,
        )
        return ((grad_keys, grad_values), grad_query)

    zero_state = jnp.zeros((seq_rows, heads_local, HEAD), jnp.float32)
    key_value_grads, grad_queries = lax.scan(
        backward_block, (zero_state, zero_state), (query_blocks, seg_blocks, logsum, grad_blocks)
    )
    grad_qkv_round = jnp.stack(
        [
            grad_queries.reshape(seq_rows, width_local),
            key_value_grads[0].reshape(seq_rows, width_local),
            key_value_grads[1].reshape(seq_rows, width_local),
        ]
    ).astype(jnp.bfloat16)
    grad_qkv_out_part = jnp.einsum(
        "jsr,jsc->jrc", low_in, grad_qkv_round.astype(jnp.float32), precision=lax.Precision.HIGHEST
    )
    grad_low_qkv = jnp.einsum(
        "jsc,jrc->jsr", grad_qkv_round, second_q, preferred_element_type=jnp.float32
    )
    grad_qkv_in_part = jnp.einsum(
        "sd,jsr->jdr", seq_hidden.astype(jnp.float32), grad_low_qkv, precision=lax.Precision.HIGHEST
    )
    first_q_wide = first_q.astype(jnp.float32)
    row_part = grad_qkv_round
    low_part = grad_low_qkv
    grad_input = grad_first + lax.psum_scatter(
        (
            jnp.einsum("jsc,jdc->sd", row_part, qkv_back, preferred_element_type=jnp.float32)
            + jnp.einsum("jsr,jdr->sd", low_part, first_q_wide, precision=lax.Precision.HIGHEST)
        ).astype(jnp.bfloat16),
        "tp",
        scatter_dimension=0,
        tiled=True,
    ).astype(jnp.float32)
    wide_grads = lax.psum(
        (
            place_set(grad_qkv_in_part, chosen, sets, 1),
            place_set(grad_attn_out_part, chosen, sets, 0),
            place_set(grad_up_in_part, chosen, sets, 0),
            place_set(grad_down_out_part, chosen, sets, 0),
        ),
        ("fsdp", "tp"),
    )
    split_grads = (
        lax.psum(place_set(grad_qkv_out_part, chosen, sets, 1).astype(jnp.bfloat16), "fsdp").astype(
            jnp.float32
        ),
        lax.psum(place_set(grad_attn_in_part, chosen, sets, 0).astype(jnp.bfloat16), "fsdp").astype(
            jnp.float32
        ),
        lax.psum(place_set(grad_up_out_part, chosen, sets, 0).astype(jnp.bfloat16), "fsdp").astype(
            jnp.float32
        ),
        lax.psum(place_set(grad_down_in_part, chosen, sets, 0).astype(jnp.bfloat16), "fsdp").astype(
            jnp.float32
        ),
    )
    return (
        layer_out,
        grad_input,
        wide_grads[0],
        split_grads[0],
        split_grads[1],
        wide_grads[1],
        wide_grads[2],
        split_grads[2],
        split_grads[3],
        wide_grads[3],
    )


def dot_nn(left, right):
    return jnp.dot(left, right, preferred_element_type=F32)


def dot_nt(left, right):
    return lax.dot_general(left, right, (((1,), (1,)), ((), ())), preferred_element_type=F32)


def flip(index, mask):
    out, bit = index, 1
    while bit <= mask:
        if mask & bit:
            out = out + bit - 2 * bit * lax.rem(lax.div(index, bit), 2)
        bit *= 2
    return out


def norm_parts(rows):
    centred = rows - jnp.mean(rows, axis=-1, keepdims=True)
    spread = jnp.mean(centred * centred, axis=-1, keepdims=True)
    rstd = lax.rsqrt(spread + 1e-05)
    return centred * rstd, rstd


def norm_pull(grad, unit, rstd):
    return rstd * (
        grad
        - jnp.mean(grad, axis=-1, keepdims=True)
        - unit * jnp.mean(grad * unit, axis=-1, keepdims=True)
    )


class Gather:
    def __init__(self, which, shard, whole, send, recv, fsdp, tp, count):
        self.which, self.shard, self.whole = which, shard, whole
        self.send, self.recv, self.fsdp, self.tp = send, recv, fsdp, tp
        bits = [1 << i for i in range(1, count.bit_length() - 1)]
        self.orders = [bits, bits[::-1]]
        self.steps = len(bits)
        self.held = [[0], [0]]
        self.sent = []
        self.count = count

    def copy(self, half, mask, bit):
        landed = mask ^ bit
        place = self.whole(flip(self.fsdp, mask), half)
        return pltpu.make_async_remote_copy(
            src_ref=self.shard(half) if mask == 0 else place,
            dst_ref=place,
            send_sem=self.send.at[self.which, half, landed],
            recv_sem=self.recv.at[self.which, half, landed],
            device_id=(flip(self.fsdp, bit), self.tp),
            device_id_type=MESH,
        )

    def launch(self, half, mask, bit):
        self.copy(half, mask, bit).start()
        self.sent.append((half, mask, bit))

    def await_block(self, half, mask, bit):
        place = self.whole(flip(self.fsdp, mask), half)
        pltpu.make_async_remote_copy(
            src_ref=place,
            dst_ref=place,
            send_sem=self.send.at[self.which, half, mask],
            recv_sem=self.recv.at[self.which, half, mask],
            device_id=(flip(self.fsdp, bit), self.tp),
            device_id_type=MESH,
        ).wait_recv()

    def stage(self, step):
        for half in range(2):
            fresh = [0]
            if step > 0:
                bit = self.orders[half][step - 1]
                fresh = [mask ^ bit for mask in self.held[half]]
                for mask in fresh:
                    self.await_block(half, mask, bit)
                self.held[half] = self.held[half] + fresh
            if step < self.steps:
                for mask in self.held[half]:
                    self.launch(half, mask, self.orders[half][step])
            for mask in fresh:
                self.launch(half, mask, 1)

    def finish(self):
        for half in range(2):
            for mask in self.held[half]:
                self.await_block(half, mask ^ 1, 1)

    def drain(self):
        for half, mask, bit in self.sent:
            self.copy(half, mask, bit).wait_send()


def layer_kernel(cfg, *refs):
    F, T, S, D, H, FL, C = (cfg[k] for k in ("F", "T", "S", "D", "H", "FL", "C"))
    Q, heads, block = S // T, H // HEAD, D // F
    R = Q // C
    M = T * R
    NT = min(256, FL)
    (
        hidden_in, cotangent, seg_row, seg_col, qkv_w, proj_w, up_w, down_w,
        vectors, up_bias, qkv_bias, wide_f, heads_f, units_f,
        layer_out, grad_input, wide_g, heads_g, units_g,
        hidden, qkv_all, proj_all, up_all, down_all,
        qkv, probs, mixed, normed, act, slope, grad_feed, grad_pre, grad_branch, grad_mixed, grad_qkv,
        part, from_low, from_high, unit_one, rstd_one, grad_own,
        low_q, low_o, low_u, low_d, back_q, back_o, back_u, back_d,
        w_send, w_recv, up_send, up_recv, dn_send, dn_recv, g_up_send, g_up_recv, g_dn_send, g_dn_recv,
        own_sem,
    ) = refs
    f, z = lax.axis_index("fsdp"), lax.axis_index("tp")
    bits = [1 << i for i in range(F.bit_length() - 1)]

    barrier = pltpu.get_barrier_semaphore()
    for bit in bits:
        pl.semaphore_signal(barrier, inc=1, device_id=(flip(f, bit), z), device_id_type=MESH)

    @pl.when(z > 0)
    def _():
        pl.semaphore_signal(barrier, inc=1, device_id=(f, z - 1), device_id_type=MESH)

    @pl.when(z < T - 1)
    def _():
        pl.semaphore_signal(barrier, inc=1, device_id=(f, z + 1), device_id_type=MESH)

    inside = (z > 0) & (z < T - 1)

    @pl.when(inside)
    def _():
        pl.semaphore_wait(barrier, len(bits) + 2)

    @pl.when(jnp.logical_not(inside))
    def _():
        pl.semaphore_wait(barrier, len(bits) + 1)

    rows_of = lambda total, half: pl.ds(half * (total // 2), total // 2)
    gathers = [
        Gather(0, lambda h: qkv_w.at[:, rows_of(block, h)], lambda g, h: qkv_all.at[:, g, rows_of(block, h)], w_send, w_recv, f, z, F),
        Gather(1, lambda h: proj_w.at[rows_of(H, h)], lambda g, h: proj_all.at[g, rows_of(H, h)], w_send, w_recv, f, z, F),
        Gather(2, lambda h: up_w.at[rows_of(block, h)], lambda g, h: up_all.at[g, rows_of(block, h)], w_send, w_recv, f, z, F),
        Gather(3, lambda h: down_w.at[rows_of(FL, h)], lambda g, h: down_all.at[g, rows_of(FL, h)], w_send, w_recv, f, z, F),
    ]
    K = gathers[0].steps
    own_copies = [
        pltpu.make_async_copy(hidden_in, hidden.at[:, z], own_sem.at[0]),
        pltpu.make_async_copy(qkv_w, qkv_all.at[:, f], own_sem.at[1]),
        pltpu.make_async_copy(proj_w, proj_all.at[f], own_sem.at[2]),
        pltpu.make_async_copy(up_w, up_all.at[f], own_sem.at[3]),
        pltpu.make_async_copy(down_w, down_all.at[f], own_sem.at[4]),
    ]

    def line_copy(src, dst, send, recv, c, q, step):
        return pltpu.make_async_remote_copy(
            src_ref=src, dst_ref=dst, send_sem=send.at[c, q], recv_sem=recv.at[c, q],
            device_id=(f, z + step), device_id_type=MESH,
        )

    def rs_copy(c, q, step):
        landing, send, recv = (from_low, up_send, up_recv) if step > 0 else (from_high, dn_send, dn_recv)
        return line_copy(part.at[c, q], landing.at[c, q], send, recv, c, q, step)

    def rs_wait(c, q, step):
        landing, send, recv = (from_low, up_send, up_recv) if step > 0 else (from_high, dn_send, dn_recv)
        line_copy(landing.at[c, q], landing.at[c, q], send, recv, c, q, -step).wait_recv()

    def rs(c, t):
        def add(q, landing):
            part[c, q] = (part[c, q].astype(F32) + landing[c, q].astype(F32)).astype(BF16)

        @pl.when(z <= t - 1)
        def _():
            q = T - t + z

            @pl.when(z > 0)
            def _():
                rs_wait(c, q, 1)
                add(q, from_low)

            rs_copy(c, q, 1).start()

        @pl.when(z >= T - t)
        def _():
            q = z - (T - t)

            @pl.when(z < T - 1)
            def _():
                rs_wait(c, q, -1)
                add(q, from_high)

            rs_copy(c, q, -1).start()

    def rs_sum(c):
        @pl.when(z > 0)
        def _():
            rs_wait(c, z, 1)

        @pl.when(z < T - 1)
        def _():
            rs_wait(c, z, -1)

        return (part[c, z].astype(F32) + from_low[c, z].astype(F32)) + from_high[c, z].astype(F32)

    def rs_drain(c):
        for q in range(T):
            if q > 0:

                @pl.when(z < q)
                def _(q=q):
                    rs_copy(c, q, 1).wait_send()

            if q < T - 1:

                @pl.when(z > q)
                def _(q=q):
                    rs_copy(c, q, -1).wait_send()

    def ag_copy(buffer, c, q, step):
        send, recv = (g_up_send, g_up_recv) if step > 0 else (g_dn_send, g_dn_recv)
        if c is None:
            return line_copy(buffer.at[:, q], buffer.at[:, q], send, recv, C, q, step)
        return line_copy(buffer.at[c, q], buffer.at[c, q], send, recv, c, q, step)

    def ag_wait(buffer, c, q, step):
        send, recv = (g_up_send, g_up_recv) if step > 0 else (g_dn_send, g_dn_recv)
        place = buffer.at[:, q] if c is None else buffer.at[c, q]
        line_copy(place, place, send, recv, C if c is None else c, q, -step).wait_recv()

    def ag(buffer, c, t):
        if t == 1:

            @pl.when(z < T - 1)
            def _():
                ag_copy(buffer, c, z, 1).start()

            @pl.when(z > 0)
            def _():
                ag_copy(buffer, c, z, -1).start()

            return

        @pl.when(z >= t - 1)
        def _():
            q = z - (t - 1)
            ag_wait(buffer, c, q, 1)

            @pl.when(z < T - 1)
            def _():
                ag_copy(buffer, c, q, 1).start()

        @pl.when(z <= T - t)
        def _():
            q = z + (t - 1)
            ag_wait(buffer, c, q, -1)

            @pl.when(z > 0)
            def _():
                ag_copy(buffer, c, q, -1).start()

    def ag_drain(buffer, c):
        for q in range(T):

            @pl.when((z >= q) & (z < T - 1))
            def _(q=q):
                ag_copy(buffer, c, q, 1).wait_send()

            @pl.when((z <= q) & (z > 0))
            def _(q=q):
                ag_copy(buffer, c, q, -1).wait_send()

    a_q = lambda j: wide_f.at[pl.ds(16 * j, 16)]
    b_o, a_u, b_d = (wide_f.at[pl.ds(16 * k, 16)] for k in (3, 4, 5))
    b_q = lambda j: heads_f.at[pl.ds(16 * j, 16)]
    a_o = heads_f.at[pl.ds(48, 16)]
    b_u, a_d = (units_f.at[pl.ds(16 * k, 16)] for k in (0, 1))
    v_proj, v_down, gain_a, shift_a, gain_b, shift_b = (vectors.at[pl.ds(k, 1)] for k in range(6))

    def chunk(buffer, c):
        return buffer[c].reshape(M, buffer.shape[-1])

    def cols_of(g, size):
        return pl.ds(pl.multiple_of(g * size, size), size)

    def project():
        width = min(256, H)
        for j in range(3):
            low_j = dot_nt(hidden[...].reshape(S, D), a_q(j)[...]).astype(BF16)
            low_q[j] = low_j

            @pl.loop(0, H // width)
            def _(n, j=j, low_j=low_j):
                cols = cols_of(n, width)
                rows = dot_nn(hidden[...].reshape(S, D), qkv_all[j, :, :, cols].reshape(D, width))
                rows += dot_nn(low_j, b_q(j)[:, cols]) + qkv_bias[pl.ds(j, 1), cols]
                qkv[j, :, cols] = rows.astype(BF16)

    scale = 1.0 / math.sqrt(HEAD)

    def attend():
        @pl.loop(0, heads)
        def _(h):
            cols = cols_of(h, HEAD)
            value_t = qkv[2, :, cols].T
            width = min(256, S)

            @pl.loop(0, S // width)
            def _(n):
                rows = cols_of(n, width)
                scores = dot_nt(qkv[1, :, cols], qkv[0, rows, cols]) * scale
                scores = jnp.where(seg_col[...] == seg_row[:, rows], scores, -1e30)
                weights = jnp.exp(scores - jnp.max(scores, axis=0, keepdims=True))
                weights = weights * (1.0 / jnp.sum(weights, axis=0, keepdims=True))
                low = weights.astype(BF16)
                probs[h, :, rows] = low
                mixed[rows, cols] = dot_nn(value_t, low).T.astype(BF16)

    def attend_back():
        @pl.loop(0, heads)
        def _(h):
            cols = cols_of(h, HEAD)
            key_t = qkv[1, :, cols].T
            width = min(256, S)

            @pl.loop(0, S // width)
            def _(n):
                rows = cols_of(n, width)
                weights = probs[h, :, rows].astype(F32)
                grad = dot_nt(qkv[2, :, cols], grad_mixed[rows, cols])
                centre = jnp.sum(grad * weights, axis=0, keepdims=True)
                low = (weights * (grad - centre)).astype(BF16)
                grad_scores[:, rows] = low
                grad_qkv[0, rows, cols] = (dot_nn(key_t, low).T * scale).astype(BF16)

            grad_qkv[1, :, cols] = (dot_nn(grad_scores[...], qkv[0, :, cols]) * scale).astype(BF16)
            grad_qkv[2, :, cols] = dot_nn(probs[h], grad_mixed[:, cols]).astype(BF16)

    grad_scores = slope.at[pl.ds(0, S), pl.ds(0, S)]

    def span(c):
        return pl.ds(c * M, M)

    def put_part(c, cols, rows):
        part[c, :, :, cols] = rows.astype(BF16).reshape(T, R, rows.shape[-1])

    def mix_out(c):
        low = dot_nt(mixed[span(c)], a_o[...]).astype(BF16)
        low_o[span(c)] = low

        @pl.loop(0, F)
        def _(g):
            cols = cols_of(g, block)
            put_part(c, cols, dot_nn(mixed[span(c)], proj_all[g]) + dot_nn(low, b_o[:, cols]))

    def feed_up(c):
        low = dot_nt(chunk(normed, c), a_u[...]).astype(BF16)
        low_u[span(c)] = low

        @pl.loop(0, FL // NT)
        def _(n):
            cols = cols_of(n, NT)
            pre = dot_nn(chunk(normed, c), up_all[:, :, cols].reshape(D, NT))
            pre += dot_nn(low, b_u[:, cols]) + up_bias[:, cols]
            square = pre * pre
            bend = jnp.tanh(ROOT * (pre + 0.044715 * square * pre))
            half = 0.5 * (1.0 + bend)
            act[span(c), cols] = (pre * half).astype(BF16)
            rise = half + 0.5 * pre * (1.0 - bend * bend) * (ROOT * (1.0 + 3 * 0.044715 * square))
            slope[span(c), cols] = rise.astype(BF16)

    def feed_down(c):
        low = dot_nt(act[span(c)], a_d[...]).astype(BF16)
        low_d[span(c)] = low

        @pl.loop(0, F)
        def _(g):
            cols = cols_of(g, block)
            put_part(c, cols, dot_nn(act[span(c)], down_all[g]) + dot_nn(low, b_d[:, cols]))

    def back_down(c):
        low = dot_nt(chunk(grad_feed, c), b_d[...]).astype(BF16)
        back_d[span(c)] = low

        @pl.loop(0, FL // NT)
        def _(n):
            cols = cols_of(n, NT)
            total = dot_nn(low, a_d[:, cols])
            for g in range(F):
                rows = grad_feed[c, :, :, pl.ds(g * block, block)].reshape(M, block)
                total += dot_nt(rows, down_all[g, cols])
            grad_pre[span(c), cols] = (total * slope[span(c), cols].astype(F32)).astype(BF16)

    def back_up(c):
        low = dot_nt(grad_pre[span(c)], b_u[...]).astype(BF16)
        back_u[span(c)] = low

        @pl.loop(0, F)
        def _(g):
            cols = cols_of(g, block)
            put_part(c, cols, dot_nt(grad_pre[span(c)], up_all[g]) + dot_nn(low, a_u[:, cols]))

    def back_mix(c):
        low = dot_nt(chunk(grad_branch, c), b_o[...]).astype(BF16)
        back_o[span(c)] = low
        total = dot_nn(low, a_o[...])
        for g in range(F):
            rows = grad_branch[c, :, :, pl.ds(g * block, block)].reshape(M, block)
            total += dot_nt(rows, proj_all[g])
        grad_mixed[span(c)] = total.astype(BF16)

    def back_project(c):
        lows = []
        for j in range(3):
            low = dot_nt(grad_qkv[j, span(c)], b_q(j)[...]).astype(BF16)
            back_q[j, span(c)] = low
            lows.append(low)

        @pl.loop(0, F)
        def _(g):
            cols = cols_of(g, block)
            total = dot_nn(lows[0], a_q(0)[:, cols])
            for j in range(3):
                if j:
                    total += dot_nn(lows[j], a_q(j)[:, cols])
                total += dot_nt(grad_qkv[j, span(c)], qkv_all[j, g])
            put_part(c, cols, total)

    def own(c):
        return pl.ds(c * R, R)

    def meet_one(c):
        total = rs_sum(c) + hidden[c, z].astype(F32) + v_proj[...]
        unit, rstd = norm_parts(total)
        unit_one[own(c)] = unit
        rstd_one[own(c)] = jnp.broadcast_to(rstd, (R, 128))
        normed[c, z] = (unit * gain_a[...] + shift_a[...]).astype(BF16)

    def meet_two(c):
        total = rs_sum(c) + unit_one[own(c)] * gain_a[...] + shift_a[...] + v_down[...]
        unit, rstd = norm_parts(total)
        layer_out[own(c)] = unit * gain_b[...] + shift_b[...]
        grad = norm_pull(cotangent[own(c)].astype(F32) * gain_b[...], unit, rstd)
        grad_own[own(c)] = grad
        grad_feed[c, z] = grad.astype(BF16)

    def meet_three(c):
        grad = (grad_own[own(c)] + rs_sum(c)) * gain_a[...]
        grad = norm_pull(grad, unit_one[own(c)], rstd_one[own(c)][:, :1])
        grad_own[own(c)] = grad
        grad_branch[c, z] = grad.astype(BF16)

    def meet_four(c):
        grad_input[own(c)] = grad_own[own(c)] + rs_sum(c)

    def factor(low, right):
        return dot_nn(low.astype(F32).T.astype(BF16), right)

    def factors_feed():
        units_g[pl.ds(0, 16)] = factor(low_u[...], grad_pre[...])
        units_g[pl.ds(16, 16)] = factor(back_d[...], act[...])
        wide_g[pl.ds(64, 16)] = factor(back_u[...], normed[...].reshape(S, D))
        wide_g[pl.ds(80, 16)] = factor(low_d[...], grad_feed[...].reshape(S, D))

    def factors_mix():
        heads_g[pl.ds(48, 16)] = factor(back_o[...], mixed[...])
        wide_g[pl.ds(48, 16)] = factor(low_o[...], grad_branch[...].reshape(S, D))

    def factors_project():
        for j in range(3):
            heads_g[pl.ds(16 * j, 16)] = factor(low_q[j], grad_qkv[j])
            wide_g[pl.ds(16 * j, 16)] = factor(back_q[j], hidden[...].reshape(S, D))

    from_low[:, 0] = jnp.zeros((C, R, D), BF16)
    from_high[:, T - 1] = jnp.zeros((C, R, D), BF16)
    qkv_g, proj_g, up_g, down_g = gathers
    def own_hidden(step):
        return line_copy(hidden_in, hidden.at[:, z], g_up_send if step > 0 else g_dn_send, g_up_recv if step > 0 else g_dn_recv, C, z, step)

    @pl.when(z < T - 1)
    def _():
        own_hidden(1).start()

    @pl.when(z > 0)
    def _():
        own_hidden(-1).start()

    qkv_g.stage(0)
    for copy in own_copies:
        copy.start()
    schedule(cfg, dict(locals()))


def schedule(cfg, env):
    T, C, K = cfg["T"], cfg["C"], env["K"]
    rs, ag, hidden = env["rs"], env["ag"], env["hidden"]
    qkv_g, proj_g, up_g, down_g = env["gathers"]
    chunks = range(C)
    for step in range(1, K + 1):
        qkv_g.stage(step)
        if step == 1:
            proj_g.stage(0)
            ag(hidden, None, 2)
    if K == 0:
        proj_g.stage(0)
    if K >= 1:
        proj_g.stage(1)
    up_g.stage(0)
    if K < 1:
        ag(hidden, None, 2)
    for t in range(3, T + 1):
        ag(hidden, None, t)
    for step in range(2, K + 1):
        proj_g.stage(step)
    down_g.stage(0)
    qkv_g.finish()
    for copy in env["own_copies"]:
        copy.wait()
    env["project"]()
    env["attend"]()
    for step in range(1, K + 1):
        up_g.stage(step)
    proj_g.finish()
    buffers = [env["normed"], env["grad_feed"], env["grad_branch"]]
    meets = [env["meet_one"], env["meet_two"], env["meet_three"], env["meet_four"]]

    def work(k, c):
        if k > 0:
            env["rs_drain"](c)
        if k == 0:
            env["mix_out"](c)
        if k == 1:
            if c == 0:
                for step in range(1, K + 1):
                    down_g.stage(step)
                up_g.finish()
            env["feed_up"](c)
            if c == 0:
                down_g.finish()
            env["feed_down"](c)
        if k == 2:
            env["back_down"](c)
            env["back_up"](c)
        if k == 3:
            env["back_project"](c)
        rs(c, 1)

    for k in range(3):
        for c in chunks:
            work(k, c)
        for t in range(2, T):
            for c in chunks:
                rs(c, t)
        for c in chunks:
            meets[k](c)
            if k > 0:
                env["ag_drain"](buffers[k - 1], c)
            ag(buffers[k], c, 1)
        for t in range(2, T + 1):
            for c in chunks:
                ag(buffers[k], c, t)
    for c in chunks:
        env["back_mix"](c)
    env["attend_back"]()
    for c in chunks:
        work(3, c)
    env["factors_feed"]()
    env["factors_mix"]()
    env["factors_project"]()
    for t in range(2, T):
        for c in chunks:
            rs(c, t)
    for c in chunks:
        meets[3](c)
    for c in chunks:
        env["rs_drain"](c)
        env["ag_drain"](buffers[2], c)
    env["ag_drain"](hidden, None)
    for gather in env["gathers"]:
        gather.drain()


def spread(mesh, body):
    placed = (
        P(("fsdp", "tp"), None),
        P(("fsdp", "tp"), None),
        P("fsdp", None),
        P("fsdp"),
        P(None, "fsdp", "tp"),
        P(None, "tp"),
        P("tp", "fsdp"),
        P(),
        P("fsdp", "tp"),
        P("tp"),
        P("tp", "fsdp"),
        P(),
        P(),
        P(),
        P(),
        P(None, None, None, "tp"),
        P(None, "tp", None),
        P(),
        P(),
        P(None, None, "tp"),
        P(None, "tp", None),
        P(),
    )
    return jax.shard_map(
        body,
        mesh=mesh,
        in_specs=placed,
        out_specs=(
            P(("fsdp", "tp"), None),
            P(("fsdp", "tp"), None),
            P(),
            P(None, None, None, "tp"),
            P(None, "tp", None),
            P(),
            P(),
            P(None, None, "tp"),
            P(None, "tp", None),
            P(),
        ),
        check_vma=False,
    )


def chunks_for(rows):
    return 2 if rows % 32 == 0 else 1


def kernel_per_device(F, T):
    def per_device(
        hidden_in, cotangent, segment_ids, adapter_set, qkv_weight, qkv_bias, proj_weight, proj_bias,
        up_weight, up_bias, down_weight, down_bias, norm_gain, norm_bias, qkv_adapt_in, qkv_adapt_out,
        attn_adapt_in, attn_adapt_out, up_adapt_in, up_adapt_out, down_adapt_in, down_adapt_out,
    ):
        Q, D = hidden_in.shape
        H, FL = qkv_weight.shape[2], up_weight.shape[1]
        S, C, sets = Q * T, chunks_for(Q), qkv_adapt_in.shape[1]
        R, block = Q // C, D // F
        cfg = dict(F=F, T=T, S=S, D=D, H=H, FL=FL, C=C)
        chosen = adapter_set[0]
        turn = lambda table: jnp.swapaxes(table, -1, -2)
        pick = lambda table, axis: choose_set(table, chosen, axis)
        wide_f = jnp.concatenate(
            [
                pick(turn(qkv_adapt_in), 1).reshape(-1, D),
                pick(attn_adapt_out, 0),
                pick(turn(up_adapt_in), 0),
                pick(down_adapt_out, 0),
            ]
        )
        heads_f = jnp.concatenate(
            [pick(qkv_adapt_out, 1).reshape(-1, H), pick(turn(attn_adapt_in), 0)]
        )
        units_f = jnp.concatenate([pick(up_adapt_out, 0), pick(turn(down_adapt_in), 0)])
        vectors = jnp.stack(
            [proj_bias, down_bias, norm_gain[0], norm_bias[0], norm_gain[1], norm_bias[1]]
        ).astype(F32)
        bias_rows = jnp.stack([qkv_bias[0], jnp.zeros_like(qkv_bias[0]), qkv_bias[1]]).astype(F32)
        segments = segment_ids[0].reshape(T, C, R).transpose(1, 0, 2).reshape(S)
        vmem, anywhere = pl.BlockSpec(memory_space=pltpu.VMEM), pl.BlockSpec(memory_space=pl.ANY)
        dma = pltpu.SemaphoreType.DMA
        bank = lambda *shape: pltpu.VMEM(shape, BF16)
        wide_bank = lambda *shape: pltpu.VMEM(shape, F32)
        scratch = (
            [bank(C, T, R, D), bank(3, F, block, H), bank(F, H, block), bank(F, block, FL), bank(F, FL, block)]
            + [bank(3, S, H), bank(H // HEAD, S, S), bank(S, H), bank(C, T, R, D), bank(S, FL), bank(S, FL)]
            + [bank(C, T, R, D), bank(S, FL), bank(C, T, R, D), bank(S, H), bank(3, S, H)]
            + [bank(C, T, R, D), bank(C, T, R, D), bank(C, T, R, D)]
            + [wide_bank(Q, D), wide_bank(Q, 128), wide_bank(Q, D)]
            + [bank(3, S, RANK), bank(S, RANK), bank(S, RANK), bank(S, RANK)] * 2
            + [dma((4, 2, F)), dma((4, 2, F))]
            + [dma((C, T))] * 4
            + [dma((C + 1, T))] * 4
            + [dma((5,))]
        )
        flops = 2 * S * (4 * D * H + 2 * D * FL) * 2
        outs = pl.pallas_call(
            functools.partial(layer_kernel, cfg),
            out_shape=[
                jax.ShapeDtypeStruct((Q, D), F32),
                jax.ShapeDtypeStruct((Q, D), F32),
                jax.ShapeDtypeStruct((6 * RANK, D), F32),
                jax.ShapeDtypeStruct((4 * RANK, H), F32),
                jax.ShapeDtypeStruct((2 * RANK, FL), F32),
            ],
            in_specs=[anywhere] + [vmem] * 3 + [anywhere] * 4 + [vmem] * 6,
            out_specs=[vmem] * 5,
            scratch_shapes=scratch,
            compiler_params=pltpu.CompilerParams(
                collective_id=0, has_side_effects=True, vmem_limit_bytes=62 * 1024 * 1024
            ),
            cost_estimate=pl.CostEstimate(flops=flops, bytes_accessed=30000000, transcendentals=0),
        )(
            hidden_in.reshape(C, R, D), cotangent, segments[None, :], segments[:, None],
            qkv_weight, proj_weight, up_weight, down_weight,
            vectors, up_bias.astype(F32)[None, :], bias_rows, wide_f, heads_f, units_f,
        )
        layer_out, grad_input, wide_g, heads_g, units_g = outs
        onehot = (jnp.arange(sets) == chosen).astype(F32)[:, None, None]
        wide_t = lax.psum((wide_g * onehot).astype(BF16), ("fsdp", "tp")).astype(F32)
        heads_t, units_t = lax.psum(
            ((heads_g * onehot).astype(BF16), (units_g * onehot).astype(BF16)), "fsdp"
        )
        heads_t, units_t = heads_t.astype(F32), units_t.astype(F32)
        trio = lambda table: table.reshape(sets, 3, RANK, -1).transpose(1, 0, 2, 3)
        return (
            layer_out,
            grad_input,
            turn(trio(wide_t[:, :48])),
            trio(heads_t[:, :48]),
            turn(heads_t[:, 48:]),
            wide_t[:, 48:64],
            turn(wide_t[:, 64:80]),
            units_t[:, :16],
            turn(units_t[:, 16:]),
            wide_t[:, 80:],
        )

    return per_device


def solution(mesh):
    F, T = mesh.shape["fsdp"], mesh.shape["tp"]

    def whole(*args):
        width = args[0].shape[1]
        fits = F & (F - 1) == 0 and (width // F) % 128 == 0 and T > 1 and F > 1
        return spread(mesh, kernel_per_device(F, T) if fits else per_device)(*args)

    return whole
```

```python
import functools
import math

import jax
import jax.numpy as jnp
from jax import lax
from jax.experimental import pallas as pl
from jax.experimental.pallas import tpu as pltpu
from jax.sharding import PartitionSpec as P

HEAD = 128
RANK = 16
MESH = pl.DeviceIdType.MESH
F32 = jnp.float32
BF16 = jnp.bfloat16
ROOT = math.sqrt(2.0 / math.pi)


def layer_norm(field_in, gain_row, shift_row):
    centre = jnp.mean(field_in, axis=-1, keepdims=True)
    centred = field_in - centre
    spread = jnp.mean(centred * centred, axis=-1, keepdims=True)
    return centred * lax.rsqrt(spread + 1e-05) * gain_row + shift_row


def precise_dot(left, right):
    return jnp.dot(left, right, precision=lax.Precision.HIGHEST)


def mixed_dot(left, right):
    return jnp.dot(left, right, preferred_element_type=jnp.float32)


def choose_set(table, index, axis):
    return lax.dynamic_index_in_dim(table, index, axis, keepdims=False)


def place_set(grad, index, sets, axis):
    onehot = (jnp.arange(sets) == index).astype(jnp.float32)
    shape_list = [1] * (grad.ndim + 1)
    shape_list[axis] = sets
    return jnp.expand_dims(grad, axis) * onehot.reshape(shape_list)


def per_device(
    hidden_in,
    cotangent,
    segment_ids,
    adapter_set,
    qkv_weight,
    qkv_bias,
    proj_weight,
    proj_bias,
    up_weight,
    up_bias,
    down_weight,
    down_bias,
    norm_gain,
    norm_bias,
    qkv_adapt_in,
    qkv_adapt_out,
    attn_adapt_in,
    attn_adapt_out,
    up_adapt_in,
    up_adapt_out,
    down_adapt_in,
    down_adapt_out,
):
    width_local = qkv_weight.shape[2]
    heads_local = width_local // HEAD
    sets = qkv_adapt_in.shape[1]
    chosen = adapter_set[0]
    segments = segment_ids[0]
    seq_rows = segments.shape[0]
    block_rows = min(512, seq_rows)
    blocks = seq_rows // block_rows
    score_scale = 1.0 / math.sqrt(HEAD)
    gains = norm_gain.astype(jnp.float32)
    shifts = norm_bias.astype(jnp.float32)
    first_q = choose_set(qkv_adapt_in, chosen, 1)
    second_q = choose_set(qkv_adapt_out, chosen, 1)
    first_o = choose_set(attn_adapt_in, chosen, 0)
    second_o = choose_set(attn_adapt_out, chosen, 0)
    first_u = choose_set(up_adapt_in, chosen, 0)
    second_u = choose_set(up_adapt_out, chosen, 0)
    first_d = choose_set(down_adapt_in, chosen, 0)
    second_d = choose_set(down_adapt_out, chosen, 0)
    seq_hidden = lax.all_gather(hidden_in, "tp", axis=0, tiled=True)
    qkv_full, proj_full = (
        lax.all_gather(qkv_weight, "fsdp", axis=1, tiled=True),
        lax.all_gather(proj_weight, "fsdp", axis=1, tiled=True),
    )
    main_term = jnp.einsum("sd,jdc->jsc", seq_hidden, qkv_full, preferred_element_type=jnp.float32)
    low_in = jnp.einsum("sd,jdr->jsr", seq_hidden, first_q, preferred_element_type=jnp.float32)
    low_term = jnp.einsum(
        "jsr,jrc->jsc", low_in, second_q.astype(jnp.float32), precision=lax.Precision.HIGHEST
    )
    bias_rows = jnp.stack([qkv_bias[0], jnp.zeros_like(qkv_bias[0]), qkv_bias[1]]).astype(
        jnp.float32
    )[:, None, :]
    qkv_round = (main_term + low_term + bias_rows).astype(jnp.bfloat16)
    queries = qkv_round[0].reshape(seq_rows, heads_local, HEAD)
    keys = qkv_round[1].reshape(seq_rows, heads_local, HEAD)
    values = qkv_round[2].reshape(seq_rows, heads_local, HEAD)
    query_blocks = queries.reshape(blocks, block_rows, heads_local, HEAD)
    seg_blocks = segments.reshape(blocks, block_rows)

    def scores_of(query_rows, seg_rows):
        raw_scores = (
            jnp.einsum("bhe,she->hbs", query_rows, keys, preferred_element_type=jnp.float32)
            * score_scale
        )
        same_doc = (seg_rows[:, None] == segments[None, :])[None]
        return jnp.where(same_doc, raw_scores, -1e30)

    def forward_block(inputs):
        query_rows, seg_rows = inputs
        scores = scores_of(query_rows, seg_rows)
        row_top = jnp.max(scores, axis=-1, keepdims=True)
        weights = jnp.exp(scores - row_top)
        row_total = jnp.sum(weights, axis=-1, keepdims=True)
        attn_probs = (weights / row_total).astype(jnp.bfloat16)
        attn_mixed = jnp.einsum(
            "hbs,she->bhe", attn_probs, values, preferred_element_type=jnp.float32
        )
        return (attn_mixed, (row_top + jnp.log(row_total))[..., 0])

    attn_mixed, logsum = lax.map(forward_block, (query_blocks, seg_blocks))
    attended = attn_mixed.reshape(seq_rows, width_local).astype(jnp.bfloat16)
    low_attn = mixed_dot(attended, first_o)
    second_o_wide = second_o.astype(jnp.float32)
    row_part = attended
    low_part = low_attn
    attn_sum = lax.psum_scatter(
        mixed_dot(row_part, proj_full) + precise_dot(low_part, second_o_wide),
        "tp",
        scatter_dimension=0,
        tiled=True,
    )
    first_sum = hidden_in.astype(jnp.float32) + attn_sum + proj_bias.astype(jnp.float32)
    normed = layer_norm(first_sum, gains[0], shifts[0])
    normed_round = normed.astype(jnp.bfloat16)
    seq_normed = lax.all_gather(normed_round, "tp", axis=0, tiled=True)
    up_full, down_full = (
        lax.all_gather(up_weight, "fsdp", axis=0, tiled=True),
        lax.all_gather(down_weight, "fsdp", axis=1, tiled=True),
    )
    low_up = mixed_dot(seq_normed, first_u)
    pre_act = (
        mixed_dot(seq_normed, up_full)
        + precise_dot(low_up, second_u.astype(jnp.float32))
        + up_bias.astype(jnp.float32)
    )
    act_round = jax.nn.gelu(pre_act, approximate=True).astype(jnp.bfloat16)
    low_down = mixed_dot(act_round, first_d)
    second_d_wide = second_d.astype(jnp.float32)
    row_part = act_round
    low_part = low_down
    ffn_sum = lax.psum_scatter(
        mixed_dot(row_part, down_full) + precise_dot(low_part, second_d_wide),
        "tp",
        scatter_dimension=0,
        tiled=True,
    )
    second_sum = normed + ffn_sum + down_bias.astype(jnp.float32)
    layer_out = layer_norm(second_sum, gains[1], shifts[1])
    unused, norm_back = jax.vjp(
        lambda field_in: layer_norm(field_in, gains[1], shifts[1]), second_sum
    )
    grad_second = norm_back(cotangent.astype(jnp.float32))[0]
    grad_feed_round = grad_second.astype(jnp.bfloat16)
    seq_grad_feed = lax.all_gather(grad_feed_round, "tp", axis=0, tiled=True)
    up_back, down_back = (
        lax.all_gather(up_weight, "fsdp", axis=0, tiled=True),
        lax.all_gather(down_weight, "fsdp", axis=1, tiled=True),
    )
    grad_low_down = mixed_dot(seq_grad_feed, second_d.T)
    grad_act = jnp.einsum(
        "sd,fd->sf", seq_grad_feed, down_back, preferred_element_type=jnp.float32
    ) + precise_dot(grad_low_down, first_d.astype(jnp.float32).T)
    unused, gelu_back = jax.vjp(lambda field_in: jax.nn.gelu(field_in, approximate=True), pre_act)
    grad_pre_round = gelu_back(grad_act)[0].astype(jnp.bfloat16)
    grad_down_out_part = precise_dot(low_down.T, seq_grad_feed.astype(jnp.float32))
    grad_down_in_part = precise_dot(act_round.astype(jnp.float32).T, grad_low_down)
    grad_low_up = mixed_dot(grad_pre_round, second_u.T)
    grad_up_out_part = precise_dot(low_up.T, grad_pre_round.astype(jnp.float32))
    grad_up_in_part = precise_dot(seq_normed.astype(jnp.float32).T, grad_low_up)
    first_u_wide = first_u.astype(jnp.float32)
    row_part = grad_pre_round
    low_part = grad_low_up
    grad_normed = grad_second + lax.psum_scatter(
        jnp.einsum("sf,df->sd", row_part, up_back, preferred_element_type=jnp.float32)
        + precise_dot(low_part, first_u_wide.T),
        "tp",
        scatter_dimension=0,
        tiled=True,
    )
    unused, norm_front = jax.vjp(
        lambda field_in: layer_norm(field_in, gains[0], shifts[0]), first_sum
    )
    grad_first = norm_front(grad_normed)[0]
    grad_branch_round = grad_first.astype(jnp.bfloat16)
    seq_grad_branch = lax.all_gather(grad_branch_round, "tp", axis=0, tiled=True)
    qkv_back, proj_back = (
        lax.all_gather(qkv_weight, "fsdp", axis=1, tiled=True),
        lax.all_gather(proj_weight, "fsdp", axis=1, tiled=True),
    )
    grad_low_attn = mixed_dot(seq_grad_branch, second_o.T)
    grad_attended = jnp.einsum(
        "sd,cd->sc", seq_grad_branch, proj_back, preferred_element_type=jnp.float32
    ) + precise_dot(grad_low_attn, first_o.astype(jnp.float32).T)
    grad_attended_round = grad_attended.astype(jnp.bfloat16)
    grad_attn_out_part = precise_dot(low_attn.T, seq_grad_branch.astype(jnp.float32))
    grad_attn_in_part = precise_dot(attended.astype(jnp.float32).T, grad_low_attn)
    grad_blocks = grad_attended_round.reshape(blocks, block_rows, heads_local, HEAD)

    def backward_block(carry, inputs):
        grad_keys, grad_values = carry
        query_rows, seg_rows, lse_rows, grad_rows = inputs
        scores = scores_of(query_rows, seg_rows)
        attn_probs = jnp.exp(scores - lse_rows[..., None])
        grad_probs = jnp.einsum(
            "bhe,she->hbs", grad_rows, values, preferred_element_type=jnp.float32
        )
        centre = jnp.sum(grad_probs * attn_probs, axis=-1, keepdims=True)
        grad_scores = (attn_probs * (grad_probs - centre)).astype(jnp.bfloat16)
        grad_query = (
            jnp.einsum("hbs,she->bhe", grad_scores, keys, preferred_element_type=jnp.float32)
            * score_scale
        )
        grad_keys = (
            grad_keys
            + jnp.einsum(
                "hbs,bhe->she", grad_scores, query_rows, preferred_element_type=jnp.float32
            )
            * score_scale
        )
        grad_values = grad_values + jnp.einsum(
            "hbs,bhe->she",
            attn_probs.astype(jnp.bfloat16),
            grad_rows,
            preferred_element_type=jnp.float32,
        )
        return ((grad_keys, grad_values), grad_query)

    zero_state = jnp.zeros((seq_rows, heads_local, HEAD), jnp.float32)
    key_value_grads, grad_queries = lax.scan(
        backward_block, (zero_state, zero_state), (query_blocks, seg_blocks, logsum, grad_blocks)
    )
    grad_qkv_round = jnp.stack(
        [
            grad_queries.reshape(seq_rows, width_local),
            key_value_grads[0].reshape(seq_rows, width_local),
            key_value_grads[1].reshape(seq_rows, width_local),
        ]
    ).astype(jnp.bfloat16)
    grad_qkv_out_part = jnp.einsum(
        "jsr,jsc->jrc", low_in, grad_qkv_round.astype(jnp.float32), precision=lax.Precision.HIGHEST
    )
    grad_low_qkv = jnp.einsum(
        "jsc,jrc->jsr", grad_qkv_round, second_q, preferred_element_type=jnp.float32
    )
    grad_qkv_in_part = jnp.einsum(
        "sd,jsr->jdr", seq_hidden.astype(jnp.float32), grad_low_qkv, precision=lax.Precision.HIGHEST
    )
    first_q_wide = first_q.astype(jnp.float32)
    row_part = grad_qkv_round
    low_part = grad_low_qkv
    grad_input = grad_first + lax.psum_scatter(
        (
            jnp.einsum("jsc,jdc->sd", row_part, qkv_back, preferred_element_type=jnp.float32)
            + jnp.einsum("jsr,jdr->sd", low_part, first_q_wide, precision=lax.Precision.HIGHEST)
        ).astype(jnp.bfloat16),
        "tp",
        scatter_dimension=0,
        tiled=True,
    ).astype(jnp.float32)
    wide_grads = lax.psum(
        (
            place_set(grad_qkv_in_part, chosen, sets, 1),
            place_set(grad_attn_out_part, chosen, sets, 0),
            place_set(grad_up_in_part, chosen, sets, 0),
            place_set(grad_down_out_part, chosen, sets, 0),
        ),
        ("fsdp", "tp"),
    )
    split_grads = (
        lax.psum(place_set(grad_qkv_out_part, chosen, sets, 1).astype(jnp.bfloat16), "fsdp").astype(
            jnp.float32
        ),
        lax.psum(place_set(grad_attn_in_part, chosen, sets, 0).astype(jnp.bfloat16), "fsdp").astype(
            jnp.float32
        ),
        lax.psum(place_set(grad_up_out_part, chosen, sets, 0).astype(jnp.bfloat16), "fsdp").astype(
            jnp.float32
        ),
        lax.psum(place_set(grad_down_in_part, chosen, sets, 0).astype(jnp.bfloat16), "fsdp").astype(
            jnp.float32
        ),
    )
    return (
        layer_out,
        grad_input,
        wide_grads[0],
        split_grads[0],
        split_grads[1],
        wide_grads[1],
        wide_grads[2],
        split_grads[2],
        split_grads[3],
        wide_grads[3],
    )


def dot_nn(left, right):
    return jnp.dot(left, right, preferred_element_type=F32)


def dot_nt(left, right):
    return lax.dot_general(left, right, (((1,), (1,)), ((), ())), preferred_element_type=F32)


def flip(index, mask):
    out, bit = index, 1
    while bit <= mask:
        if mask & bit:
            out = out + bit - 2 * bit * lax.rem(lax.div(index, bit), 2)
        bit *= 2
    return out


def norm_parts(rows):
    centred = rows - jnp.mean(rows, axis=-1, keepdims=True)
    spread = jnp.mean(centred * centred, axis=-1, keepdims=True)
    rstd = lax.rsqrt(spread + 1e-05)
    return centred * rstd, rstd


def norm_pull(grad, unit, rstd):
    return rstd * (
        grad
        - jnp.mean(grad, axis=-1, keepdims=True)
        - unit * jnp.mean(grad * unit, axis=-1, keepdims=True)
    )


class Gather:
    def __init__(self, which, shard, whole, send, recv, fsdp, tp, count):
        self.which, self.shard, self.whole = which, shard, whole
        self.send, self.recv, self.fsdp, self.tp = send, recv, fsdp, tp
        bits = [1 << i for i in range(1, count.bit_length() - 1)]
        self.orders = [bits, bits[::-1]]
        self.steps = len(bits)
        self.held = [[0], [0]]
        self.sent = []
        self.count = count

    def copy(self, half, mask, bit):
        landed = mask ^ bit
        place = self.whole(flip(self.fsdp, mask), half)
        return pltpu.make_async_remote_copy(
            src_ref=self.shard(half) if mask == 0 else place,
            dst_ref=place,
            send_sem=self.send.at[self.which, half, landed],
            recv_sem=self.recv.at[self.which, half, landed],
            device_id=(flip(self.fsdp, bit), self.tp),
            device_id_type=MESH,
        )

    def launch(self, half, mask, bit):
        self.copy(half, mask, bit).start()
        self.sent.append((half, mask, bit))

    def await_block(self, half, mask, bit):
        place = self.whole(flip(self.fsdp, mask), half)
        pltpu.make_async_remote_copy(
            src_ref=place,
            dst_ref=place,
            send_sem=self.send.at[self.which, half, mask],
            recv_sem=self.recv.at[self.which, half, mask],
            device_id=(flip(self.fsdp, bit), self.tp),
            device_id_type=MESH,
        ).wait_recv()

    def stage(self, step):
        for half in range(2):
            fresh = [0]
            if step > 0:
                bit = self.orders[half][step - 1]
                fresh = [mask ^ bit for mask in self.held[half]]
                for mask in fresh:
                    self.await_block(half, mask, bit)
                self.held[half] = self.held[half] + fresh
            if step < self.steps:
                for mask in self.held[half]:
                    self.launch(half, mask, self.orders[half][step])
            for mask in fresh:
                self.launch(half, mask, 1)

    def finish(self):
        for half in range(2):
            for mask in self.held[half]:
                self.await_block(half, mask ^ 1, 1)

    def drain(self):
        for half, mask, bit in self.sent:
            self.copy(half, mask, bit).wait_send()


def layer_kernel(cfg, *refs):
    F, T, S, D, H, FL, C = (cfg[k] for k in ("F", "T", "S", "D", "H", "FL", "C"))
    Q, heads, block = S // T, H // HEAD, D // F
    R = Q // C
    M = T * R
    NT = min(256, FL)
    (
        hidden_in, cotangent, seg_row, seg_col, chosen, qkv_w, proj_w, up_w, down_w,
        side_bias, up_bias, qkv_bias, gains, shifts,
        q_in, q_out, o_in, o_out, u_in, u_out, d_in, d_out,
        layer_out, grad_input, feed_all, units_all, mix_all, heads_all,
        hidden, qkv_all, proj_all, up_all, down_all,
        qkv, probs, mixed, normed, act, slope, grad_feed, grad_pre, grad_branch, grad_mixed, grad_qkv,
        part, from_low, from_high, unit_one, rstd_one, grad_own,
        low_q, low_o, low_u, low_d, back_q, back_o, back_u, back_d,
        wide_f, heads_f, units_f, wide_stage, heads_stage, units_stage,
        feed_part, feed_land, feed_full, mix_part, mix_land, mix_full, units_g, heads_g,
        stage_sem, deal_send, deal_recv, share_send, share_recv,
        w_send, w_recv, up_send, up_recv, dn_send, dn_recv, g_up_send, g_up_recv, g_dn_send, g_dn_recv,
        own_sem,
    ) = refs
    f, z = lax.axis_index("fsdp"), lax.axis_index("tp")
    bits = [1 << i for i in range(F.bit_length() - 1)]

    barrier = pltpu.get_barrier_semaphore()
    for bit in bits:
        pl.semaphore_signal(barrier, inc=1, device_id=(flip(f, bit), z), device_id_type=MESH)

    turns = [lax.rem(z + k, T) for k in range(T)]
    for k in range(1, T):
        pl.semaphore_signal(barrier, inc=1, device_id=(f, turns[k]), device_id_type=MESH)
    pl.semaphore_wait(barrier, len(bits) + T - 1)

    rows_of = lambda total, half: pl.ds(half * (total // 2), total // 2)
    gathers = [
        Gather(0, lambda h: qkv_w.at[:, rows_of(block, h)], lambda g, h: qkv_all.at[:, g, rows_of(block, h)], w_send, w_recv, f, z, F),
        Gather(1, lambda h: proj_w.at[rows_of(H, h)], lambda g, h: proj_all.at[g, rows_of(H, h)], w_send, w_recv, f, z, F),
        Gather(2, lambda h: up_w.at[rows_of(block, h)], lambda g, h: up_all.at[g, rows_of(block, h)], w_send, w_recv, f, z, F),
        Gather(3, lambda h: down_w.at[rows_of(FL, h)], lambda g, h: down_all.at[g, rows_of(FL, h)], w_send, w_recv, f, z, F),
    ]
    pair = lambda ref, n: lambda h: ref.at[..., rows_of(n, h), :]
    pair_all = lambda ref, n: lambda g, h: ref.at[g, ..., rows_of(n, h), :]
    for k, (shard, whole) in enumerate(
        [(feed_full, feed_all), (units_g, units_all), (mix_full, mix_all), (heads_g, heads_all)]
    ):
        n = shard.shape[-2]
        gathers.append(Gather(4 + k, pair(shard, n), pair_all(whole, n), w_send, w_recv, f, z, F))
    K = gathers[0].steps
    own_copies = [
        pltpu.make_async_copy(hidden_in, hidden.at[:, z], own_sem.at[0]),
        pltpu.make_async_copy(qkv_w, qkv_all.at[:, f], own_sem.at[1]),
        pltpu.make_async_copy(proj_w, proj_all.at[f], own_sem.at[2]),
        pltpu.make_async_copy(up_w, up_all.at[f], own_sem.at[3]),
        pltpu.make_async_copy(down_w, down_all.at[f], own_sem.at[4]),
    ]
    own_grads = [
        pltpu.make_async_copy(feed_full, feed_all.at[f], own_sem.at[5]),
        pltpu.make_async_copy(units_g, units_all.at[f], own_sem.at[6]),
        pltpu.make_async_copy(mix_full, mix_all.at[f], own_sem.at[7]),
        pltpu.make_async_copy(heads_g, heads_all.at[f], own_sem.at[8]),
    ]

    def deal_copy(which, part_ref, land_ref, k):
        return pltpu.make_async_remote_copy(
            src_ref=part_ref.at[turns[k]], dst_ref=land_ref.at[k - 1],
            send_sem=deal_send.at[which, k - 1], recv_sem=deal_recv.at[which, k - 1],
            device_id=(f, turns[k]), device_id_type=MESH,
        )

    def share_copy(which, full_ref, k, place):
        return pltpu.make_async_remote_copy(
            src_ref=full_ref.at[place], dst_ref=full_ref.at[place],
            send_sem=share_send.at[which, k - 1], recv_sem=share_recv.at[which, k - 1],
            device_id=(f, turns[k]), device_id_type=MESH,
        )

    exchanges = [(feed_part, feed_land, feed_full), (mix_part, mix_land, mix_full)]

    def deal(which):
        for k in range(1, T):
            deal_copy(which, exchanges[which][0], exchanges[which][1], k).start()

    def share(which):
        part_ref, land_ref, full_ref = exchanges[which]
        total = part_ref[z].astype(F32)
        for k in range(1, T):
            deal_copy(which, part_ref, land_ref, k).wait_recv()
            total += land_ref[k - 1].astype(F32)
        full_ref[z] = total.astype(BF16)
        for k in range(1, T):
            share_copy(which, full_ref, k, z).start()

    def pass_on(which):
        for k in range(1, T):
            share_copy(which, exchanges[which][2], k, turns[T - k]).wait_recv()
        for k in (2 * which, 2 * which + 1):
            own_grads[k].start()
            gathers[4 + k].stage(0)

    def pass_drain(which):
        for k in range(1, T):
            deal_copy(which, exchanges[which][0], exchanges[which][1], k).wait_send()
            share_copy(which, exchanges[which][2], k, z).wait_send()
        for k in (2 * which, 2 * which + 1):
            own_grads[k].wait()

    def line_copy(src, dst, send, recv, c, q, step):
        return pltpu.make_async_remote_copy(
            src_ref=src, dst_ref=dst, send_sem=send.at[c, q], recv_sem=recv.at[c, q],
            device_id=(f, z + step), device_id_type=MESH,
        )

    def rs_copy(c, q, step):
        landing, send, recv = (from_low, up_send, up_recv) if step > 0 else (from_high, dn_send, dn_recv)
        return line_copy(part.at[c, q], landing.at[c, q], send, recv, c, q, step)

    def rs_wait(c, q, step):
        landing, send, recv = (from_low, up_send, up_recv) if step > 0 else (from_high, dn_send, dn_recv)
        line_copy(landing.at[c, q], landing.at[c, q], send, recv, c, q, -step).wait_recv()

    def rs(c, t):
        def add(q, landing):
            part[c, q] = (part[c, q].astype(F32) + landing[c, q].astype(F32)).astype(BF16)

        @pl.when(z <= t - 1)
        def _():
            q = T - t + z

            @pl.when(z > 0)
            def _():
                rs_wait(c, q, 1)
                add(q, from_low)

            rs_copy(c, q, 1).start()

        @pl.when(z >= T - t)
        def _():
            q = z - (T - t)

            @pl.when(z < T - 1)
            def _():
                rs_wait(c, q, -1)
                add(q, from_high)

            rs_copy(c, q, -1).start()

    def rs_sum(c):
        @pl.when(z > 0)
        def _():
            rs_wait(c, z, 1)

        @pl.when(z < T - 1)
        def _():
            rs_wait(c, z, -1)

        return (part[c, z].astype(F32) + from_low[c, z].astype(F32)) + from_high[c, z].astype(F32)

    def rs_drain(c):
        for q in range(T):
            if q > 0:

                @pl.when(z < q)
                def _(q=q):
                    rs_copy(c, q, 1).wait_send()

            if q < T - 1:

                @pl.when(z > q)
                def _(q=q):
                    rs_copy(c, q, -1).wait_send()

    def ag_copy(buffer, c, q, step):
        send, recv = (g_up_send, g_up_recv) if step > 0 else (g_dn_send, g_dn_recv)
        if c is None:
            return line_copy(buffer.at[:, q], buffer.at[:, q], send, recv, C, q, step)
        return line_copy(buffer.at[c, q], buffer.at[c, q], send, recv, c, q, step)

    def ag_wait(buffer, c, q, step):
        send, recv = (g_up_send, g_up_recv) if step > 0 else (g_dn_send, g_dn_recv)
        place = buffer.at[:, q] if c is None else buffer.at[c, q]
        line_copy(place, place, send, recv, C if c is None else c, q, -step).wait_recv()

    def ag(buffer, c, t):
        if t == 1:

            @pl.when(z < T - 1)
            def _():
                ag_copy(buffer, c, z, 1).start()

            @pl.when(z > 0)
            def _():
                ag_copy(buffer, c, z, -1).start()

            return

        @pl.when(z >= t - 1)
        def _():
            q = z - (t - 1)
            ag_wait(buffer, c, q, 1)

            @pl.when(z < T - 1)
            def _():
                ag_copy(buffer, c, q, 1).start()

        @pl.when(z <= T - t)
        def _():
            q = z + (t - 1)
            ag_wait(buffer, c, q, -1)

            @pl.when(z > 0)
            def _():
                ag_copy(buffer, c, q, -1).start()

    def ag_drain(buffer, c):
        for q in range(T):

            @pl.when((z >= q) & (z < T - 1))
            def _(q=q):
                ag_copy(buffer, c, q, 1).wait_send()

            @pl.when((z <= q) & (z > 0))
            def _(q=q):
                ag_copy(buffer, c, q, -1).wait_send()

    a_q = lambda j: wide_f.at[j]
    b_o, a_u, b_d = wide_f.at[3], wide_f.at[4], wide_f.at[5]
    b_q = lambda j: heads_f.at[j]
    a_o = heads_f.at[3]
    b_u, a_d = units_f.at[0], units_f.at[1]
    line = lambda ref, k: ref[pl.ds(k, 1)].astype(F32)
    sets = q_in.shape[1]
    pick = (lax.broadcasted_iota(jnp.int32, (sets, 128), 0) == chosen[...]).astype(F32)

    def stage_copies(s):
        slot = s % 2
        pairs = [
            (q_in.at[:, s], wide_stage.at[slot, pl.ds(0, 3)]),
            (o_out.at[s], wide_stage.at[slot, 3]),
            (u_in.at[s], wide_stage.at[slot, 4]),
            (d_out.at[s], wide_stage.at[slot, 5]),
            (q_out.at[:, s], heads_stage.at[slot, pl.ds(0, 3)]),
            (o_in.at[s], heads_stage.at[slot, 3]),
            (u_out.at[s], units_stage.at[slot, 0]),
            (d_in.at[s], units_stage.at[slot, 1]),
        ]
        return [
            pltpu.make_async_copy(src, dst, stage_sem.at[slot, k])
            for k, (src, dst) in enumerate(pairs)
        ]

    def choose(s):
        for copy in stage_copies(s):
            copy.wait()
        weight = pick[s : s + 1, :1].astype(BF16)
        for stage, held in ((wide_stage, wide_f), (heads_stage, heads_f), (units_stage, units_f)):
            for k in range(held.shape[0]):
                term = stage[s % 2, k] * weight
                held[k] = term if s == 0 else held[k] + term
        if s + 2 < sets:
            for copy in stage_copies(s + 2):
                copy.start()

    def chunk(buffer, c):
        return buffer[c].reshape(M, buffer.shape[-1])

    def cols_of(g, size):
        return pl.ds(pl.multiple_of(g * size, size), size)

    def project():
        width = min(256, H)
        for j in range(3):
            low_j = dot_nt(hidden[...].reshape(S, D), a_q(j)[...]).astype(BF16)
            low_q[j] = low_j

            @pl.loop(0, H // width)
            def _(n, j=j, low_j=low_j):
                cols = cols_of(n, width)
                rows = dot_nn(hidden[...].reshape(S, D), qkv_all[j, :, :, cols].reshape(D, width))
                rows += dot_nn(low_j, b_q(j)[:, cols])
                if j != 1:
                    rows += qkv_bias[pl.ds(j // 2, 1), cols].astype(F32)
                qkv[j, :, cols] = rows.astype(BF16)

    scale = 1.0 / math.sqrt(HEAD)

    def attend():
        @pl.loop(0, heads)
        def _(h):
            cols = cols_of(h, HEAD)
            value_t = qkv[2, :, cols].T
            width = min(256, S)

            @pl.loop(0, S // width)
            def _(n):
                rows = cols_of(n, width)
                scores = dot_nt(qkv[1, :, cols], qkv[0, rows, cols]) * scale
                scores = jnp.where(seg_col[...] == seg_row[:, rows], scores, -1e30)
                weights = jnp.exp(scores - jnp.max(scores, axis=0, keepdims=True))
                weights = weights * (1.0 / jnp.sum(weights, axis=0, keepdims=True))
                low = weights.astype(BF16)
                probs[h, :, rows] = low
                mixed[rows, cols] = dot_nn(value_t, low).T.astype(BF16)

    def attend_back():
        @pl.loop(0, heads)
        def _(h):
            cols = cols_of(h, HEAD)
            key_t = qkv[1, :, cols].T
            width = min(256, S)

            @pl.loop(0, S // width)
            def _(n):
                rows = cols_of(n, width)
                weights = probs[h, :, rows].astype(F32)
                grad = dot_nt(qkv[2, :, cols], grad_mixed[rows, cols])
                centre = jnp.sum(grad * weights, axis=0, keepdims=True)
                low = (weights * (grad - centre)).astype(BF16)
                grad_scores[:, rows] = low
                grad_qkv[0, rows, cols] = (dot_nn(key_t, low).T * scale).astype(BF16)

            grad_qkv[1, :, cols] = (dot_nn(grad_scores[...], qkv[0, :, cols]) * scale).astype(BF16)
            grad_qkv[2, :, cols] = dot_nn(probs[h], grad_mixed[:, cols]).astype(BF16)

    grad_scores = slope.at[pl.ds(0, S), pl.ds(0, S)]

    def span(c):
        return pl.ds(c * M, M)

    def put_part(c, cols, rows):
        part[c, :, :, cols] = rows.astype(BF16).reshape(T, R, rows.shape[-1])

    def mix_out(c):
        low = dot_nt(mixed[span(c)], a_o[...]).astype(BF16)
        low_o[span(c)] = low

        @pl.loop(0, F)
        def _(g):
            cols = cols_of(g, block)
            put_part(c, cols, dot_nn(mixed[span(c)], proj_all[g]) + dot_nn(low, b_o[:, cols]))

    def feed_up(c):
        low = dot_nt(chunk(normed, c), a_u[...]).astype(BF16)
        low_u[span(c)] = low

        @pl.loop(0, FL // NT)
        def _(n):
            cols = cols_of(n, NT)
            pre = dot_nn(chunk(normed, c), up_all[:, :, cols].reshape(D, NT))
            pre += dot_nn(low, b_u[:, cols]) + up_bias[:, cols].astype(F32)
            square = pre * pre
            bend = jnp.tanh(ROOT * (pre + 0.044715 * square * pre))
            half = 0.5 * (1.0 + bend)
            act[span(c), cols] = (pre * half).astype(BF16)
            rise = half + 0.5 * pre * (1.0 - bend * bend) * (ROOT * (1.0 + 3 * 0.044715 * square))
            slope[span(c), cols] = rise.astype(BF16)

    def feed_down(c):
        low = dot_nt(act[span(c)], a_d[...]).astype(BF16)
        low_d[span(c)] = low

        @pl.loop(0, F)
        def _(g):
            cols = cols_of(g, block)
            put_part(c, cols, dot_nn(act[span(c)], down_all[g]) + dot_nn(low, b_d[:, cols]))

    def back_down(c):
        low = dot_nt(chunk(grad_feed, c), b_d[...]).astype(BF16)
        back_d[span(c)] = low

        @pl.loop(0, FL // NT)
        def _(n):
            cols = cols_of(n, NT)
            total = dot_nn(low, a_d[:, cols])
            for g in range(F):
                rows = grad_feed[c, :, :, pl.ds(g * block, block)].reshape(M, block)
                total += dot_nt(rows, down_all[g, cols])
            grad_pre[span(c), cols] = (total * slope[span(c), cols].astype(F32)).astype(BF16)

    def back_up(c):
        low = dot_nt(grad_pre[span(c)], b_u[...]).astype(BF16)
        back_u[span(c)] = low

        @pl.loop(0, F)
        def _(g):
            cols = cols_of(g, block)
            put_part(c, cols, dot_nt(grad_pre[span(c)], up_all[g]) + dot_nn(low, a_u[:, cols]))

    def back_mix(c):
        low = dot_nt(chunk(grad_branch, c), b_o[...]).astype(BF16)
        back_o[span(c)] = low
        total = dot_nn(low, a_o[...])
        for g in range(F):
            rows = grad_branch[c, :, :, pl.ds(g * block, block)].reshape(M, block)
            total += dot_nt(rows, proj_all[g])
        grad_mixed[span(c)] = total.astype(BF16)

    def back_project(c):
        lows = []
        for j in range(3):
            low = dot_nt(grad_qkv[j, span(c)], b_q(j)[...]).astype(BF16)
            back_q[j, span(c)] = low
            lows.append(low)

        @pl.loop(0, F)
        def _(g):
            cols = cols_of(g, block)
            total = dot_nn(lows[0], a_q(0)[:, cols])
            for j in range(3):
                if j:
                    total += dot_nn(lows[j], a_q(j)[:, cols])
                total += dot_nt(grad_qkv[j, span(c)], qkv_all[j, g])
            put_part(c, cols, total)

    def own(c):
        return pl.ds(c * R, R)

    def meet_one(c):
        total = rs_sum(c) + hidden[c, z].astype(F32) + line(side_bias, 0)
        unit, rstd = norm_parts(total)
        unit_one[own(c)] = unit
        rstd_one[own(c)] = jnp.broadcast_to(rstd, (R, 128))
        normed[c, z] = (unit * line(gains, 0) + line(shifts, 0)).astype(BF16)

    def meet_two(c):
        total = rs_sum(c) + unit_one[own(c)] * line(gains, 0) + line(shifts, 0) + line(side_bias, 1)
        unit, rstd = norm_parts(total)
        layer_out[own(c)] = unit * line(gains, 1) + line(shifts, 1)
        grad = norm_pull(cotangent[own(c)].astype(F32) * line(gains, 1), unit, rstd)
        grad_own[own(c)] = grad
        grad_feed[c, z] = grad.astype(BF16)

    def meet_three(c):
        grad = (grad_own[own(c)] + rs_sum(c)) * line(gains, 0)
        grad = norm_pull(grad, unit_one[own(c)], rstd_one[own(c)][:, :1])
        grad_own[own(c)] = grad
        grad_branch[c, z] = grad.astype(BF16)

    def meet_four(c):
        grad_input[own(c)] = grad_own[own(c)] + rs_sum(c)

    def factor(low, right):
        return dot_nn(low.astype(F32).T.astype(BF16), right).astype(BF16)

    def by_columns(low, right, place, row):
        turned = low.astype(F32).T.astype(BF16)
        for q in range(T):
            cols = pl.ds(q * H, H)
            rows = right[:, :, :, cols].reshape(S, H)
            place[q, pl.ds(row, 16)] = dot_nn(turned, rows).astype(BF16)

    def factors_feed():
        units_g[pl.ds(0, 16)] = factor(low_u[...], grad_pre[...])
        units_g[pl.ds(16, 16)] = factor(back_d[...], act[...])
        by_columns(back_u[...], normed, feed_part, 0)
        by_columns(low_d[...], grad_feed, feed_part, 16)

    def factors_mix():
        heads_g[pl.ds(48, 16)] = factor(back_o[...], mixed[...])
        by_columns(low_o[...], grad_branch, mix_part, 48)

    def factors_project():
        for j in range(3):
            heads_g[pl.ds(16 * j, 16)] = factor(low_q[j], grad_qkv[j])
            by_columns(back_q[j], hidden, mix_part, 16 * j)
        marks = jnp.concatenate([pick[:, :1], jnp.zeros((32 - sets, 1), F32)])
        heads_g[pl.ds(64, 32)] = jnp.broadcast_to(marks, (32, H)).astype(BF16)

    from_low[:, 0] = jnp.zeros((C, R, D), BF16)
    from_high[:, T - 1] = jnp.zeros((C, R, D), BF16)
    qkv_g = gathers[0]
    def own_hidden(step):
        return line_copy(hidden_in, hidden.at[:, z], g_up_send if step > 0 else g_dn_send, g_up_recv if step > 0 else g_dn_recv, C, z, step)

    @pl.when(z < T - 1)
    def _():
        own_hidden(1).start()

    @pl.when(z > 0)
    def _():
        own_hidden(-1).start()

    qkv_g.stage(0)
    for copy in own_copies + stage_copies(0) + stage_copies(1):
        copy.start()
    schedule(cfg, dict(locals()))


def schedule(cfg, env):
    T, C, K = cfg["T"], cfg["C"], env["K"]
    rs, ag, hidden = env["rs"], env["ag"], env["hidden"]
    qkv_g, proj_g, up_g, down_g = env["gathers"][:4]
    chunks = range(C)
    for s in range(2):
        env["choose"](s)
    for step in range(1, K + 1):
        qkv_g.stage(step)
        if step == 1:
            proj_g.stage(0)
            ag(hidden, None, 2)
            for s in range(2, 5):
                env["choose"](s)
    if K == 0:
        proj_g.stage(0)
    if K >= 1:
        proj_g.stage(1)
    up_g.stage(0)
    if K < 1:
        ag(hidden, None, 2)
        for s in range(2, 5):
            env["choose"](s)
    for s in range(5, env["sets"]):
        env["choose"](s)
    for t in range(3, T + 1):
        ag(hidden, None, t)
    for step in range(2, K + 1):
        proj_g.stage(step)
    down_g.stage(0)
    qkv_g.finish()
    for copy in env["own_copies"]:
        copy.wait()
    env["project"]()
    env["attend"]()
    if K:
        up_g.stage(1)
    proj_g.finish()
    buffers = [env["normed"], env["grad_feed"], env["grad_branch"]]
    meets = [env["meet_one"], env["meet_two"], env["meet_three"], env["meet_four"]]

    def work(k, c):
        if k > 0:
            env["rs_drain"](c)
        if k == 0:
            env["mix_out"](c)
        if k == 1:
            if c == 0:
                for step in range(2, K + 1):
                    up_g.stage(step)
                up_g.finish()
            env["feed_up"](c)
            if c == 0:
                for step in range(2, K + 1):
                    down_g.stage(step)
                down_g.finish()
            env["feed_down"](c)
        if k == 2:
            env["back_down"](c)
            env["back_up"](c)
        if k == 3:
            env["back_project"](c)
        rs(c, 1)

    def meet(k, c):
        meets[k](c)
        if k > 0:
            env["ag_drain"](buffers[k - 1], c)
        ag(buffers[k], c, 1)

    steps = []
    for k in range(3):
        steps.append((work, k))
        steps += [(lambda t, c: rs(c, t), t) for t in range(2, T)]
        steps.append((meet, k))
        steps += [(lambda kt, c: ag(buffers[kt[0]], c, kt[1]), (k, t)) for t in range(2, T + 1)]
    steps.append((lambda unused, c: env["back_mix"](c), None))
    lag = cfg["lag"]
    for at in range(len(steps) + lag * (C - 1)):
        if at == 1 and K:
            down_g.stage(1)
        for c in chunks:
            if 0 <= at - lag * c < len(steps):
                step, detail = steps[at - lag * c]
                step(detail, c)
        if at == 2 * (2 * T - 1) + 1 + lag * (C - 1):
            env["factors_feed"]()
            env["deal"](0)
    env["share"](0)
    env["attend_back"]()
    env["pass_on"](0)
    for c in chunks:
        work(3, c)
    env["factors_mix"]()
    env["factors_project"]()
    env["deal"](1)
    grads = env["gathers"][4:]
    for t in range(2, T):
        for c in chunks:
            rs(c, t)
        if t == 2:
            env["share"](1)
            for gather in grads[:2]:
                if K:
                    gather.stage(1)
    env["pass_on"](1)
    for c in chunks:
        meets[3](c)
    for step in range(2, K + 1):
        for gather in grads[:2]:
            gather.stage(step)
    for step in range(1, K + 1):
        for gather in grads[2:]:
            gather.stage(step)
    for gather in grads:
        gather.finish()
    for c in chunks:
        env["rs_drain"](c)
        env["ag_drain"](buffers[2], c)
    env["ag_drain"](hidden, None)
    for which in range(2):
        env["pass_drain"](which)
    for gather in env["gathers"]:
        gather.drain()


def spread(mesh, body):
    placed = (
        P(("fsdp", "tp"), None),
        P(("fsdp", "tp"), None),
        P("fsdp", None),
        P("fsdp"),
        P(None, "fsdp", "tp"),
        P(None, "tp"),
        P("tp", "fsdp"),
        P(),
        P("fsdp", "tp"),
        P("tp"),
        P("tp", "fsdp"),
        P(),
        P(),
        P(),
        P(),
        P(None, None, None, "tp"),
        P(None, "tp", None),
        P(),
        P(),
        P(None, None, "tp"),
        P(None, "tp", None),
        P(),
    )
    return jax.shard_map(
        body,
        mesh=mesh,
        in_specs=placed,
        out_specs=(
            P(("fsdp", "tp"), None),
            P(("fsdp", "tp"), None),
            P(),
            P(None, None, None, "tp"),
            P(None, "tp", None),
            P(),
            P(),
            P(None, None, "tp"),
            P(None, "tp", None),
            P(),
        ),
        check_vma=False,
    )


def chunks_for(rows):
    return max(c for c in (1, 2, 4) if rows % (16 * c) == 0)


def place_kernel(feed_all, units_all, mix_all, heads_all, *outs):
    q_in, q_out, o_in, o_out, u_in, u_out, d_in, d_out = outs
    F, T, _, H = feed_all.shape
    sets = o_in.shape[0]
    for ref in outs:
        ref[...] = jnp.zeros_like(ref)
    order = lax.broadcasted_iota(jnp.int32, (32, 1), 0).astype(F32)
    for g in range(F):
        marks = heads_all[g, pl.ds(64, 32), pl.ds(0, 128)][:, :1].astype(F32)
        s = jnp.minimum(jnp.sum(marks * order).astype(jnp.int32), sets - 1)
        for t in range(T):
            cols = pl.ds(t * H, H)
            u_in[s, :, cols] += feed_all[g, t, pl.ds(0, 16)].astype(F32)
            d_out[s, :, cols] += feed_all[g, t, pl.ds(16, 16)].astype(F32)
            o_out[s, :, cols] += mix_all[g, t, pl.ds(48, 16)].astype(F32)
            for j in range(3):
                q_in[j, s, :, cols] += mix_all[g, t, pl.ds(16 * j, 16)].astype(F32)
        for j in range(3):
            q_out[j, s] += heads_all[g, pl.ds(16 * j, 16)].astype(F32)
        o_in[s] += heads_all[g, pl.ds(48, 16)].astype(F32)
        u_out[s] += units_all[g, pl.ds(0, 16)].astype(F32)
        d_in[s] += units_all[g, pl.ds(16, 16)].astype(F32)


def kernel_per_device(F, T):
    def per_device(
        hidden_in, cotangent, segment_ids, adapter_set, qkv_weight, qkv_bias, proj_weight, proj_bias,
        up_weight, up_bias, down_weight, down_bias, norm_gain, norm_bias, qkv_adapt_in, qkv_adapt_out,
        attn_adapt_in, attn_adapt_out, up_adapt_in, up_adapt_out, down_adapt_in, down_adapt_out,
    ):
        Q, D = hidden_in.shape
        H, FL = qkv_weight.shape[2], up_weight.shape[1]
        S, C, sets = Q * T, chunks_for(Q), qkv_adapt_in.shape[1]
        R, block = Q // C, D // F
        cfg = dict(F=F, T=T, S=S, D=D, H=H, FL=FL, C=C, lag=1)
        turn = lambda table: jnp.swapaxes(table, -1, -2)
        segments = segment_ids[0].reshape(T, C, R).transpose(1, 0, 2).reshape(S)
        vmem, anywhere = pl.BlockSpec(memory_space=pltpu.VMEM), pl.BlockSpec(memory_space=pl.ANY)
        dma = pltpu.SemaphoreType.DMA
        bank = lambda *shape: pltpu.VMEM(shape, BF16)
        wide_bank = lambda *shape: pltpu.VMEM(shape, F32)
        scratch = (
            [bank(C, T, R, D), bank(3, F, block, H), bank(F, H, block), bank(F, block, FL), bank(F, FL, block)]
            + [bank(3, S, H), bank(H // HEAD, S, S), bank(S, H), bank(C, T, R, D), bank(S, FL), bank(S, FL)]
            + [bank(C, T, R, D), bank(S, FL), bank(C, T, R, D), bank(S, H), bank(3, S, H)]
            + [bank(C, T, R, D), bank(C, T, R, D), bank(C, T, R, D)]
            + [wide_bank(Q, D), wide_bank(Q, 128), wide_bank(Q, D)]
            + [bank(3, S, RANK), bank(S, RANK), bank(S, RANK), bank(S, RANK)] * 2
            + [bank(6, RANK, D), bank(4, RANK, H), bank(2, RANK, FL)]
            + [bank(2, 6, RANK, D), bank(2, 4, RANK, H), bank(2, 2, RANK, FL)]
            + [bank(T, 32, H), bank(T - 1, 32, H), bank(T, 32, H)]
            + [bank(T, 64, H), bank(T - 1, 64, H), bank(T, 64, H)]
            + [bank(32, FL), bank(96, H)]
            + [dma((2, 8))] + [dma((2, T - 1))] * 4
            + [dma((8, 2, F)), dma((8, 2, F))]
            + [dma((C, T))] * 4
            + [dma((C + 1, T))] * 4
            + [dma((9,))]
        )
        flops = 2 * S * (4 * D * H + 2 * D * FL) * 2
        outs = pl.pallas_call(
            functools.partial(layer_kernel, cfg),
            out_shape=[
                jax.ShapeDtypeStruct((Q, D), F32),
                jax.ShapeDtypeStruct((Q, D), F32),
                jax.ShapeDtypeStruct((F, T, 32, H), BF16),
                jax.ShapeDtypeStruct((F, 32, FL), BF16),
                jax.ShapeDtypeStruct((F, T, 64, H), BF16),
                jax.ShapeDtypeStruct((F, 96, H), BF16),
            ],
            in_specs=[anywhere] + [vmem] * 4 + [anywhere] * 4 + [vmem] * 5 + [anywhere] * 8,
            out_specs=[vmem] * 2 + [anywhere] * 4,
            scratch_shapes=scratch,
            compiler_params=pltpu.CompilerParams(
                collective_id=0, has_side_effects=True, vmem_limit_bytes=62 * 1024 * 1024
            ),
            cost_estimate=pl.CostEstimate(flops=flops, bytes_accessed=30000000, transcendentals=0),
        )(
            hidden_in.reshape(C, R, D), cotangent, segments[None, :], segments[:, None],
            adapter_set[None, :], qkv_weight, proj_weight, up_weight, down_weight,
            jnp.stack([proj_bias, down_bias]), up_bias[None, :], qkv_bias, norm_gain, norm_bias,
            turn(qkv_adapt_in), qkv_adapt_out, turn(attn_adapt_in), attn_adapt_out,
            turn(up_adapt_in), up_adapt_out, turn(down_adapt_in), down_adapt_out,
        )
        layer_out, grad_input = outs[:2]
        table = lambda *shape: jax.ShapeDtypeStruct(shape, F32)
        q_in, q_out, o_in, o_out, u_in, u_out, d_in, d_out = pl.pallas_call(
            place_kernel,
            out_shape=[
                table(3, sets, RANK, D), table(3, sets, RANK, H), table(sets, RANK, H), table(sets, RANK, D),
                table(sets, RANK, D), table(sets, RANK, FL), table(sets, RANK, FL), table(sets, RANK, D),
            ],
            in_specs=[vmem] * 4,
            out_specs=[vmem] * 8,
            compiler_params=pltpu.CompilerParams(vmem_limit_bytes=40 * 1024 * 1024),
        )(*outs[2:])
        return (
            layer_out, grad_input, turn(q_in), q_out, turn(o_in), o_out, turn(u_in), u_out, turn(d_in), d_out,
        )

    return per_device


def solution(mesh):
    F, T = mesh.shape["fsdp"], mesh.shape["tp"]

    def whole(*args):
        width = args[0].shape[1]
        fits = F & (F - 1) == 0 and (width // F) % 128 == 0 and T > 1 and F > 1 and args[14].shape[1] <= 32
        return spread(mesh, kernel_per_device(F, T) if fits else per_device)(*args)

    return whole
```

```python
import functools
import math

import jax
import jax.numpy as jnp
from jax import lax
from jax.experimental import pallas as pl
from jax.experimental.pallas import tpu as pltpu
from jax.sharding import PartitionSpec as P

HEAD = 128
RANK = 16
MESH = pl.DeviceIdType.MESH
F32 = jnp.float32
BF16 = jnp.bfloat16
ROOT = math.sqrt(2.0 / math.pi)


def layer_norm(field_in, gain_row, shift_row):
    centre = jnp.mean(field_in, axis=-1, keepdims=True)
    centred = field_in - centre
    spread = jnp.mean(centred * centred, axis=-1, keepdims=True)
    return centred * lax.rsqrt(spread + 1e-05) * gain_row + shift_row


def precise_dot(left, right):
    return jnp.dot(left, right, precision=lax.Precision.HIGHEST)


def mixed_dot(left, right):
    return jnp.dot(left, right, preferred_element_type=jnp.float32)


def choose_set(table, index, axis):
    return lax.dynamic_index_in_dim(table, index, axis, keepdims=False)


def place_set(grad, index, sets, axis):
    onehot = (jnp.arange(sets) == index).astype(jnp.float32)
    shape_list = [1] * (grad.ndim + 1)
    shape_list[axis] = sets
    return jnp.expand_dims(grad, axis) * onehot.reshape(shape_list)


def per_device(
    hidden_in,
    cotangent,
    segment_ids,
    adapter_set,
    qkv_weight,
    qkv_bias,
    proj_weight,
    proj_bias,
    up_weight,
    up_bias,
    down_weight,
    down_bias,
    norm_gain,
    norm_bias,
    qkv_adapt_in,
    qkv_adapt_out,
    attn_adapt_in,
    attn_adapt_out,
    up_adapt_in,
    up_adapt_out,
    down_adapt_in,
    down_adapt_out,
):
    width_local = qkv_weight.shape[2]
    heads_local = width_local // HEAD
    sets = qkv_adapt_in.shape[1]
    chosen = adapter_set[0]
    segments = segment_ids[0]
    seq_rows = segments.shape[0]
    block_rows = min(512, seq_rows)
    blocks = seq_rows // block_rows
    score_scale = 1.0 / math.sqrt(HEAD)
    gains = norm_gain.astype(jnp.float32)
    shifts = norm_bias.astype(jnp.float32)
    first_q = choose_set(qkv_adapt_in, chosen, 1)
    second_q = choose_set(qkv_adapt_out, chosen, 1)
    first_o = choose_set(attn_adapt_in, chosen, 0)
    second_o = choose_set(attn_adapt_out, chosen, 0)
    first_u = choose_set(up_adapt_in, chosen, 0)
    second_u = choose_set(up_adapt_out, chosen, 0)
    first_d = choose_set(down_adapt_in, chosen, 0)
    second_d = choose_set(down_adapt_out, chosen, 0)
    seq_hidden = lax.all_gather(hidden_in, "tp", axis=0, tiled=True)
    qkv_full, proj_full = (
        lax.all_gather(qkv_weight, "fsdp", axis=1, tiled=True),
        lax.all_gather(proj_weight, "fsdp", axis=1, tiled=True),
    )
    main_term = jnp.einsum("sd,jdc->jsc", seq_hidden, qkv_full, preferred_element_type=jnp.float32)
    low_in = jnp.einsum("sd,jdr->jsr", seq_hidden, first_q, preferred_element_type=jnp.float32)
    low_term = jnp.einsum(
        "jsr,jrc->jsc", low_in, second_q.astype(jnp.float32), precision=lax.Precision.HIGHEST
    )
    bias_rows = jnp.stack([qkv_bias[0], jnp.zeros_like(qkv_bias[0]), qkv_bias[1]]).astype(
        jnp.float32
    )[:, None, :]
    qkv_round = (main_term + low_term + bias_rows).astype(jnp.bfloat16)
    queries = qkv_round[0].reshape(seq_rows, heads_local, HEAD)
    keys = qkv_round[1].reshape(seq_rows, heads_local, HEAD)
    values = qkv_round[2].reshape(seq_rows, heads_local, HEAD)
    query_blocks = queries.reshape(blocks, block_rows, heads_local, HEAD)
    seg_blocks = segments.reshape(blocks, block_rows)

    def scores_of(query_rows, seg_rows):
        raw_scores = (
            jnp.einsum("bhe,she->hbs", query_rows, keys, preferred_element_type=jnp.float32)
            * score_scale
        )
        same_doc = (seg_rows[:, None] == segments[None, :])[None]
        return jnp.where(same_doc, raw_scores, -1e30)

    def forward_block(inputs):
        query_rows, seg_rows = inputs
        scores = scores_of(query_rows, seg_rows)
        row_top = jnp.max(scores, axis=-1, keepdims=True)
        weights = jnp.exp(scores - row_top)
        row_total = jnp.sum(weights, axis=-1, keepdims=True)
        attn_probs = (weights / row_total).astype(jnp.bfloat16)
        attn_mixed = jnp.einsum(
            "hbs,she->bhe", attn_probs, values, preferred_element_type=jnp.float32
        )
        return (attn_mixed, (row_top + jnp.log(row_total))[..., 0])

    attn_mixed, logsum = lax.map(forward_block, (query_blocks, seg_blocks))
    attended = attn_mixed.reshape(seq_rows, width_local).astype(jnp.bfloat16)
    low_attn = mixed_dot(attended, first_o)
    second_o_wide = second_o.astype(jnp.float32)
    row_part = attended
    low_part = low_attn
    attn_sum = lax.psum_scatter(
        mixed_dot(row_part, proj_full) + precise_dot(low_part, second_o_wide),
        "tp",
        scatter_dimension=0,
        tiled=True,
    )
    first_sum = hidden_in.astype(jnp.float32) + attn_sum + proj_bias.astype(jnp.float32)
    normed = layer_norm(first_sum, gains[0], shifts[0])
    normed_round = normed.astype(jnp.bfloat16)
    seq_normed = lax.all_gather(normed_round, "tp", axis=0, tiled=True)
    up_full, down_full = (
        lax.all_gather(up_weight, "fsdp", axis=0, tiled=True),
        lax.all_gather(down_weight, "fsdp", axis=1, tiled=True),
    )
    low_up = mixed_dot(seq_normed, first_u)
    pre_act = (
        mixed_dot(seq_normed, up_full)
        + precise_dot(low_up, second_u.astype(jnp.float32))
        + up_bias.astype(jnp.float32)
    )
    act_round = jax.nn.gelu(pre_act, approximate=True).astype(jnp.bfloat16)
    low_down = mixed_dot(act_round, first_d)
    second_d_wide = second_d.astype(jnp.float32)
    row_part = act_round
    low_part = low_down
    ffn_sum = lax.psum_scatter(
        mixed_dot(row_part, down_full) + precise_dot(low_part, second_d_wide),
        "tp",
        scatter_dimension=0,
        tiled=True,
    )
    second_sum = normed + ffn_sum + down_bias.astype(jnp.float32)
    layer_out = layer_norm(second_sum, gains[1], shifts[1])
    unused, norm_back = jax.vjp(
        lambda field_in: layer_norm(field_in, gains[1], shifts[1]), second_sum
    )
    grad_second = norm_back(cotangent.astype(jnp.float32))[0]
    grad_feed_round = grad_second.astype(jnp.bfloat16)
    seq_grad_feed = lax.all_gather(grad_feed_round, "tp", axis=0, tiled=True)
    up_back, down_back = (
        lax.all_gather(up_weight, "fsdp", axis=0, tiled=True),
        lax.all_gather(down_weight, "fsdp", axis=1, tiled=True),
    )
    grad_low_down = mixed_dot(seq_grad_feed, second_d.T)
    grad_act = jnp.einsum(
        "sd,fd->sf", seq_grad_feed, down_back, preferred_element_type=jnp.float32
    ) + precise_dot(grad_low_down, first_d.astype(jnp.float32).T)
    unused, gelu_back = jax.vjp(lambda field_in: jax.nn.gelu(field_in, approximate=True), pre_act)
    grad_pre_round = gelu_back(grad_act)[0].astype(jnp.bfloat16)
    grad_down_out_part = precise_dot(low_down.T, seq_grad_feed.astype(jnp.float32))
    grad_down_in_part = precise_dot(act_round.astype(jnp.float32).T, grad_low_down)
    grad_low_up = mixed_dot(grad_pre_round, second_u.T)
    grad_up_out_part = precise_dot(low_up.T, grad_pre_round.astype(jnp.float32))
    grad_up_in_part = precise_dot(seq_normed.astype(jnp.float32).T, grad_low_up)
    first_u_wide = first_u.astype(jnp.float32)
    row_part = grad_pre_round
    low_part = grad_low_up
    grad_normed = grad_second + lax.psum_scatter(
        jnp.einsum("sf,df->sd", row_part, up_back, preferred_element_type=jnp.float32)
        + precise_dot(low_part, first_u_wide.T),
        "tp",
        scatter_dimension=0,
        tiled=True,
    )
    unused, norm_front = jax.vjp(
        lambda field_in: layer_norm(field_in, gains[0], shifts[0]), first_sum
    )
    grad_first = norm_front(grad_normed)[0]
    grad_branch_round = grad_first.astype(jnp.bfloat16)
    seq_grad_branch = lax.all_gather(grad_branch_round, "tp", axis=0, tiled=True)
    qkv_back, proj_back = (
        lax.all_gather(qkv_weight, "fsdp", axis=1, tiled=True),
        lax.all_gather(proj_weight, "fsdp", axis=1, tiled=True),
    )
    grad_low_attn = mixed_dot(seq_grad_branch, second_o.T)
    grad_attended = jnp.einsum(
        "sd,cd->sc", seq_grad_branch, proj_back, preferred_element_type=jnp.float32
    ) + precise_dot(grad_low_attn, first_o.astype(jnp.float32).T)
    grad_attended_round = grad_attended.astype(jnp.bfloat16)
    grad_attn_out_part = precise_dot(low_attn.T, seq_grad_branch.astype(jnp.float32))
    grad_attn_in_part = precise_dot(attended.astype(jnp.float32).T, grad_low_attn)
    grad_blocks = grad_attended_round.reshape(blocks, block_rows, heads_local, HEAD)

    def backward_block(carry, inputs):
        grad_keys, grad_values = carry
        query_rows, seg_rows, lse_rows, grad_rows = inputs
        scores = scores_of(query_rows, seg_rows)
        attn_probs = jnp.exp(scores - lse_rows[..., None])
        grad_probs = jnp.einsum(
            "bhe,she->hbs", grad_rows, values, preferred_element_type=jnp.float32
        )
        centre = jnp.sum(grad_probs * attn_probs, axis=-1, keepdims=True)
        grad_scores = (attn_probs * (grad_probs - centre)).astype(jnp.bfloat16)
        grad_query = (
            jnp.einsum("hbs,she->bhe", grad_scores, keys, preferred_element_type=jnp.float32)
            * score_scale
        )
        grad_keys = (
            grad_keys
            + jnp.einsum(
                "hbs,bhe->she", grad_scores, query_rows, preferred_element_type=jnp.float32
            )
            * score_scale
        )
        grad_values = grad_values + jnp.einsum(
            "hbs,bhe->she",
            attn_probs.astype(jnp.bfloat16),
            grad_rows,
            preferred_element_type=jnp.float32,
        )
        return ((grad_keys, grad_values), grad_query)

    zero_state = jnp.zeros((seq_rows, heads_local, HEAD), jnp.float32)
    key_value_grads, grad_queries = lax.scan(
        backward_block, (zero_state, zero_state), (query_blocks, seg_blocks, logsum, grad_blocks)
    )
    grad_qkv_round = jnp.stack(
        [
            grad_queries.reshape(seq_rows, width_local),
            key_value_grads[0].reshape(seq_rows, width_local),
            key_value_grads[1].reshape(seq_rows, width_local),
        ]
    ).astype(jnp.bfloat16)
    grad_qkv_out_part = jnp.einsum(
        "jsr,jsc->jrc", low_in, grad_qkv_round.astype(jnp.float32), precision=lax.Precision.HIGHEST
    )
    grad_low_qkv = jnp.einsum(
        "jsc,jrc->jsr", grad_qkv_round, second_q, preferred_element_type=jnp.float32
    )
    grad_qkv_in_part = jnp.einsum(
        "sd,jsr->jdr", seq_hidden.astype(jnp.float32), grad_low_qkv, precision=lax.Precision.HIGHEST
    )
    first_q_wide = first_q.astype(jnp.float32)
    row_part = grad_qkv_round
    low_part = grad_low_qkv
    grad_input = grad_first + lax.psum_scatter(
        (
            jnp.einsum("jsc,jdc->sd", row_part, qkv_back, preferred_element_type=jnp.float32)
            + jnp.einsum("jsr,jdr->sd", low_part, first_q_wide, precision=lax.Precision.HIGHEST)
        ).astype(jnp.bfloat16),
        "tp",
        scatter_dimension=0,
        tiled=True,
    ).astype(jnp.float32)
    wide_grads = lax.psum(
        (
            place_set(grad_qkv_in_part, chosen, sets, 1),
            place_set(grad_attn_out_part, chosen, sets, 0),
            place_set(grad_up_in_part, chosen, sets, 0),
            place_set(grad_down_out_part, chosen, sets, 0),
        ),
        ("fsdp", "tp"),
    )
    split_grads = (
        lax.psum(place_set(grad_qkv_out_part, chosen, sets, 1).astype(jnp.bfloat16), "fsdp").astype(
            jnp.float32
        ),
        lax.psum(place_set(grad_attn_in_part, chosen, sets, 0).astype(jnp.bfloat16), "fsdp").astype(
            jnp.float32
        ),
        lax.psum(place_set(grad_up_out_part, chosen, sets, 0).astype(jnp.bfloat16), "fsdp").astype(
            jnp.float32
        ),
        lax.psum(place_set(grad_down_in_part, chosen, sets, 0).astype(jnp.bfloat16), "fsdp").astype(
            jnp.float32
        ),
    )
    return (
        layer_out,
        grad_input,
        wide_grads[0],
        split_grads[0],
        split_grads[1],
        wide_grads[1],
        wide_grads[2],
        split_grads[2],
        split_grads[3],
        wide_grads[3],
    )


def dot_nn(left, right):
    return jnp.dot(left, right, preferred_element_type=F32)


def dot_nt(left, right):
    return lax.dot_general(left, right, (((1,), (1,)), ((), ())), preferred_element_type=F32)


def flip(index, mask):
    out, bit = index, 1
    while bit <= mask:
        if mask & bit:
            out = out + bit - 2 * bit * lax.rem(lax.div(index, bit), 2)
        bit *= 2
    return out


def norm_parts(rows):
    centred = rows - jnp.mean(rows, axis=-1, keepdims=True)
    spread = jnp.mean(centred * centred, axis=-1, keepdims=True)
    rstd = lax.rsqrt(spread + 1e-05)
    return centred * rstd, rstd


def norm_pull(grad, unit, rstd):
    return rstd * (
        grad
        - jnp.mean(grad, axis=-1, keepdims=True)
        - unit * jnp.mean(grad * unit, axis=-1, keepdims=True)
    )


class Gather:
    def __init__(self, which, shard, whole, send, recv, fsdp, tp, count):
        self.which, self.shard, self.whole = which, shard, whole
        self.send, self.recv, self.fsdp, self.tp = send, recv, fsdp, tp
        bits = [1 << i for i in range(1, count.bit_length() - 1)]
        self.orders = [bits, bits[::-1]]
        self.steps = len(bits)
        self.held = [[0], [0]]
        self.sent = []
        self.count = count

    def copy(self, half, mask, bit):
        landed = mask ^ bit
        place = self.whole(flip(self.fsdp, mask), half)
        return pltpu.make_async_remote_copy(
            src_ref=self.shard(half) if mask == 0 else place,
            dst_ref=place,
            send_sem=self.send.at[self.which, half, landed],
            recv_sem=self.recv.at[self.which, half, landed],
            device_id=(flip(self.fsdp, bit), self.tp),
            device_id_type=MESH,
        )

    def launch(self, half, mask, bit):
        self.copy(half, mask, bit).start()
        self.sent.append((half, mask, bit))

    def await_block(self, half, mask, bit):
        place = self.whole(flip(self.fsdp, mask), half)
        pltpu.make_async_remote_copy(
            src_ref=place,
            dst_ref=place,
            send_sem=self.send.at[self.which, half, mask],
            recv_sem=self.recv.at[self.which, half, mask],
            device_id=(flip(self.fsdp, bit), self.tp),
            device_id_type=MESH,
        ).wait_recv()

    def stage(self, step):
        for half in range(2):
            fresh = [0]
            if step > 0:
                bit = self.orders[half][step - 1]
                fresh = [mask ^ bit for mask in self.held[half]]
                for mask in fresh:
                    self.await_block(half, mask, bit)
                self.held[half] = self.held[half] + fresh
            if step < self.steps:
                for mask in self.held[half]:
                    self.launch(half, mask, self.orders[half][step])
            for mask in fresh:
                self.launch(half, mask, 1)

    def finish(self):
        for half in range(2):
            for mask in self.held[half]:
                self.await_block(half, mask ^ 1, 1)

    def drain(self):
        for half, mask, bit in self.sent:
            self.copy(half, mask, bit).wait_send()


def layer_kernel(cfg, *refs):
    F, T, S, D, H, FL, C = (cfg[k] for k in ("F", "T", "S", "D", "H", "FL", "C"))
    Q, heads, block = S // T, H // HEAD, D // F
    R = Q // C
    M = T * R
    NT = math.gcd(FL, 1024)
    (
        hidden_in, cotangent, segments, chosen, qkv_w, proj_w, up_w, down_w,
        proj_bias, down_bias, up_bias, qkv_bias, gains, shifts,
        q_in, q_out, o_in, o_out, u_in, u_out, d_in, d_out,
        layer_out, grad_input, feed_all, units_all, mix_all, heads_all,
        hidden, qkv_all, proj_all, up_all, down_all,
        qkv, probs, mixed, normed, act, slope, grad_feed, grad_branch, grad_mixed, grad_qkv,
        part, from_low, from_high, unit_one, rstd_one, grad_own,
        low_q, low_o, low_u, low_d, back_q, back_o, back_u, back_d,
        seg_row, seg_col, turned,
        wide_f, heads_f, units_f, wide_stage, heads_stage, units_stage,
        feed_part, feed_land, feed_full, mix_part, mix_land, mix_full, units_g, heads_g,
        stage_sem, deal_send, deal_recv, share_send, share_recv,
        w_send, w_recv, up_send, up_recv, dn_send, dn_recv, g_up_send, g_up_recv, g_dn_send, g_dn_recv,
        own_sem,
    ) = refs
    grad_pre = slope
    f, z = lax.axis_index("fsdp"), lax.axis_index("tp")
    bits = [1 << i for i in range(F.bit_length() - 1)]

    barrier = pltpu.get_barrier_semaphore()
    for bit in bits:
        pl.semaphore_signal(barrier, inc=1, device_id=(flip(f, bit), z), device_id_type=MESH)

    turns = [lax.rem(z + k, T) for k in range(T)]
    for k in range(1, T):
        pl.semaphore_signal(barrier, inc=1, device_id=(f, turns[k]), device_id_type=MESH)
    pl.semaphore_wait(barrier, len(bits) + T - 1)

    rows_of = lambda total, half: pl.ds(half * (total // 2), total // 2)
    gathers = [
        Gather(0, lambda h: qkv_w.at[:, rows_of(block, h)], lambda g, h: qkv_all.at[:, g, rows_of(block, h)], w_send, w_recv, f, z, F),
        Gather(1, lambda h: proj_w.at[rows_of(H, h)], lambda g, h: proj_all.at[g, rows_of(H, h)], w_send, w_recv, f, z, F),
        Gather(2, lambda h: up_w.at[rows_of(block, h)], lambda g, h: up_all.at[g, rows_of(block, h)], w_send, w_recv, f, z, F),
    ]
    quarter = lambda part, h: pl.ds((2 * part + h) * (FL // 4), FL // 4)
    for part_of in range(2):
        shard = lambda h, p=part_of: down_w.at[quarter(p, h)]
        whole = lambda g, h, p=part_of: down_all.at[g, quarter(p, h)]
        gathers.append(Gather(3 + part_of, shard, whole, w_send, w_recv, f, z, F))
    pair = lambda ref, n: lambda h: ref.at[..., rows_of(n, h), :]
    pair_all = lambda ref, n: lambda g, h: ref.at[g, ..., rows_of(n, h), :]
    for k, (shard, whole) in enumerate(
        [(feed_full, feed_all), (units_g, units_all), (mix_full, mix_all), (heads_g, heads_all)]
    ):
        n = shard.shape[-2]
        gathers.append(Gather(5 + k, pair(shard, n), pair_all(whole, n), w_send, w_recv, f, z, F))
    K = gathers[0].steps
    own_copies = [
        pltpu.make_async_copy(hidden_in, hidden.at[:, z], own_sem.at[0]),
        pltpu.make_async_copy(qkv_w, qkv_all.at[:, f], own_sem.at[1]),
        pltpu.make_async_copy(proj_w, proj_all.at[f], own_sem.at[2]),
        pltpu.make_async_copy(up_w, up_all.at[f], own_sem.at[3]),
        pltpu.make_async_copy(down_w, down_all.at[f], own_sem.at[4]),
    ]
    own_grads = [
        pltpu.make_async_copy(feed_full, feed_all.at[f], own_sem.at[5]),
        pltpu.make_async_copy(units_g, units_all.at[f], own_sem.at[6]),
        pltpu.make_async_copy(mix_full, mix_all.at[f], own_sem.at[7]),
        pltpu.make_async_copy(heads_g, heads_all.at[f], own_sem.at[8]),
    ]

    def deal_copy(which, part_ref, land_ref, k):
        return pltpu.make_async_remote_copy(
            src_ref=part_ref.at[turns[k]], dst_ref=land_ref.at[k - 1],
            send_sem=deal_send.at[which, k - 1], recv_sem=deal_recv.at[which, k - 1],
            device_id=(f, turns[k]), device_id_type=MESH,
        )

    def share_copy(which, full_ref, k, place):
        return pltpu.make_async_remote_copy(
            src_ref=full_ref.at[place], dst_ref=full_ref.at[place],
            send_sem=share_send.at[which, k - 1], recv_sem=share_recv.at[which, k - 1],
            device_id=(f, turns[k]), device_id_type=MESH,
        )

    exchanges = [(feed_part, feed_land, feed_full), (mix_part, mix_land, mix_full)]

    def deal(which):
        for k in range(1, T):
            deal_copy(which, exchanges[which][0], exchanges[which][1], k).start()

    def share(which):
        part_ref, land_ref, full_ref = exchanges[which]
        total = part_ref[z].astype(F32)
        for k in range(1, T):
            deal_copy(which, part_ref, land_ref, k).wait_recv()
            total += land_ref[k - 1].astype(F32)
        full_ref[z] = total.astype(BF16)
        for k in range(1, T):
            share_copy(which, full_ref, k, z).start()

    def pass_on(which):
        for k in range(1, T):
            share_copy(which, exchanges[which][2], k, turns[T - k]).wait_recv()
        for k in (2 * which, 2 * which + 1):
            own_grads[k].start()
            gathers[5 + k].stage(0)

    def pass_drain(which):
        for k in range(1, T):
            deal_copy(which, exchanges[which][0], exchanges[which][1], k).wait_send()
            share_copy(which, exchanges[which][2], k, z).wait_send()
        for k in (2 * which, 2 * which + 1):
            own_grads[k].wait()

    def line_copy(src, dst, send, recv, c, q, step):
        return pltpu.make_async_remote_copy(
            src_ref=src, dst_ref=dst, send_sem=send.at[c, q], recv_sem=recv.at[c, q],
            device_id=(f, z + step), device_id_type=MESH,
        )

    def rs_copy(c, q, step):
        landing, send, recv = (from_low, up_send, up_recv) if step > 0 else (from_high, dn_send, dn_recv)
        return line_copy(part.at[c, q], landing.at[c, q], send, recv, c, q, step)

    def rs_wait(c, q, step):
        landing, send, recv = (from_low, up_send, up_recv) if step > 0 else (from_high, dn_send, dn_recv)
        line_copy(landing.at[c, q], landing.at[c, q], send, recv, c, q, -step).wait_recv()

    def rs(c, t):
        def add(q, landing):
            part[c, q] = (part[c, q].astype(F32) + landing[c, q].astype(F32)).astype(BF16)

        @pl.when(z <= t - 1)
        def _():
            q = T - t + z

            @pl.when(z > 0)
            def _():
                rs_wait(c, q, 1)
                add(q, from_low)

            rs_copy(c, q, 1).start()

        @pl.when(z >= T - t)
        def _():
            q = z - (T - t)

            @pl.when(z < T - 1)
            def _():
                rs_wait(c, q, -1)
                add(q, from_high)

            rs_copy(c, q, -1).start()

    def rs_sum(c):
        @pl.when(z > 0)
        def _():
            rs_wait(c, z, 1)

        @pl.when(z < T - 1)
        def _():
            rs_wait(c, z, -1)

        return (part[c, z].astype(F32) + from_low[c, z].astype(F32)) + from_high[c, z].astype(F32)

    def rs_drain(c):
        for q in range(T):
            if q > 0:

                @pl.when(z < q)
                def _(q=q):
                    rs_copy(c, q, 1).wait_send()

            if q < T - 1:

                @pl.when(z > q)
                def _(q=q):
                    rs_copy(c, q, -1).wait_send()

    def ag_copy(buffer, c, q, step):
        send, recv = (g_up_send, g_up_recv) if step > 0 else (g_dn_send, g_dn_recv)
        if c is None:
            return line_copy(buffer.at[:, q], buffer.at[:, q], send, recv, C, q, step)
        return line_copy(buffer.at[c, q], buffer.at[c, q], send, recv, c, q, step)

    def ag_wait(buffer, c, q, step):
        send, recv = (g_up_send, g_up_recv) if step > 0 else (g_dn_send, g_dn_recv)
        place = buffer.at[:, q] if c is None else buffer.at[c, q]
        line_copy(place, place, send, recv, C if c is None else c, q, -step).wait_recv()

    def ag(buffer, c, t):
        if t == 1:

            @pl.when(z < T - 1)
            def _():
                ag_copy(buffer, c, z, 1).start()

            @pl.when(z > 0)
            def _():
                ag_copy(buffer, c, z, -1).start()

            return

        @pl.when(z >= t - 1)
        def _():
            q = z - (t - 1)
            ag_wait(buffer, c, q, 1)

            @pl.when(z < T - 1)
            def _():
                ag_copy(buffer, c, q, 1).start()

        @pl.when(z <= T - t)
        def _():
            q = z + (t - 1)
            ag_wait(buffer, c, q, -1)

            @pl.when(z > 0)
            def _():
                ag_copy(buffer, c, q, -1).start()

    def ag_drain(buffer, c):
        for q in range(T):

            @pl.when((z >= q) & (z < T - 1))
            def _(q=q):
                ag_copy(buffer, c, q, 1).wait_send()

            @pl.when((z <= q) & (z > 0))
            def _(q=q):
                ag_copy(buffer, c, q, -1).wait_send()

    a_q = lambda j: wide_f.at[j]
    b_o, a_u, b_d = wide_f.at[3], wide_f.at[4], wide_f.at[5]
    b_q = lambda j: heads_f.at[j]
    a_o = heads_f.at[3]
    b_u, a_d = units_f.at[0], units_f.at[1]
    line = lambda ref, k: ref[pl.ds(k, 1)].astype(F32)
    flat = lambda ref: ref[...].reshape(1, ref.shape[0]).astype(F32)
    sets = q_in.shape[1]
    pick = (lax.broadcasted_iota(jnp.int32, (sets, 128), 0) == chosen[...]).astype(F32)

    def stage_copies(s):
        slot = s % 2
        pairs = [
            (q_in.at[:, s], wide_stage.at[slot, pl.ds(0, 3)]),
            (o_out.at[s], wide_stage.at[slot, 3]),
            (u_in.at[s], wide_stage.at[slot, 4]),
            (d_out.at[s], wide_stage.at[slot, 5]),
            (q_out.at[:, s], heads_stage.at[slot, pl.ds(0, 3)]),
            (o_in.at[s], heads_stage.at[slot, 3]),
            (u_out.at[s], units_stage.at[slot, 0]),
            (d_in.at[s], units_stage.at[slot, 1]),
        ]
        return [
            pltpu.make_async_copy(src, dst, stage_sem.at[slot, k])
            for k, (src, dst) in enumerate(pairs)
        ]

    def choose(s):
        for copy in stage_copies(s):
            copy.wait()
        weight = pick[s : s + 1, :1].astype(BF16)
        for stage, held in ((wide_stage, wide_f), (heads_stage, heads_f), (units_stage, units_f)):
            for k in range(held.shape[0]):
                term = stage[s % 2, k] * weight
                held[k] = term if s == 0 else held[k] + term
        if s + 2 < sets:
            for copy in stage_copies(s + 2):
                copy.start()

    def chunk(buffer, c, n, cols=slice(None)):
        rows = buffer[c : c + n, :, :, cols]
        return rows.reshape(n * M, rows.shape[-1])

    def cols_of(g, size):
        return pl.ds(pl.multiple_of(g * size, size), size)

    def project():
        width = math.gcd(H, 512)
        for j in range(3):
            low_j = dot_nt(hidden[...].reshape(S, D), a_q(j)[...]).astype(BF16)
            low_q[j] = low_j

            @pl.loop(0, H // width)
            def _(n, j=j, low_j=low_j):
                cols = cols_of(n, width)
                rows = dot_nn(hidden[...].reshape(S, D), qkv_all[j, :, :, cols].reshape(D, width))
                rows += dot_nn(low_j, b_q(j)[:, cols])
                if j != 1:
                    rows += qkv_bias[pl.ds(j // 2, 1), cols].astype(F32)
                qkv[j, :, cols] = rows.astype(BF16)

    scale = 1.0 / math.sqrt(HEAD)

    def mark_segments():
        row = segments[...].astype(F32)
        pieces = [row[:, q * Q + c * R : q * Q + c * R + R] for c in range(C) for q in range(T)]
        row = jnp.concatenate(pieces, axis=1)
        seg_row[...] = row
        seg_col[...] = jnp.broadcast_to(row, (128, S)).T

    def turn_heads(j):
        @pl.loop(0, heads)
        def _(h):
            turned[cols_of(h, HEAD)] = qkv[j, :, cols_of(h, HEAD)].T

    def attend(c):
        rows = pl.ds(c * M, M)

        @pl.loop(0, heads)
        def _(h):
            cols = cols_of(h, HEAD)
            scores = dot_nt(qkv[1, :, cols], qkv[0, rows, cols]) * scale
            scores = jnp.where(seg_col[:, :1] == seg_row[:, rows], scores, -1e30)
            weights = jnp.exp(scores - jnp.max(scores, axis=0, keepdims=True))
            low = (weights * (1.0 / jnp.sum(weights, axis=0, keepdims=True))).astype(BF16)
            probs[h, :, rows] = low
            mixed[rows, cols] = dot_nn(turned[cols], low).T.astype(BF16)

    def attend_back(c):
        rows = pl.ds(c * M, M)

        @pl.loop(0, heads)
        def _(h):
            cols = cols_of(h, HEAD)
            weights = probs[h, :, rows].astype(F32)
            grad = dot_nt(qkv[2, :, cols], grad_mixed[rows, cols])
            centre = jnp.sum(grad * weights, axis=0, keepdims=True)
            low = (weights * (grad - centre)).astype(BF16)
            grad_scores[:, pl.ds(pl.multiple_of(h * S + c * M, M), M)] = low
            grad_qkv[0, rows, cols] = (dot_nn(turned[cols], low).T * scale).astype(BF16)

    def attend_sums():
        @pl.loop(0, heads)
        def _(h):
            cols = cols_of(h, HEAD)
            low = grad_scores[:, cols_of(h, S)]
            grad_qkv[1, :, cols] = (dot_nn(low, qkv[0, :, cols]) * scale).astype(BF16)
            grad_qkv[2, :, cols] = dot_nn(probs[h], grad_mixed[:, cols]).astype(BF16)

    grad_scores = slope

    def span(c, n):
        return pl.ds(c * M, n * M)

    def put_part(c, n, cols, rows):
        part[c : c + n, :, :, cols] = rows.astype(BF16).reshape(n, T, R, rows.shape[-1])

    group = math.gcd(F, 4)

    def by_blocks(body):
        @pl.loop(0, F // group)
        def _(turn):
            for k in range(group):
                g = turn * group + k
                body(g, cols_of(g, block))

    def mix_out(c, n):
        low = dot_nt(mixed[span(c, n)], a_o[...]).astype(BF16)
        low_o[span(c, n)] = low
        for g in range(F):
            cols = pl.ds(g * block, block)
            put_part(c, n, cols, dot_nn(mixed[span(c, n)], proj_all[g]) + dot_nn(low, b_o[:, cols]))

    def feed_up(c, n):
        low = dot_nt(chunk(normed, c, n), a_u[...]).astype(BF16)
        low_u[span(c, n)] = low

        @pl.loop(0, FL // NT)
        def _(turn):
            cols = cols_of(turn, NT)
            pre = dot_nn(chunk(normed, c, n), up_all[:, :, cols].reshape(D, NT))
            pre += dot_nn(low, b_u[:, cols]) + up_bias[cols].reshape(1, NT).astype(F32)
            square = pre * pre
            bend = jnp.tanh(ROOT * (pre + 0.044715 * square * pre))
            half = 0.5 * (1.0 + bend)
            act[span(c, n), cols] = (pre * half).astype(BF16)
            rise = half + 0.5 * pre * (1.0 - bend * bend) * (ROOT * (1.0 + 3 * 0.044715 * square))
            slope[span(c, n), cols] = rise.astype(BF16)

    def feed_down(c, n):
        low = dot_nt(act[span(c, n)], a_d[...]).astype(BF16)
        low_d[span(c, n)] = low

        @by_blocks
        def _(g, cols):
            put_part(c, n, cols, dot_nn(act[span(c, n)], down_all[g]) + dot_nn(low, b_d[:, cols]))

    def back_down(c, n):
        low = dot_nt(chunk(grad_feed, c, n), b_d[...]).astype(BF16)
        back_d[span(c, n)] = low

        @pl.loop(0, FL // NT)
        def _(turn):
            cols = cols_of(turn, NT)
            total = dot_nn(low, a_d[:, cols])
            for g in range(F):
                total += dot_nt(chunk(grad_feed, c, n, pl.ds(g * block, block)), down_all[g, cols])
            grad_pre[span(c, n), cols] = (total * slope[span(c, n), cols].astype(F32)).astype(BF16)

    def back_up(c, n):
        low = dot_nt(grad_pre[span(c, n)], b_u[...]).astype(BF16)
        back_u[span(c, n)] = low

        @by_blocks
        def _(g, cols):
            put_part(c, n, cols, dot_nt(grad_pre[span(c, n)], up_all[g]) + dot_nn(low, a_u[:, cols]))

    def back_mix(c, n):
        low = dot_nt(chunk(grad_branch, c, n), b_o[...]).astype(BF16)
        back_o[span(c, n)] = low
        total = dot_nn(low, a_o[...])
        for g in range(F):
            total += dot_nt(chunk(grad_branch, c, n, pl.ds(g * block, block)), proj_all[g])
        grad_mixed[span(c, n)] = total.astype(BF16)

    def back_project(c, n):
        lows = []
        for j in range(3):
            low = dot_nt(grad_qkv[j, span(c, n)], b_q(j)[...]).astype(BF16)
            back_q[j, span(c, n)] = low
            lows.append(low)

        @by_blocks
        def _(g, cols):
            total = dot_nn(lows[0], a_q(0)[:, cols])
            for j in range(3):
                if j:
                    total += dot_nn(lows[j], a_q(j)[:, cols])
                total += dot_nt(grad_qkv[j, span(c, n)], qkv_all[j, g])
            put_part(c, n, cols, total)

    def own(c):
        return pl.ds(c * R, R)

    def meet_one(c):
        total = rs_sum(c) + hidden[c, z].astype(F32) + flat(proj_bias)
        unit, rstd = norm_parts(total)
        unit_one[own(c)] = unit
        rstd_one[own(c)] = jnp.broadcast_to(rstd, (R, 128))
        normed[c, z] = (unit * line(gains, 0) + line(shifts, 0)).astype(BF16)

    def meet_two(c):
        total = rs_sum(c) + unit_one[own(c)] * line(gains, 0) + line(shifts, 0) + flat(down_bias)
        unit, rstd = norm_parts(total)
        layer_out[own(c)] = unit * line(gains, 1) + line(shifts, 1)
        grad = norm_pull(cotangent[own(c)].astype(F32) * line(gains, 1), unit, rstd)
        grad_own[own(c)] = grad
        grad_feed[c, z] = grad.astype(BF16)

    def meet_three(c):
        grad = (grad_own[own(c)] + rs_sum(c)) * line(gains, 0)
        grad = norm_pull(grad, unit_one[own(c)], rstd_one[own(c)][:, :1])
        grad_own[own(c)] = grad
        grad_branch[c, z] = grad.astype(BF16)

    def meet_four(c):
        grad_input[own(c)] = grad_own[own(c)] + rs_sum(c)

    def factor(low, right):
        return dot_nn(low.astype(F32).T.astype(BF16), right).astype(BF16)

    def by_columns(low, right, place, row):
        turned = low.astype(F32).T.astype(BF16)
        for q in range(T):
            cols = pl.ds(q * H, H)
            rows = right[:, :, :, cols].reshape(S, H)
            place[q, pl.ds(row, 16)] = dot_nn(turned, rows).astype(BF16)

    def factors_feed():
        units_g[pl.ds(0, 16)] = factor(low_u[...], grad_pre[...])
        units_g[pl.ds(16, 16)] = factor(back_d[...], act[...])
        by_columns(back_u[...], normed, feed_part, 0)
        by_columns(low_d[...], grad_feed, feed_part, 16)

    def factors_mix():
        heads_g[pl.ds(48, 16)] = factor(back_o[...], mixed[...])
        by_columns(low_o[...], grad_branch, mix_part, 48)

    def factors_project():
        for j in range(3):
            heads_g[pl.ds(16 * j, 16)] = factor(low_q[j], grad_qkv[j])
            by_columns(back_q[j], hidden, mix_part, 16 * j)
        marks = jnp.concatenate([pick[:, :1], jnp.zeros((32 - sets, 1), F32)])
        heads_g[pl.ds(64, 32)] = jnp.broadcast_to(marks, (32, H)).astype(BF16)

    from_low[:, 0] = jnp.zeros((C, R, D), BF16)
    from_high[:, T - 1] = jnp.zeros((C, R, D), BF16)
    qkv_g = gathers[0]
    def own_hidden(step):
        return line_copy(hidden_in, hidden.at[:, z], g_up_send if step > 0 else g_dn_send, g_up_recv if step > 0 else g_dn_recv, C, z, step)

    @pl.when(z < T - 1)
    def _():
        own_hidden(1).start()

    @pl.when(z > 0)
    def _():
        own_hidden(-1).start()

    qkv_g.stage(0)
    for copy in own_copies + stage_copies(0) + stage_copies(1):
        copy.start()
    schedule(cfg, dict(locals()))


def schedule(cfg, env):
    T, C, K = cfg["T"], cfg["C"], env["K"]
    rs, ag, hidden = env["rs"], env["ag"], env["hidden"]
    qkv_g, proj_g, up_g, down_g, rest_g = env["gathers"][:5]
    env["mark_segments"]()
    for s in range(2):
        env["choose"](s)
    for step in range(1, K + 1):
        qkv_g.stage(step)
        if step == 1:
            proj_g.stage(0)
            ag(hidden, None, 2)
            for s in range(2, 5):
                env["choose"](s)
    if K == 0:
        proj_g.stage(0)
    if K >= 1:
        proj_g.stage(1)
    up_g.stage(0)
    if K < 1:
        ag(hidden, None, 2)
        for s in range(2, 5):
            env["choose"](s)
    for s in range(5, env["sets"]):
        env["choose"](s)
    for t in range(3, T + 1):
        ag(hidden, None, t)
    for step in range(2, K + 1):
        proj_g.stage(step)
    down_g.stage(0)
    rest_g.stage(0)
    qkv_g.finish()
    for copy in env["own_copies"]:
        copy.wait()
    env["project"]()
    env["turn_heads"](2)
    if K:
        up_g.stage(1)
    proj_g.finish()
    buffers = [env["normed"], env["grad_feed"], env["grad_branch"]]
    meets = [env["meet_one"], env["meet_two"], env["meet_three"], env["meet_four"]]

    def start_sum(chunks):
        for c in chunks:
            rs(c, 1)

    def work(kind, k, first, n):
        group = range(first, first + n)
        if kind == "up":
            if first == 0:
                up_g.finish()
            env["feed_up"](first, n)
            return
        if kind == "mix":
            env["back_mix"](first, n)
            for c in group:
                env["attend_back"](c)
            return
        if k > 0:
            for c in group:
                env["rs_drain"](c)
        if k == 0:
            for c in group:
                env["attend"](c)
            if first + n == C:
                env["turn_heads"](1)
            env["mix_out"](first, n)
        if k == 1:
            if first == 0:
                for gather in (down_g, rest_g):
                    for step in range(2, K + 1):
                        gather.stage(step)
                down_g.finish()
                rest_g.finish()
            env["feed_down"](first, n)
        if k == 2:
            env["back_down"](first, n)
            env["back_up"](first, n)
        if k == 3:
            env["back_project"](first, n)
        start_sum(group)
        if k == 2 and first + n == C:
            env["factors_feed"]()
            env["deal"](0)

    def meet(k, c):
        meets[k](c)
        if k > 0:
            env["ag_drain"](buffers[k - 1], c)
        ag(buffers[k], c, 1)

    steps = []
    for k in range(3):
        steps += [("up", k, 0)] if k == 1 else []
        steps += [("work", k, 0)] + [("rs", k, t) for t in range(2, T)] + [("meet", k, 0)]
        steps += [("ag", k, t) for t in range(2, T + 1)]
    steps.append(("mix", 3, 0))
    groups, at, came, turn = cfg["groups"], [0] * C, {}, 0
    while min(at) < len(steps):
        if turn == 1 and K:
            down_g.stage(1)
            rest_g.stage(1)
        if turn == cfg["up_turn"]:
            for step in range(2, K + 1):
                up_g.stage(step)
        for c in range(C):
            if turn < cfg["lag"] * c or at[c] == len(steps):
                continue
            kind, k, t = steps[at[c]]
            if kind in ("up", "work", "mix"):
                n = groups[k]
                first = c // n * n
                came.setdefault((kind, k, first), set()).add(c)
                if len(came[kind, k, first]) < n:
                    continue
                work(kind, k, first, n)
                for member in range(first, first + n):
                    at[member] += 1
                continue
            if kind == "rs":
                rs(c, t)
            if kind == "meet":
                meet(k, c)
            if kind == "ag":
                ag(buffers[k], c, t)
            at[c] += 1
        turn += 1
    env["share"](0)
    env["attend_sums"]()
    n, grads = groups[4], env["gathers"][5:]
    for c in range(0, C, n):
        work("work", 3, c, n)
        if c == 0:
            env["pass_on"](0)
    env["factors_mix"]()
    env["factors_project"]()
    env["deal"](1)
    for t in range(2, T):
        for c in range(C):
            rs(c, t)
            if t == T - 1 and c == C // 2 - 1:
                env["pass_on"](1)
        if t == 2:
            env["share"](1)
            for step in range(1, K + 1):
                for gather in grads[:2]:
                    gather.stage(step)
    if C == 1 or T == 2:
        if T == 2:
            env["share"](1)
            for step in range(1, K + 1):
                for gather in grads[:2]:
                    gather.stage(step)
        env["pass_on"](1)
    for step in range(1, K + 1):
        for c in range(C * (step - 1) // K, C * step // K):
            meets[3](c)
        for gather in grads[2:]:
            gather.stage(step)
    if K == 0:
        for c in range(C):
            meets[3](c)
    for gather in grads:
        gather.finish()
    for c in range(C):
        env["rs_drain"](c)
        env["ag_drain"](buffers[2], c)
    env["ag_drain"](hidden, None)
    for which in range(2):
        env["pass_drain"](which)
    for gather in env["gathers"]:
        gather.drain()


def spread(mesh, body):
    placed = (
        P(("fsdp", "tp"), None),
        P(("fsdp", "tp"), None),
        P("fsdp", None),
        P("fsdp"),
        P(None, "fsdp", "tp"),
        P(None, "tp"),
        P("tp", "fsdp"),
        P(),
        P("fsdp", "tp"),
        P("tp"),
        P("tp", "fsdp"),
        P(),
        P(),
        P(),
        P(),
        P(None, None, None, "tp"),
        P(None, "tp", None),
        P(),
        P(),
        P(None, None, "tp"),
        P(None, "tp", None),
        P(),
    )
    return jax.shard_map(
        body,
        mesh=mesh,
        in_specs=placed,
        out_specs=(
            P(("fsdp", "tp"), None),
            P(("fsdp", "tp"), None),
            P(),
            P(None, None, None, "tp"),
            P(None, "tp", None),
            P(),
            P(),
            P(None, None, "tp"),
            P(None, "tp", None),
            P(),
        ),
        check_vma=False,
    )


def chunks_for(rows):
    return max(c for c in (1, 2, 4) if rows % (16 * c) == 0)


def place_kernel(layer_in, grad_in, feed_in, units_in, mix_in, heads_in, layer_out, grad_out, *refs):
    outs, tables = refs[:8], refs[8:16]
    feed_all, units_all, mix_all, heads_all, rows_a, rows_b, sems = refs[16:]
    F, T, _, H = feed_all.shape
    sets = outs[2].shape[0]
    loads = [(heads_in, heads_all), (feed_in, feed_all), (units_in, units_all), (mix_in, mix_all)]
    loads += [(layer_in, rows_a), (grad_in, rows_b)]
    loads = [pltpu.make_async_copy(a, b, sems.at[k]) for k, (a, b) in enumerate(loads)]
    stores = list(zip(tables, outs)) + [(rows_a, layer_out), (rows_b, grad_out)]
    stores = [pltpu.make_async_copy(a, b, sems.at[6 + k]) for k, (a, b) in enumerate(stores)]
    for copy in loads:
        copy.start()
    order = lax.broadcasted_iota(jnp.int32, (32, 1), 0).astype(F32)
    q_in, q_out, o_in, o_out, u_in, u_out, d_in, d_out = range(8)
    loads[0].wait()
    chosen = []
    for g in range(F):
        marks = heads_all[g, pl.ds(64, 32), pl.ds(0, 128)][:, :1].astype(F32)
        chosen.append(jnp.clip(jnp.sum(marks * order).astype(jnp.int32), 0, sets - 1))

    def fill(which, rows_of):
        ref = tables[which]
        ref[...] = jnp.zeros_like(ref)
        for g in range(F):
            rows_of(ref, g, chosen[g])
        stores[which].start()

    def whole(source, row):
        def add(ref, g, s):
            ref[s] += source[g, pl.ds(row, 16)].astype(F32)

        return add

    def columns(source, row):
        def add(ref, g, s):
            for t in range(T):
                ref[s, :, pl.ds(t * H, H)] += source[g, t, pl.ds(row, 16)].astype(F32)

        return add

    def trio(add_of):
        def add(ref, g, s):
            for j in range(3):
                add_of(16 * j)(ref.at[j], g, s)

        return add

    fill(q_out, trio(lambda row: whole(heads_all, row)))
    fill(o_in, whole(heads_all, 48))
    loads[1].wait()
    fill(u_in, columns(feed_all, 0))
    fill(d_out, columns(feed_all, 16))
    loads[2].wait()
    fill(u_out, whole(units_all, 0))
    fill(d_in, whole(units_all, 16))
    loads[3].wait()
    fill(o_out, columns(mix_all, 48))
    fill(q_in, trio(lambda row: columns(mix_all, row)))
    for copy in loads[4:]:
        copy.wait()
    for copy in stores[8:]:
        copy.start()
    for copy in stores:
        copy.wait()


def kernel_per_device(F, T):
    def per_device(
        hidden_in, cotangent, segment_ids, adapter_set, qkv_weight, qkv_bias, proj_weight, proj_bias,
        up_weight, up_bias, down_weight, down_bias, norm_gain, norm_bias, qkv_adapt_in, qkv_adapt_out,
        attn_adapt_in, attn_adapt_out, up_adapt_in, up_adapt_out, down_adapt_in, down_adapt_out,
    ):
        Q, D = hidden_in.shape
        H, FL = qkv_weight.shape[2], up_weight.shape[1]
        S, C, sets = Q * T, chunks_for(Q), qkv_adapt_in.shape[1]
        R, block = Q // C, D // F
        cfg = dict(F=F, T=T, S=S, D=D, H=H, FL=FL, C=C, lag=1, groups=(1, 1, 1, 1, 1), up_turn=T + 1)
        turn = lambda table: jnp.swapaxes(table, -1, -2)
        vmem, anywhere = pl.BlockSpec(memory_space=pltpu.VMEM), pl.BlockSpec(memory_space=pl.ANY)
        dma = pltpu.SemaphoreType.DMA
        bank = lambda *shape: pltpu.VMEM(shape, BF16)
        wide_bank = lambda *shape: pltpu.VMEM(shape, F32)
        scratch = (
            [bank(C, T, R, D), bank(3, F, block, H), bank(F, H, block), bank(F, block, FL), bank(F, FL, block)]
            + [bank(3, S, H), bank(H // HEAD, S, S), bank(S, H), bank(C, T, R, D), bank(S, FL), bank(S, FL)]
            + [bank(C, T, R, D), bank(C, T, R, D), bank(S, H), bank(3, S, H)]
            + [bank(C, T, R, D), bank(C, T, R, D), bank(C, T, R, D)]
            + [wide_bank(Q, D), wide_bank(Q, 128), wide_bank(Q, D)]
            + [bank(3, S, RANK), bank(S, RANK), bank(S, RANK), bank(S, RANK)] * 2
            + [wide_bank(1, S), wide_bank(S, 128), bank(H, S)]
            + [bank(6, RANK, D), bank(4, RANK, H), bank(2, RANK, FL)]
            + [bank(2, 6, RANK, D), bank(2, 4, RANK, H), bank(2, 2, RANK, FL)]
            + [bank(T, 32, H), bank(T - 1, 32, H), bank(T, 32, H)]
            + [bank(T, 64, H), bank(T - 1, 64, H), bank(T, 64, H)]
            + [bank(32, FL), bank(96, H)]
            + [dma((2, 8))] + [dma((2, T - 1))] * 4
            + [dma((9, 2, F)), dma((9, 2, F))]
            + [dma((C, T))] * 4
            + [dma((C + 1, T))] * 4
            + [dma((9,))]
        )
        flops = 2 * S * (4 * D * H + 2 * D * FL) * 2
        outs = pl.pallas_call(
            functools.partial(layer_kernel, cfg),
            out_shape=[
                jax.ShapeDtypeStruct((Q, D), F32),
                jax.ShapeDtypeStruct((Q, D), F32),
                jax.ShapeDtypeStruct((F, T, 32, H), BF16),
                jax.ShapeDtypeStruct((F, 32, FL), BF16),
                jax.ShapeDtypeStruct((F, T, 64, H), BF16),
                jax.ShapeDtypeStruct((F, 96, H), BF16),
            ],
            in_specs=[anywhere] + [vmem] * 3 + [anywhere] * 4 + [vmem] * 6 + [anywhere] * 8,
            out_specs=[vmem] * 2 + [anywhere] * 4,
            scratch_shapes=scratch,
            compiler_params=pltpu.CompilerParams(
                collective_id=0, has_side_effects=True, vmem_limit_bytes=62 * 1024 * 1024
            ),
            cost_estimate=pl.CostEstimate(flops=flops, bytes_accessed=30000000, transcendentals=0),
        )(
            hidden_in.reshape(C, R, D), cotangent, segment_ids, adapter_set[None, :],
            qkv_weight, proj_weight, up_weight, down_weight,
            proj_bias, down_bias, up_bias, qkv_bias, norm_gain, norm_bias,
            turn(qkv_adapt_in), qkv_adapt_out, turn(attn_adapt_in), attn_adapt_out,
            turn(up_adapt_in), up_adapt_out, turn(down_adapt_in), down_adapt_out,
        )
        shapes = [
            (3, sets, RANK, D), (3, sets, RANK, H), (sets, RANK, H), (sets, RANK, D),
            (sets, RANK, D), (sets, RANK, FL), (sets, RANK, FL), (sets, RANK, D),
        ]
        table = lambda *shape: jax.ShapeDtypeStruct(shape, F32)
        layer_out, grad_input, q_in, q_out, o_in, o_out, u_in, u_out, d_in, d_out = pl.pallas_call(
            place_kernel,
            out_shape=[table(Q, D), table(Q, D)] + [table(*shape) for shape in shapes],
            in_specs=[anywhere] * 6,
            out_specs=[anywhere] * 10,
            scratch_shapes=[wide_bank(*shape) for shape in shapes]
            + [bank(*out.shape) for out in outs[2:]]
            + [wide_bank(Q, D), wide_bank(Q, D), dma((16,))],
            compiler_params=pltpu.CompilerParams(vmem_limit_bytes=62 * 1024 * 1024),
        )(*outs)
        return (
            layer_out, grad_input, turn(q_in), q_out, turn(o_in), o_out, turn(u_in), u_out, turn(d_in), d_out,
        )

    return per_device


def solution(mesh):
    F, T = mesh.shape["fsdp"], mesh.shape["tp"]

    def whole(*args):
        width = args[0].shape[1]
        fits = F & (F - 1) == 0 and (width // F) % 128 == 0 and T > 1 and F > 1 and args[14].shape[1] <= 32 and width // T * args[2].shape[1] <= args[8].shape[1] // T * HEAD
        return spread(mesh, kernel_per_device(F, T) if fits else per_device)(*args)

    return whole
```

```python
import functools
import math

import jax
import jax.numpy as jnp
from jax import lax
from jax.experimental import pallas as pl
from jax.experimental.pallas import tpu as pltpu
from jax.sharding import PartitionSpec as P

HEAD = 128
RANK = 16
MESH = pl.DeviceIdType.MESH
F32 = jnp.float32
BF16 = jnp.bfloat16
ROOT = math.sqrt(2.0 / math.pi)


def layer_norm(field_in, gain_row, shift_row):
    centre = jnp.mean(field_in, axis=-1, keepdims=True)
    centred = field_in - centre
    spread = jnp.mean(centred * centred, axis=-1, keepdims=True)
    return centred * lax.rsqrt(spread + 1e-05) * gain_row + shift_row


def precise_dot(left, right):
    return jnp.dot(left, right, precision=lax.Precision.HIGHEST)


def mixed_dot(left, right):
    return jnp.dot(left, right, preferred_element_type=jnp.float32)


def choose_set(table, index, axis):
    return lax.dynamic_index_in_dim(table, index, axis, keepdims=False)


def place_set(grad, index, sets, axis):
    onehot = (jnp.arange(sets) == index).astype(jnp.float32)
    shape_list = [1] * (grad.ndim + 1)
    shape_list[axis] = sets
    return jnp.expand_dims(grad, axis) * onehot.reshape(shape_list)


def per_device(
    hidden_in,
    cotangent,
    segment_ids,
    adapter_set,
    qkv_weight,
    qkv_bias,
    proj_weight,
    proj_bias,
    up_weight,
    up_bias,
    down_weight,
    down_bias,
    norm_gain,
    norm_bias,
    qkv_adapt_in,
    qkv_adapt_out,
    attn_adapt_in,
    attn_adapt_out,
    up_adapt_in,
    up_adapt_out,
    down_adapt_in,
    down_adapt_out,
):
    width_local = qkv_weight.shape[2]
    heads_local = width_local // HEAD
    sets = qkv_adapt_in.shape[1]
    chosen = adapter_set[0]
    segments = segment_ids[0]
    seq_rows = segments.shape[0]
    block_rows = min(512, seq_rows)
    blocks = seq_rows // block_rows
    score_scale = 1.0 / math.sqrt(HEAD)
    gains = norm_gain.astype(jnp.float32)
    shifts = norm_bias.astype(jnp.float32)
    first_q = choose_set(qkv_adapt_in, chosen, 1)
    second_q = choose_set(qkv_adapt_out, chosen, 1)
    first_o = choose_set(attn_adapt_in, chosen, 0)
    second_o = choose_set(attn_adapt_out, chosen, 0)
    first_u = choose_set(up_adapt_in, chosen, 0)
    second_u = choose_set(up_adapt_out, chosen, 0)
    first_d = choose_set(down_adapt_in, chosen, 0)
    second_d = choose_set(down_adapt_out, chosen, 0)
    seq_hidden = lax.all_gather(hidden_in, "tp", axis=0, tiled=True)
    qkv_full, proj_full = (
        lax.all_gather(qkv_weight, "fsdp", axis=1, tiled=True),
        lax.all_gather(proj_weight, "fsdp", axis=1, tiled=True),
    )
    main_term = jnp.einsum("sd,jdc->jsc", seq_hidden, qkv_full, preferred_element_type=jnp.float32)
    low_in = jnp.einsum("sd,jdr->jsr", seq_hidden, first_q, preferred_element_type=jnp.float32)
    low_term = jnp.einsum(
        "jsr,jrc->jsc", low_in, second_q.astype(jnp.float32), precision=lax.Precision.HIGHEST
    )
    bias_rows = jnp.stack([qkv_bias[0], jnp.zeros_like(qkv_bias[0]), qkv_bias[1]]).astype(
        jnp.float32
    )[:, None, :]
    qkv_round = (main_term + low_term + bias_rows).astype(jnp.bfloat16)
    queries = qkv_round[0].reshape(seq_rows, heads_local, HEAD)
    keys = qkv_round[1].reshape(seq_rows, heads_local, HEAD)
    values = qkv_round[2].reshape(seq_rows, heads_local, HEAD)
    query_blocks = queries.reshape(blocks, block_rows, heads_local, HEAD)
    seg_blocks = segments.reshape(blocks, block_rows)

    def scores_of(query_rows, seg_rows):
        raw_scores = (
            jnp.einsum("bhe,she->hbs", query_rows, keys, preferred_element_type=jnp.float32)
            * score_scale
        )
        same_doc = (seg_rows[:, None] == segments[None, :])[None]
        return jnp.where(same_doc, raw_scores, -1e30)

    def forward_block(inputs):
        query_rows, seg_rows = inputs
        scores = scores_of(query_rows, seg_rows)
        row_top = jnp.max(scores, axis=-1, keepdims=True)
        weights = jnp.exp(scores - row_top)
        row_total = jnp.sum(weights, axis=-1, keepdims=True)
        attn_probs = (weights / row_total).astype(jnp.bfloat16)
        attn_mixed = jnp.einsum(
            "hbs,she->bhe", attn_probs, values, preferred_element_type=jnp.float32
        )
        return (attn_mixed, (row_top + jnp.log(row_total))[..., 0])

    attn_mixed, logsum = lax.map(forward_block, (query_blocks, seg_blocks))
    attended = attn_mixed.reshape(seq_rows, width_local).astype(jnp.bfloat16)
    low_attn = mixed_dot(attended, first_o)
    second_o_wide = second_o.astype(jnp.float32)
    row_part = attended
    low_part = low_attn
    attn_sum = lax.psum_scatter(
        mixed_dot(row_part, proj_full) + precise_dot(low_part, second_o_wide),
        "tp",
        scatter_dimension=0,
        tiled=True,
    )
    first_sum = hidden_in.astype(jnp.float32) + attn_sum + proj_bias.astype(jnp.float32)
    normed = layer_norm(first_sum, gains[0], shifts[0])
    normed_round = normed.astype(jnp.bfloat16)
    seq_normed = lax.all_gather(normed_round, "tp", axis=0, tiled=True)
    up_full, down_full = (
        lax.all_gather(up_weight, "fsdp", axis=0, tiled=True),
        lax.all_gather(down_weight, "fsdp", axis=1, tiled=True),
    )
    low_up = mixed_dot(seq_normed, first_u)
    pre_act = (
        mixed_dot(seq_normed, up_full)
        + precise_dot(low_up, second_u.astype(jnp.float32))
        + up_bias.astype(jnp.float32)
    )
    act_round = jax.nn.gelu(pre_act, approximate=True).astype(jnp.bfloat16)
    low_down = mixed_dot(act_round, first_d)
    second_d_wide = second_d.astype(jnp.float32)
    row_part = act_round
    low_part = low_down
    ffn_sum = lax.psum_scatter(
        mixed_dot(row_part, down_full) + precise_dot(low_part, second_d_wide),
        "tp",
        scatter_dimension=0,
        tiled=True,
    )
    second_sum = normed + ffn_sum + down_bias.astype(jnp.float32)
    layer_out = layer_norm(second_sum, gains[1], shifts[1])
    unused, norm_back = jax.vjp(
        lambda field_in: layer_norm(field_in, gains[1], shifts[1]), second_sum
    )
    grad_second = norm_back(cotangent.astype(jnp.float32))[0]
    grad_feed_round = grad_second.astype(jnp.bfloat16)
    seq_grad_feed = lax.all_gather(grad_feed_round, "tp", axis=0, tiled=True)
    up_back, down_back = (
        lax.all_gather(up_weight, "fsdp", axis=0, tiled=True),
        lax.all_gather(down_weight, "fsdp", axis=1, tiled=True),
    )
    grad_low_down = mixed_dot(seq_grad_feed, second_d.T)
    grad_act = jnp.einsum(
        "sd,fd->sf", seq_grad_feed, down_back, preferred_element_type=jnp.float32
    ) + precise_dot(grad_low_down, first_d.astype(jnp.float32).T)
    unused, gelu_back = jax.vjp(lambda field_in: jax.nn.gelu(field_in, approximate=True), pre_act)
    grad_pre_round = gelu_back(grad_act)[0].astype(jnp.bfloat16)
    grad_down_out_part = precise_dot(low_down.T, seq_grad_feed.astype(jnp.float32))
    grad_down_in_part = precise_dot(act_round.astype(jnp.float32).T, grad_low_down)
    grad_low_up = mixed_dot(grad_pre_round, second_u.T)
    grad_up_out_part = precise_dot(low_up.T, grad_pre_round.astype(jnp.float32))
    grad_up_in_part = precise_dot(seq_normed.astype(jnp.float32).T, grad_low_up)
    first_u_wide = first_u.astype(jnp.float32)
    row_part = grad_pre_round
    low_part = grad_low_up
    grad_normed = grad_second + lax.psum_scatter(
        jnp.einsum("sf,df->sd", row_part, up_back, preferred_element_type=jnp.float32)
        + precise_dot(low_part, first_u_wide.T),
        "tp",
        scatter_dimension=0,
        tiled=True,
    )
    unused, norm_front = jax.vjp(
        lambda field_in: layer_norm(field_in, gains[0], shifts[0]), first_sum
    )
    grad_first = norm_front(grad_normed)[0]
    grad_branch_round = grad_first.astype(jnp.bfloat16)
    seq_grad_branch = lax.all_gather(grad_branch_round, "tp", axis=0, tiled=True)
    qkv_back, proj_back = (
        lax.all_gather(qkv_weight, "fsdp", axis=1, tiled=True),
        lax.all_gather(proj_weight, "fsdp", axis=1, tiled=True),
    )
    grad_low_attn = mixed_dot(seq_grad_branch, second_o.T)
    grad_attended = jnp.einsum(
        "sd,cd->sc", seq_grad_branch, proj_back, preferred_element_type=jnp.float32
    ) + precise_dot(grad_low_attn, first_o.astype(jnp.float32).T)
    grad_attended_round = grad_attended.astype(jnp.bfloat16)
    grad_attn_out_part = precise_dot(low_attn.T, seq_grad_branch.astype(jnp.float32))
    grad_attn_in_part = precise_dot(attended.astype(jnp.float32).T, grad_low_attn)
    grad_blocks = grad_attended_round.reshape(blocks, block_rows, heads_local, HEAD)

    def backward_block(carry, inputs):
        grad_keys, grad_values = carry
        query_rows, seg_rows, lse_rows, grad_rows = inputs
        scores = scores_of(query_rows, seg_rows)
        attn_probs = jnp.exp(scores - lse_rows[..., None])
        grad_probs = jnp.einsum(
            "bhe,she->hbs", grad_rows, values, preferred_element_type=jnp.float32
        )
        centre = jnp.sum(grad_probs * attn_probs, axis=-1, keepdims=True)
        grad_scores = (attn_probs * (grad_probs - centre)).astype(jnp.bfloat16)
        grad_query = (
            jnp.einsum("hbs,she->bhe", grad_scores, keys, preferred_element_type=jnp.float32)
            * score_scale
        )
        grad_keys = (
            grad_keys
            + jnp.einsum(
                "hbs,bhe->she", grad_scores, query_rows, preferred_element_type=jnp.float32
            )
            * score_scale
        )
        grad_values = grad_values + jnp.einsum(
            "hbs,bhe->she",
            attn_probs.astype(jnp.bfloat16),
            grad_rows,
            preferred_element_type=jnp.float32,
        )
        return ((grad_keys, grad_values), grad_query)

    zero_state = jnp.zeros((seq_rows, heads_local, HEAD), jnp.float32)
    key_value_grads, grad_queries = lax.scan(
        backward_block, (zero_state, zero_state), (query_blocks, seg_blocks, logsum, grad_blocks)
    )
    grad_qkv_round = jnp.stack(
        [
            grad_queries.reshape(seq_rows, width_local),
            key_value_grads[0].reshape(seq_rows, width_local),
            key_value_grads[1].reshape(seq_rows, width_local),
        ]
    ).astype(jnp.bfloat16)
    grad_qkv_out_part = jnp.einsum(
        "jsr,jsc->jrc", low_in, grad_qkv_round.astype(jnp.float32), precision=lax.Precision.HIGHEST
    )
    grad_low_qkv = jnp.einsum(
        "jsc,jrc->jsr", grad_qkv_round, second_q, preferred_element_type=jnp.float32
    )
    grad_qkv_in_part = jnp.einsum(
        "sd,jsr->jdr", seq_hidden.astype(jnp.float32), grad_low_qkv, precision=lax.Precision.HIGHEST
    )
    first_q_wide = first_q.astype(jnp.float32)
    row_part = grad_qkv_round
    low_part = grad_low_qkv
    grad_input = grad_first + lax.psum_scatter(
        (
            jnp.einsum("jsc,jdc->sd", row_part, qkv_back, preferred_element_type=jnp.float32)
            + jnp.einsum("jsr,jdr->sd", low_part, first_q_wide, precision=lax.Precision.HIGHEST)
        ).astype(jnp.bfloat16),
        "tp",
        scatter_dimension=0,
        tiled=True,
    ).astype(jnp.float32)
    wide_grads = lax.psum(
        (
            place_set(grad_qkv_in_part, chosen, sets, 1),
            place_set(grad_attn_out_part, chosen, sets, 0),
            place_set(grad_up_in_part, chosen, sets, 0),
            place_set(grad_down_out_part, chosen, sets, 0),
        ),
        ("fsdp", "tp"),
    )
    split_grads = (
        lax.psum(place_set(grad_qkv_out_part, chosen, sets, 1).astype(jnp.bfloat16), "fsdp").astype(
            jnp.float32
        ),
        lax.psum(place_set(grad_attn_in_part, chosen, sets, 0).astype(jnp.bfloat16), "fsdp").astype(
            jnp.float32
        ),
        lax.psum(place_set(grad_up_out_part, chosen, sets, 0).astype(jnp.bfloat16), "fsdp").astype(
            jnp.float32
        ),
        lax.psum(place_set(grad_down_in_part, chosen, sets, 0).astype(jnp.bfloat16), "fsdp").astype(
            jnp.float32
        ),
    )
    return (
        layer_out,
        grad_input,
        wide_grads[0],
        split_grads[0],
        split_grads[1],
        wide_grads[1],
        wide_grads[2],
        split_grads[2],
        split_grads[3],
        wide_grads[3],
    )


def dot_nn(left, right):
    return jnp.dot(left, right, preferred_element_type=F32)


def dot_nt(left, right):
    return lax.dot_general(left, right, (((1,), (1,)), ((), ())), preferred_element_type=F32)


def flip(index, mask):
    out, bit = index, 1
    while bit <= mask:
        if mask & bit:
            out = out + bit - 2 * bit * lax.rem(lax.div(index, bit), 2)
        bit *= 2
    return out


def norm_parts(rows):
    centred = rows - jnp.mean(rows, axis=-1, keepdims=True)
    spread = jnp.mean(centred * centred, axis=-1, keepdims=True)
    rstd = lax.rsqrt(spread + 1e-05)
    return centred * rstd, rstd


def norm_pull(grad, unit, rstd):
    return rstd * (
        grad
        - jnp.mean(grad, axis=-1, keepdims=True)
        - unit * jnp.mean(grad * unit, axis=-1, keepdims=True)
    )


class Gather:
    def __init__(self, which, shard, whole, send, recv, fsdp, tp, count):
        self.which, self.shard, self.whole = which, shard, whole
        self.send, self.recv, self.fsdp, self.tp = send, recv, fsdp, tp
        bits = [1 << i for i in range(1, count.bit_length() - 1)]
        self.orders = [bits, bits[::-1]]
        self.steps = len(bits)
        self.held = [[0], [0]]
        self.sent = []
        self.count = count

    def copy(self, half, mask, bit):
        landed = mask ^ bit
        place = self.whole(flip(self.fsdp, mask), half)
        return pltpu.make_async_remote_copy(
            src_ref=self.shard(half) if mask == 0 else place,
            dst_ref=place,
            send_sem=self.send.at[self.which, half, landed],
            recv_sem=self.recv.at[self.which, half, landed],
            device_id=(flip(self.fsdp, bit), self.tp),
            device_id_type=MESH,
        )

    def launch(self, half, mask, bit):
        self.copy(half, mask, bit).start()
        self.sent.append((half, mask, bit))

    def await_block(self, half, mask, bit):
        place = self.whole(flip(self.fsdp, mask), half)
        pltpu.make_async_remote_copy(
            src_ref=place,
            dst_ref=place,
            send_sem=self.send.at[self.which, half, mask],
            recv_sem=self.recv.at[self.which, half, mask],
            device_id=(flip(self.fsdp, bit), self.tp),
            device_id_type=MESH,
        ).wait_recv()

    def stage(self, step):
        for half in range(2):
            fresh = [0]
            if step > 0:
                bit = self.orders[half][step - 1]
                fresh = [mask ^ bit for mask in self.held[half]]
                for mask in fresh:
                    self.await_block(half, mask, bit)
                self.held[half] = self.held[half] + fresh
            if step < self.steps:
                for mask in self.held[half]:
                    self.launch(half, mask, self.orders[half][step])
            for mask in fresh:
                self.launch(half, mask, 1)

    def finish(self):
        for half in range(2):
            for mask in self.held[half]:
                self.await_block(half, mask ^ 1, 1)

    def drain(self):
        for half, mask, bit in self.sent:
            self.copy(half, mask, bit).wait_send()


def layer_kernel(cfg, *refs):
    F, T, S, D, H, FL, C = (cfg[k] for k in ("F", "T", "S", "D", "H", "FL", "C"))
    Q, heads, block = S // T, H // HEAD, D // F
    R = Q // C
    M = T * R
    NT = math.gcd(FL, 1024)
    (
        hidden_in, cotangent, segments, chosen, qkv_w, proj_w, up_w, down_w,
        proj_bias, down_bias, up_bias, qkv_bias, gains, shifts,
        q_in, q_out, o_in, o_out, u_in, u_out, d_in, d_out,
        layer_out, grad_input, feed_all, units_all, mix_all, heads_all,
        hidden, qkv_all, proj_all, up_all, down_all,
        qkv, probs, mixed, normed, act, slope, grad_feed, grad_branch, grad_mixed, grad_qkv,
        part, from_low, from_high, unit_one, rstd_one, grad_own,
        low_q, low_o, low_u, low_d, back_q, back_o, back_u, back_d,
        seg_row, seg_col, turned,
        wide_f, heads_f, units_f, wide_stage, heads_stage, units_stage,
        feed_part, feed_land, feed_full, mix_part, mix_land, mix_full, units_g, heads_g,
        stage_sem, deal_send, deal_recv,
        w_send, w_recv, up_send, up_recv, dn_send, dn_recv, g_up_send, g_up_recv, g_dn_send, g_dn_recv,
        own_sem,
    ) = refs
    grad_pre = slope
    f, z = lax.axis_index("fsdp"), lax.axis_index("tp")
    bits = [1 << i for i in range(F.bit_length() - 1)]

    barrier = pltpu.get_barrier_semaphore()
    for bit in bits:
        pl.semaphore_signal(barrier, inc=1, device_id=(flip(f, bit), z), device_id_type=MESH)

    turns = [lax.rem(z + k, T) for k in range(T)]
    for k in range(1, T):
        pl.semaphore_signal(barrier, inc=1, device_id=(f, turns[k]), device_id_type=MESH)
    pl.semaphore_wait(barrier, len(bits) + T - 1)

    rows_of = lambda total, half: pl.ds(half * (total // 2), total // 2)
    gathers = [
        Gather(0, lambda h: qkv_w.at[:, rows_of(block, h)], lambda g, h: qkv_all.at[:, g, rows_of(block, h)], w_send, w_recv, f, z, F),
        Gather(1, lambda h: proj_w.at[rows_of(H, h)], lambda g, h: proj_all.at[g, rows_of(H, h)], w_send, w_recv, f, z, F),
        Gather(2, lambda h: up_w.at[rows_of(block, h)], lambda g, h: up_all.at[g, rows_of(block, h)], w_send, w_recv, f, z, F),
    ]
    quarter = lambda part, h: pl.ds((2 * part + h) * (FL // 4), FL // 4)
    for part_of in range(2):
        shard = lambda h, p=part_of: down_w.at[quarter(p, h)]
        whole = lambda g, h, p=part_of: down_all.at[g, quarter(p, h)]
        gathers.append(Gather(3 + part_of, shard, whole, w_send, w_recv, f, z, F))
    pair = lambda ref, n: lambda h: ref.at[..., rows_of(n, h), :]
    pair_all = lambda ref, n: lambda g, h: ref.at[g, ..., rows_of(n, h), :]
    for k, (shard, whole) in enumerate(
        [(feed_full, feed_all), (units_g, units_all), (mix_full, mix_all), (heads_g, heads_all)]
    ):
        n = shard.shape[-2]
        gathers.append(Gather(5 + k, pair(shard, n), pair_all(whole, n), w_send, w_recv, f, z, F))
    K = gathers[0].steps
    own_copies = [
        pltpu.make_async_copy(hidden_in, hidden.at[:, z], own_sem.at[0]),
        pltpu.make_async_copy(qkv_w, qkv_all.at[:, f], own_sem.at[1]),
        pltpu.make_async_copy(proj_w, proj_all.at[f], own_sem.at[2]),
        pltpu.make_async_copy(up_w, up_all.at[f], own_sem.at[3]),
        pltpu.make_async_copy(down_w, down_all.at[f], own_sem.at[4]),
    ]
    own_grads = [
        pltpu.make_async_copy(feed_full, feed_all.at[f], own_sem.at[5]),
        pltpu.make_async_copy(units_g, units_all.at[f], own_sem.at[6]),
        pltpu.make_async_copy(mix_full, mix_all.at[f], own_sem.at[7]),
        pltpu.make_async_copy(heads_g, heads_all.at[f], own_sem.at[8]),
    ]

    def deal_copy(which, k):
        part_ref, land_ref = exchanges[which]
        return pltpu.make_async_remote_copy(
            src_ref=part_ref, dst_ref=land_ref.at[k - 1],
            send_sem=deal_send.at[which, k - 1], recv_sem=deal_recv.at[which, k - 1],
            device_id=(f, turns[k]), device_id_type=MESH,
        )

    exchanges = [(feed_part, feed_land), (mix_part, mix_land)]

    def deal(which):
        for k in range(1, T):
            deal_copy(which, k).start()

    def collect(which):
        part_ref, land_ref = exchanges[which]
        total = part_ref[...].astype(F32)
        for k in range(1, T):
            deal_copy(which, k).wait_recv()
            total += land_ref[k - 1].astype(F32)
        return total.astype(BF16)

    def pass_on(which):
        for k in (2 * which, 2 * which + 1):
            own_grads[k].start()
            gathers[5 + k].stage(0)

    def pass_drain(which):
        for k in range(1, T):
            deal_copy(which, k).wait_send()
        for k in (2 * which, 2 * which + 1):
            own_grads[k].wait()

    def line_copy(src, dst, send, recv, c, q, step):
        return pltpu.make_async_remote_copy(
            src_ref=src, dst_ref=dst, send_sem=send.at[c, q], recv_sem=recv.at[c, q],
            device_id=(f, z + step), device_id_type=MESH,
        )

    def rs_copy(c, q, step):
        landing, send, recv = (from_low, up_send, up_recv) if step > 0 else (from_high, dn_send, dn_recv)
        return line_copy(part.at[c, q], landing.at[c, q], send, recv, c, q, step)

    def rs_wait(c, q, step):
        landing, send, recv = (from_low, up_send, up_recv) if step > 0 else (from_high, dn_send, dn_recv)
        line_copy(landing.at[c, q], landing.at[c, q], send, recv, c, q, -step).wait_recv()

    def rs(c, t):
        def add(q, landing):
            part[c, q] = (part[c, q].astype(F32) + landing[c, q].astype(F32)).astype(BF16)

        @pl.when(z <= t - 1)
        def _():
            q = T - t + z

            @pl.when(z > 0)
            def _():
                rs_wait(c, q, 1)
                add(q, from_low)

            rs_copy(c, q, 1).start()

        @pl.when(z >= T - t)
        def _():
            q = z - (T - t)

            @pl.when(z < T - 1)
            def _():
                rs_wait(c, q, -1)
                add(q, from_high)

            rs_copy(c, q, -1).start()

    def rs_sum(c):
        @pl.when(z > 0)
        def _():
            rs_wait(c, z, 1)

        @pl.when(z < T - 1)
        def _():
            rs_wait(c, z, -1)

        return (part[c, z].astype(F32) + from_low[c, z].astype(F32)) + from_high[c, z].astype(F32)

    def rs_drain(c):
        for q in range(T):
            if q > 0:

                @pl.when(z < q)
                def _(q=q):
                    rs_copy(c, q, 1).wait_send()

            if q < T - 1:

                @pl.when(z > q)
                def _(q=q):
                    rs_copy(c, q, -1).wait_send()

    def ag_copy(buffer, c, q, step):
        send, recv = (g_up_send, g_up_recv) if step > 0 else (g_dn_send, g_dn_recv)
        if c is None:
            return line_copy(buffer.at[:, q], buffer.at[:, q], send, recv, C, q, step)
        return line_copy(buffer.at[c, q], buffer.at[c, q], send, recv, c, q, step)

    def ag_wait(buffer, c, q, step):
        send, recv = (g_up_send, g_up_recv) if step > 0 else (g_dn_send, g_dn_recv)
        place = buffer.at[:, q] if c is None else buffer.at[c, q]
        line_copy(place, place, send, recv, C if c is None else c, q, -step).wait_recv()

    def ag(buffer, c, t):
        if t == 1:

            @pl.when(z < T - 1)
            def _():
                ag_copy(buffer, c, z, 1).start()

            @pl.when(z > 0)
            def _():
                ag_copy(buffer, c, z, -1).start()

            return

        @pl.when(z >= t - 1)
        def _():
            q = z - (t - 1)
            ag_wait(buffer, c, q, 1)

            @pl.when(z < T - 1)
            def _():
                ag_copy(buffer, c, q, 1).start()

        @pl.when(z <= T - t)
        def _():
            q = z + (t - 1)
            ag_wait(buffer, c, q, -1)

            @pl.when(z > 0)
            def _():
                ag_copy(buffer, c, q, -1).start()

    def ag_drain(buffer, c):
        for q in range(T):

            @pl.when((z >= q) & (z < T - 1))
            def _(q=q):
                ag_copy(buffer, c, q, 1).wait_send()

            @pl.when((z <= q) & (z > 0))
            def _(q=q):
                ag_copy(buffer, c, q, -1).wait_send()

    a_q = lambda j: wide_f.at[j]
    b_o, a_u, b_d = wide_f.at[3], wide_f.at[4], wide_f.at[5]
    b_q = lambda j: heads_f.at[j]
    a_o = heads_f.at[3]
    b_u, a_d = units_f.at[0], units_f.at[1]
    line = lambda ref, k: ref[pl.ds(k, 1)].astype(F32)
    flat = lambda ref: ref[...].reshape(1, ref.shape[0]).astype(F32)
    sets = q_in.shape[1]
    pick = (lax.broadcasted_iota(jnp.int32, (sets, 128), 0) == chosen[...]).astype(F32)

    def stage_copies(s):
        slot = s % 2
        pairs = [
            (q_in.at[:, s], wide_stage.at[slot, pl.ds(0, 3)]),
            (o_out.at[s], wide_stage.at[slot, 3]),
            (u_in.at[s], wide_stage.at[slot, 4]),
            (d_out.at[s], wide_stage.at[slot, 5]),
            (q_out.at[:, s], heads_stage.at[slot, pl.ds(0, 3)]),
            (o_in.at[s], heads_stage.at[slot, 3]),
            (u_out.at[s], units_stage.at[slot, 0]),
            (d_in.at[s], units_stage.at[slot, 1]),
        ]
        return [
            pltpu.make_async_copy(src, dst, stage_sem.at[slot, k])
            for k, (src, dst) in enumerate(pairs)
        ]

    def choose(s):
        for copy in stage_copies(s):
            copy.wait()
        weight = pick[s : s + 1, :1].astype(BF16)
        for stage, held in ((wide_stage, wide_f), (heads_stage, heads_f), (units_stage, units_f)):
            for k in range(held.shape[0]):
                term = stage[s % 2, k] * weight
                held[k] = term if s == 0 else held[k] + term
        if s + 2 < sets:
            for copy in stage_copies(s + 2):
                copy.start()

    def chunk(buffer, c, n, cols=slice(None)):
        rows = buffer[c : c + n, :, :, cols]
        return rows.reshape(n * M, rows.shape[-1])

    def cols_of(g, size):
        return pl.ds(pl.multiple_of(g * size, size), size)

    def project():
        width = math.gcd(H, 512)
        for j in range(3):
            low_j = dot_nt(hidden[...].reshape(S, D), a_q(j)[...]).astype(BF16)
            low_q[j] = low_j

            @pl.loop(0, H // width)
            def _(n, j=j, low_j=low_j):
                cols = cols_of(n, width)
                rows = dot_nn(hidden[...].reshape(S, D), qkv_all[j, :, :, cols].reshape(D, width))
                rows += dot_nn(low_j, b_q(j)[:, cols])
                if j != 1:
                    rows += qkv_bias[pl.ds(j // 2, 1), cols].astype(F32)
                qkv[j, :, cols] = rows.astype(BF16)

    scale = 1.0 / math.sqrt(HEAD)

    def mark_segments():
        row = segments[...].astype(F32)
        pieces = [row[:, q * Q + c * R : q * Q + c * R + R] for c in range(C) for q in range(T)]
        row = jnp.concatenate(pieces, axis=1)
        seg_row[...] = row
        seg_col[...] = jnp.broadcast_to(row, (128, S)).T

    def turn_heads(j):
        @pl.loop(0, heads)
        def _(h):
            turned[cols_of(h, HEAD)] = qkv[j, :, cols_of(h, HEAD)].T

    def attend(c):
        rows = pl.ds(c * M, M)

        @pl.loop(0, heads)
        def _(h):
            cols = cols_of(h, HEAD)
            scores = dot_nt(qkv[1, :, cols], qkv[0, rows, cols]) * scale
            scores = jnp.where(seg_col[:, :1] == seg_row[:, rows], scores, -1e30)
            weights = jnp.exp(scores - jnp.max(scores, axis=0, keepdims=True))
            low = (weights * (1.0 / jnp.sum(weights, axis=0, keepdims=True))).astype(BF16)
            probs[h, :, rows] = low
            mixed[rows, cols] = dot_nn(turned[cols], low).T.astype(BF16)

    def attend_back(c):
        rows = pl.ds(c * M, M)

        @pl.loop(0, heads)
        def _(h):
            cols = cols_of(h, HEAD)
            weights = probs[h, :, rows].astype(F32)
            grad = dot_nt(qkv[2, :, cols], grad_mixed[rows, cols])
            centre = jnp.sum(grad * weights, axis=0, keepdims=True)
            low = (weights * (grad - centre)).astype(BF16)
            grad_scores[:, pl.ds(pl.multiple_of(h * S + c * M, M), M)] = low
            grad_qkv[0, rows, cols] = (dot_nn(turned[cols], low).T * scale).astype(BF16)

    def attend_sums():
        @pl.loop(0, heads)
        def _(h):
            cols = cols_of(h, HEAD)
            low = grad_scores[:, cols_of(h, S)]
            grad_qkv[1, :, cols] = (dot_nn(low, qkv[0, :, cols]) * scale).astype(BF16)
            grad_qkv[2, :, cols] = dot_nn(probs[h], grad_mixed[:, cols]).astype(BF16)

    grad_scores = slope

    def span(c, n):
        return pl.ds(c * M, n * M)

    def put_part(c, n, cols, rows):
        part[c : c + n, :, :, cols] = rows.astype(BF16).reshape(n, T, R, rows.shape[-1])

    group = math.gcd(F, 4)

    def by_blocks(body):
        @pl.loop(0, F // group)
        def _(turn):
            for k in range(group):
                g = turn * group + k
                body(g, cols_of(g, block))

    def mix_out(c, n):
        low = dot_nt(mixed[span(c, n)], a_o[...]).astype(BF16)
        low_o[span(c, n)] = low
        for g in range(F):
            cols = pl.ds(g * block, block)
            put_part(c, n, cols, dot_nn(mixed[span(c, n)], proj_all[g]) + dot_nn(low, b_o[:, cols]))

    def feed_up(c, n):
        low = dot_nt(chunk(normed, c, n), a_u[...]).astype(BF16)
        low_u[span(c, n)] = low

        @pl.loop(0, FL // NT)
        def _(turn):
            cols = cols_of(turn, NT)
            pre = dot_nn(chunk(normed, c, n), up_all[:, :, cols].reshape(D, NT))
            pre += dot_nn(low, b_u[:, cols]) + up_bias[cols].reshape(1, NT).astype(F32)
            square = pre * pre
            bend = jnp.tanh(ROOT * (pre + 0.044715 * square * pre))
            half = 0.5 * (1.0 + bend)
            act[span(c, n), cols] = (pre * half).astype(BF16)
            rise = half + 0.5 * pre * (1.0 - bend * bend) * (ROOT * (1.0 + 3 * 0.044715 * square))
            slope[span(c, n), cols] = rise.astype(BF16)

    def feed_down(c, n):
        low = dot_nt(act[span(c, n)], a_d[...]).astype(BF16)
        low_d[span(c, n)] = low

        @by_blocks
        def _(g, cols):
            put_part(c, n, cols, dot_nn(act[span(c, n)], down_all[g]) + dot_nn(low, b_d[:, cols]))

    def back_down(c, n):
        low = dot_nt(chunk(grad_feed, c, n), b_d[...]).astype(BF16)
        back_d[span(c, n)] = low

        @pl.loop(0, FL // NT)
        def _(turn):
            cols = cols_of(turn, NT)
            total = dot_nn(low, a_d[:, cols])
            for g in range(F):
                total += dot_nt(chunk(grad_feed, c, n, pl.ds(g * block, block)), down_all[g, cols])
            grad_pre[span(c, n), cols] = (total * slope[span(c, n), cols].astype(F32)).astype(BF16)

    def back_up(c, n):
        low = dot_nt(grad_pre[span(c, n)], b_u[...]).astype(BF16)
        back_u[span(c, n)] = low

        @by_blocks
        def _(g, cols):
            put_part(c, n, cols, dot_nt(grad_pre[span(c, n)], up_all[g]) + dot_nn(low, a_u[:, cols]))

    def back_mix(c, n):
        low = dot_nt(chunk(grad_branch, c, n), b_o[...]).astype(BF16)
        back_o[span(c, n)] = low
        total = dot_nn(low, a_o[...])
        for g in range(F):
            total += dot_nt(chunk(grad_branch, c, n, pl.ds(g * block, block)), proj_all[g])
        grad_mixed[span(c, n)] = total.astype(BF16)

    def back_project(c, n):
        lows = [back_q[j, span(c, n)] for j in range(3)]

        @by_blocks
        def _(g, cols):
            total = dot_nn(lows[0], a_q(0)[:, cols])
            for j in range(3):
                if j:
                    total += dot_nn(lows[j], a_q(j)[:, cols])
                total += dot_nt(grad_qkv[j, span(c, n)], qkv_all[j, g])
            put_part(c, n, cols, total)

    def own(c):
        return pl.ds(c * R, R)

    def meet_one(c):
        total = rs_sum(c) + hidden[c, z].astype(F32) + flat(proj_bias)
        unit, rstd = norm_parts(total)
        unit_one[own(c)] = unit
        rstd_one[own(c)] = jnp.broadcast_to(rstd, (R, 128))
        normed[c, z] = (unit * line(gains, 0) + line(shifts, 0)).astype(BF16)

    def meet_two(c):
        total = rs_sum(c) + unit_one[own(c)] * line(gains, 0) + line(shifts, 0) + flat(down_bias)
        unit, rstd = norm_parts(total)
        layer_out[own(c)] = unit * line(gains, 1) + line(shifts, 1)
        grad = norm_pull(cotangent[own(c)].astype(F32) * line(gains, 1), unit, rstd)
        grad_own[own(c)] = grad
        grad_feed[c, z] = grad.astype(BF16)

    def meet_three(c):
        grad = (grad_own[own(c)] + rs_sum(c)) * line(gains, 0)
        grad = norm_pull(grad, unit_one[own(c)], rstd_one[own(c)][:, :1])
        grad_own[own(c)] = grad
        grad_branch[c, z] = grad.astype(BF16)

    def meet_four(c):
        grad_input[own(c)] = grad_own[own(c)] + rs_sum(c)

    def turn_rows(low):
        return low.astype(F32).T.astype(BF16)

    def factor(low, right):
        return dot_nn(turn_rows(low[...]), right).astype(BF16)

    def by_columns(rows, right, place, row):
        count = rows.shape[0]
        for q in range(T):
            cols = pl.ds(q * H, H)
            place[pl.ds(row, count), cols] = dot_nn(rows, right[:, :, :, cols].reshape(S, H)).astype(BF16)

    def rows_feed():
        feed_part[pl.ds(0, 16)] = turn_rows(back_u[...])
        feed_part[pl.ds(16, 16)] = turn_rows(low_d[...])

    def units_feed():
        units_g[pl.ds(0, 16)] = factor(low_u, grad_pre[...])
        units_g[pl.ds(16, 16)] = factor(back_d, act[...])

    def wide_feed():
        rows = collect(0)
        by_columns(rows[:16], normed, feed_full, 0)
        by_columns(rows[16:], grad_feed, feed_full, 16)

    def rows_mix():
        for j in range(3):
            low = dot_nt(grad_qkv[j], b_q(j)[...]).astype(BF16)
            back_q[j] = low
            mix_part[pl.ds(16 * j, 16)] = turn_rows(low)
        mix_part[pl.ds(48, 16)] = turn_rows(low_o[...])

    def heads_mix():
        heads_g[pl.ds(48, 16)] = factor(back_o, mixed[...])
        for j in range(3):
            heads_g[pl.ds(16 * j, 16)] = factor(low_q.at[j], grad_qkv[j])
        marks = jnp.concatenate([pick[:, :1], jnp.zeros((32 - sets, 1), F32)])
        heads_g[pl.ds(64, 32)] = jnp.broadcast_to(marks, (32, H)).astype(BF16)

    def wide_mix():
        rows = collect(1)
        by_columns(rows[:48], hidden, mix_full, 0)
        by_columns(rows[48:], grad_branch, mix_full, 48)

    from_low[:, 0] = jnp.zeros((C, R, D), BF16)
    from_high[:, T - 1] = jnp.zeros((C, R, D), BF16)
    qkv_g = gathers[0]
    def own_hidden(step):
        return line_copy(hidden_in, hidden.at[:, z], g_up_send if step > 0 else g_dn_send, g_up_recv if step > 0 else g_dn_recv, C, z, step)

    @pl.when(z < T - 1)
    def _():
        own_hidden(1).start()

    @pl.when(z > 0)
    def _():
        own_hidden(-1).start()

    qkv_g.stage(0)
    for copy in own_copies + stage_copies(0) + stage_copies(1):
        copy.start()
    schedule(cfg, dict(locals()))


def schedule(cfg, env):
    T, C, K = cfg["T"], cfg["C"], env["K"]
    rs, ag, hidden = env["rs"], env["ag"], env["hidden"]
    qkv_g, proj_g, up_g, down_g, rest_g = env["gathers"][:5]
    env["mark_segments"]()
    for s in range(2):
        env["choose"](s)
    for step in range(1, K + 1):
        qkv_g.stage(step)
        if step == 1:
            proj_g.stage(0)
            ag(hidden, None, 2)
            for s in range(2, 5):
                env["choose"](s)
    if K == 0:
        proj_g.stage(0)
    if K >= 1:
        proj_g.stage(1)
    up_g.stage(0)
    if K < 1:
        ag(hidden, None, 2)
        for s in range(2, 5):
            env["choose"](s)
    for s in range(5, env["sets"]):
        env["choose"](s)
    for t in range(3, T + 1):
        ag(hidden, None, t)
    for step in range(2, K + 1):
        proj_g.stage(step)
    down_g.stage(0)
    rest_g.stage(0)
    qkv_g.finish()
    for copy in env["own_copies"]:
        copy.wait()
    env["project"]()
    env["turn_heads"](2)
    if K:
        up_g.stage(1)
    proj_g.finish()
    buffers = [env["normed"], env["grad_feed"], env["grad_branch"]]
    meets = [env["meet_one"], env["meet_two"], env["meet_three"], env["meet_four"]]

    def start_sum(chunks):
        for c in chunks:
            rs(c, 1)

    def work(kind, k, first, n):
        group = range(first, first + n)
        if kind == "up":
            if first == 0:
                up_g.finish()
            env["feed_up"](first, n)
            return
        if kind == "mix":
            env["back_mix"](first, n)
            for c in group:
                env["attend_back"](c)
            return
        if k > 0:
            for c in group:
                env["rs_drain"](c)
        if k == 0:
            for c in group:
                env["attend"](c)
            if first + n == C:
                env["turn_heads"](1)
            env["mix_out"](first, n)
        if k == 1:
            if first == 0:
                for gather in (down_g, rest_g):
                    for step in range(2, K + 1):
                        gather.stage(step)
                down_g.finish()
                rest_g.finish()
            env["feed_down"](first, n)
        if k == 2:
            env["back_down"](first, n)
            env["back_up"](first, n)
        if k == 3:
            env["back_project"](first, n)
        start_sum(group)
        if k == 2 and first + n == C:
            env["rows_feed"]()
            env["deal"](0)
            env["units_feed"]()

    def meet(k, c):
        meets[k](c)
        if k > 0:
            env["ag_drain"](buffers[k - 1], c)
        ag(buffers[k], c, 1)

    steps = []
    for k in range(3):
        steps += [("up", k, 0)] if k == 1 else []
        steps += [("work", k, 0)] + [("rs", k, t) for t in range(2, T)] + [("meet", k, 0)]
        steps += [("ag", k, t) for t in range(2, T + 1)]
    steps.append(("mix", 3, 0))
    groups, at, came, turn = cfg["groups"], [0] * C, {}, 0
    while min(at) < len(steps):
        if turn == 1 and K:
            down_g.stage(1)
            rest_g.stage(1)
        if turn == cfg["up_turn"]:
            for step in range(2, K + 1):
                up_g.stage(step)
        for c in range(C):
            if turn < cfg["lag"] * c or at[c] == len(steps):
                continue
            kind, k, t = steps[at[c]]
            if kind in ("up", "work", "mix"):
                n = groups[k]
                first = c // n * n
                came.setdefault((kind, k, first), set()).add(c)
                if len(came[kind, k, first]) < n:
                    continue
                work(kind, k, first, n)
                for member in range(first, first + n):
                    at[member] += 1
                continue
            if kind == "rs":
                rs(c, t)
            if kind == "meet":
                meet(k, c)
            if kind == "ag":
                ag(buffers[k], c, t)
            at[c] += 1
        turn += 1
    env["attend_sums"]()
    env["rows_mix"]()
    env["deal"](1)
    n, grads = groups[4], env["gathers"][5:]
    for c in range(0, C, n):
        work("work", 3, c, n)

    def shade(piece):
        if piece == 0:
            env["wide_feed"]()
            env["pass_on"](0)
        if piece == 1:
            env["heads_mix"]()
            env["wide_mix"]()
            env["pass_on"](1)
        if piece == 2 and K:
            for gather in grads:
                gather.stage(1)

    hops = [(c, t) for t in range(2, T) for c in range(C)]
    at_hop = [min(len(hops), share) for share in (C // 2, C, C + C // 2)]
    for i in range(len(hops) + 1):
        for piece in range(3):
            if at_hop[piece] == i:
                shade(piece)
        if i < len(hops):
            rs(*hops[i])
    for c in range(C):
        meets[3](c)
        if c == C // 2:
            for step in range(2, K + 1):
                for gather in grads:
                    gather.stage(step)
    for gather in grads:
        gather.finish()
    for c in range(C):
        env["rs_drain"](c)
        env["ag_drain"](buffers[2], c)
    env["ag_drain"](hidden, None)
    for which in range(2):
        env["pass_drain"](which)
    for gather in env["gathers"]:
        gather.drain()


def spread(mesh, body):
    placed = (
        P(("fsdp", "tp"), None),
        P(("fsdp", "tp"), None),
        P("fsdp", None),
        P("fsdp"),
        P(None, "fsdp", "tp"),
        P(None, "tp"),
        P("tp", "fsdp"),
        P(),
        P("fsdp", "tp"),
        P("tp"),
        P("tp", "fsdp"),
        P(),
        P(),
        P(),
        P(),
        P(None, None, None, "tp"),
        P(None, "tp", None),
        P(),
        P(),
        P(None, None, "tp"),
        P(None, "tp", None),
        P(),
    )
    return jax.shard_map(
        body,
        mesh=mesh,
        in_specs=placed,
        out_specs=(
            P(("fsdp", "tp"), None),
            P(("fsdp", "tp"), None),
            P(),
            P(None, None, None, "tp"),
            P(None, "tp", None),
            P(),
            P(),
            P(None, None, "tp"),
            P(None, "tp", None),
            P(),
        ),
        check_vma=False,
    )


def chunks_for(rows):
    return max(c for c in (1, 2, 4) if rows % (16 * c) == 0)


def place_kernel(layer_in, grad_in, feed_in, units_in, mix_in, heads_in, layer_out, grad_out, *refs):
    outs, tables = refs[:8], refs[8:16]
    feed_all, units_all, mix_all, heads_all, rows_a, rows_b, sems = refs[16:]
    F = feed_all.shape[0]
    sets = outs[2].shape[0]
    loads = [(heads_in, heads_all), (feed_in, feed_all), (units_in, units_all), (mix_in, mix_all)]
    loads += [(layer_in, rows_a), (grad_in, rows_b)]
    loads = [pltpu.make_async_copy(a, b, sems.at[k]) for k, (a, b) in enumerate(loads)]
    stores = list(zip(tables, outs)) + [(rows_a, layer_out), (rows_b, grad_out)]
    stores = [pltpu.make_async_copy(a, b, sems.at[6 + k]) for k, (a, b) in enumerate(stores)]
    for copy in loads:
        copy.start()
    order = lax.broadcasted_iota(jnp.int32, (32, 1), 0).astype(F32)
    q_in, q_out, o_in, o_out, u_in, u_out, d_in, d_out = range(8)
    loads[0].wait()
    chosen = []
    for g in range(F):
        marks = heads_all[g, pl.ds(64, 32), pl.ds(0, 128)][:, :1].astype(F32)
        chosen.append(jnp.clip(jnp.sum(marks * order).astype(jnp.int32), 0, sets - 1))

    def fill(which, rows_of):
        ref = tables[which]
        ref[...] = jnp.zeros_like(ref)
        for g in range(F):
            rows_of(ref, g, chosen[g])
        stores[which].start()

    def whole(source, row):
        def add(ref, g, s):
            ref[s] += source[g, pl.ds(row, 16)].astype(F32)

        return add

    def trio(add_of):
        def add(ref, g, s):
            for j in range(3):
                add_of(16 * j)(ref.at[j], g, s)

        return add

    fill(q_out, trio(lambda row: whole(heads_all, row)))
    fill(o_in, whole(heads_all, 48))
    loads[1].wait()
    fill(u_in, whole(feed_all, 0))
    fill(d_out, whole(feed_all, 16))
    loads[2].wait()
    fill(u_out, whole(units_all, 0))
    fill(d_in, whole(units_all, 16))
    loads[3].wait()
    fill(o_out, whole(mix_all, 48))
    fill(q_in, trio(lambda row: whole(mix_all, row)))
    for copy in loads[4:]:
        copy.wait()
    for copy in stores[8:]:
        copy.start()
    for copy in stores:
        copy.wait()


def kernel_per_device(F, T):
    def per_device(
        hidden_in, cotangent, segment_ids, adapter_set, qkv_weight, qkv_bias, proj_weight, proj_bias,
        up_weight, up_bias, down_weight, down_bias, norm_gain, norm_bias, qkv_adapt_in, qkv_adapt_out,
        attn_adapt_in, attn_adapt_out, up_adapt_in, up_adapt_out, down_adapt_in, down_adapt_out,
    ):
        Q, D = hidden_in.shape
        H, FL = qkv_weight.shape[2], up_weight.shape[1]
        S, C, sets = Q * T, chunks_for(Q), qkv_adapt_in.shape[1]
        R, block = Q // C, D // F
        cfg = dict(F=F, T=T, S=S, D=D, H=H, FL=FL, C=C, lag=1, groups=(1, 1, 1, 1, 1), up_turn=T + 1)
        turn = lambda table: jnp.swapaxes(table, -1, -2)
        vmem, anywhere = pl.BlockSpec(memory_space=pltpu.VMEM), pl.BlockSpec(memory_space=pl.ANY)
        dma = pltpu.SemaphoreType.DMA
        bank = lambda *shape: pltpu.VMEM(shape, BF16)
        wide_bank = lambda *shape: pltpu.VMEM(shape, F32)
        scratch = (
            [bank(C, T, R, D), bank(3, F, block, H), bank(F, H, block), bank(F, block, FL), bank(F, FL, block)]
            + [bank(3, S, H), bank(H // HEAD, S, S), bank(S, H), bank(C, T, R, D), bank(S, FL), bank(S, FL)]
            + [bank(C, T, R, D), bank(C, T, R, D), bank(S, H), bank(3, S, H)]
            + [bank(C, T, R, D), bank(C, T, R, D), bank(C, T, R, D)]
            + [wide_bank(Q, D), wide_bank(Q, 128), wide_bank(Q, D)]
            + [bank(3, S, RANK), bank(S, RANK), bank(S, RANK), bank(S, RANK)] * 2
            + [wide_bank(1, S), wide_bank(S, 128), bank(H, S)]
            + [bank(6, RANK, D), bank(4, RANK, H), bank(2, RANK, FL)]
            + [bank(2, 6, RANK, D), bank(2, 4, RANK, H), bank(2, 2, RANK, FL)]
            + [bank(32, S), bank(T - 1, 32, S), bank(32, D)]
            + [bank(64, S), bank(T - 1, 64, S), bank(64, D)]
            + [bank(32, FL), bank(96, H)]
            + [dma((2, 8))] + [dma((2, T - 1))] * 2
            + [dma((9, 2, F)), dma((9, 2, F))]
            + [dma((C, T))] * 4
            + [dma((C + 1, T))] * 4
            + [dma((9,))]
        )
        flops = 2 * S * (4 * D * H + 2 * D * FL) * 2
        outs = pl.pallas_call(
            functools.partial(layer_kernel, cfg),
            out_shape=[
                jax.ShapeDtypeStruct((Q, D), F32),
                jax.ShapeDtypeStruct((Q, D), F32),
                jax.ShapeDtypeStruct((F, 32, D), BF16),
                jax.ShapeDtypeStruct((F, 32, FL), BF16),
                jax.ShapeDtypeStruct((F, 64, D), BF16),
                jax.ShapeDtypeStruct((F, 96, H), BF16),
            ],
            in_specs=[anywhere] + [vmem] * 3 + [anywhere] * 4 + [vmem] * 6 + [anywhere] * 8,
            out_specs=[vmem] * 2 + [anywhere] * 4,
            scratch_shapes=scratch,
            compiler_params=pltpu.CompilerParams(
                collective_id=0, has_side_effects=True, vmem_limit_bytes=62 * 1024 * 1024
            ),
            cost_estimate=pl.CostEstimate(flops=flops, bytes_accessed=30000000, transcendentals=0),
        )(
            hidden_in.reshape(C, R, D), cotangent, segment_ids, adapter_set[None, :],
            qkv_weight, proj_weight, up_weight, down_weight,
            proj_bias, down_bias, up_bias, qkv_bias, norm_gain, norm_bias,
            turn(qkv_adapt_in), qkv_adapt_out, turn(attn_adapt_in), attn_adapt_out,
            turn(up_adapt_in), up_adapt_out, turn(down_adapt_in), down_adapt_out,
        )
        shapes = [
            (3, sets, RANK, D), (3, sets, RANK, H), (sets, RANK, H), (sets, RANK, D),
            (sets, RANK, D), (sets, RANK, FL), (sets, RANK, FL), (sets, RANK, D),
        ]
        table = lambda *shape: jax.ShapeDtypeStruct(shape, F32)
        layer_out, grad_input, q_in, q_out, o_in, o_out, u_in, u_out, d_in, d_out = pl.pallas_call(
            place_kernel,
            out_shape=[table(Q, D), table(Q, D)] + [table(*shape) for shape in shapes],
            in_specs=[anywhere] * 6,
            out_specs=[anywhere] * 10,
            scratch_shapes=[wide_bank(*shape) for shape in shapes]
            + [bank(*out.shape) for out in outs[2:]]
            + [wide_bank(Q, D), wide_bank(Q, D), dma((16,))],
            compiler_params=pltpu.CompilerParams(vmem_limit_bytes=62 * 1024 * 1024),
        )(*outs)
        return (
            layer_out, grad_input, turn(q_in), q_out, turn(o_in), o_out, turn(u_in), u_out, turn(d_in), d_out,
        )

    return per_device


def solution(mesh):
    F, T = mesh.shape["fsdp"], mesh.shape["tp"]

    def whole(*args):
        width = args[0].shape[1]
        fits = F & (F - 1) == 0 and (width // F) % 128 == 0 and T > 1 and F > 1 and args[14].shape[1] <= 32 and width // T * args[2].shape[1] <= args[8].shape[1] // T * HEAD
        return spread(mesh, kernel_per_device(F, T) if fits else per_device)(*args)

    return whole
```

```python
import functools
import math

import jax
import jax.numpy as jnp
from jax import lax
from jax.experimental import pallas as pl
from jax.experimental.pallas import tpu as pltpu
from jax.sharding import PartitionSpec as P

HEAD = 128
RANK = 16
MESH = pl.DeviceIdType.MESH
F32 = jnp.float32
BF16 = jnp.bfloat16
ROOT = math.sqrt(2.0 / math.pi)


def layer_norm(field_in, gain_row, shift_row):
    centre = jnp.mean(field_in, axis=-1, keepdims=True)
    centred = field_in - centre
    spread = jnp.mean(centred * centred, axis=-1, keepdims=True)
    return centred * lax.rsqrt(spread + 1e-05) * gain_row + shift_row


def precise_dot(left, right):
    return jnp.dot(left, right, precision=lax.Precision.HIGHEST)


def mixed_dot(left, right):
    return jnp.dot(left, right, preferred_element_type=jnp.float32)


def choose_set(table, index, axis):
    return lax.dynamic_index_in_dim(table, index, axis, keepdims=False)


def place_set(grad, index, sets, axis):
    onehot = (jnp.arange(sets) == index).astype(jnp.float32)
    shape_list = [1] * (grad.ndim + 1)
    shape_list[axis] = sets
    return jnp.expand_dims(grad, axis) * onehot.reshape(shape_list)


def per_device(
    hidden_in,
    cotangent,
    segment_ids,
    adapter_set,
    qkv_weight,
    qkv_bias,
    proj_weight,
    proj_bias,
    up_weight,
    up_bias,
    down_weight,
    down_bias,
    norm_gain,
    norm_bias,
    qkv_adapt_in,
    qkv_adapt_out,
    attn_adapt_in,
    attn_adapt_out,
    up_adapt_in,
    up_adapt_out,
    down_adapt_in,
    down_adapt_out,
):
    width_local = qkv_weight.shape[2]
    heads_local = width_local // HEAD
    sets = qkv_adapt_in.shape[1]
    chosen = adapter_set[0]
    segments = segment_ids[0]
    seq_rows = segments.shape[0]
    block_rows = min(512, seq_rows)
    blocks = seq_rows // block_rows
    score_scale = 1.0 / math.sqrt(HEAD)
    gains = norm_gain.astype(jnp.float32)
    shifts = norm_bias.astype(jnp.float32)
    first_q = choose_set(qkv_adapt_in, chosen, 1)
    second_q = choose_set(qkv_adapt_out, chosen, 1)
    first_o = choose_set(attn_adapt_in, chosen, 0)
    second_o = choose_set(attn_adapt_out, chosen, 0)
    first_u = choose_set(up_adapt_in, chosen, 0)
    second_u = choose_set(up_adapt_out, chosen, 0)
    first_d = choose_set(down_adapt_in, chosen, 0)
    second_d = choose_set(down_adapt_out, chosen, 0)
    seq_hidden = lax.all_gather(hidden_in, "tp", axis=0, tiled=True)
    qkv_full, proj_full = (
        lax.all_gather(qkv_weight, "fsdp", axis=1, tiled=True),
        lax.all_gather(proj_weight, "fsdp", axis=1, tiled=True),
    )
    main_term = jnp.einsum("sd,jdc->jsc", seq_hidden, qkv_full, preferred_element_type=jnp.float32)
    low_in = jnp.einsum("sd,jdr->jsr", seq_hidden, first_q, preferred_element_type=jnp.float32)
    low_term = jnp.einsum(
        "jsr,jrc->jsc", low_in, second_q.astype(jnp.float32), precision=lax.Precision.HIGHEST
    )
    bias_rows = jnp.stack([qkv_bias[0], jnp.zeros_like(qkv_bias[0]), qkv_bias[1]]).astype(
        jnp.float32
    )[:, None, :]
    qkv_round = (main_term + low_term + bias_rows).astype(jnp.bfloat16)
    queries = qkv_round[0].reshape(seq_rows, heads_local, HEAD)
    keys = qkv_round[1].reshape(seq_rows, heads_local, HEAD)
    values = qkv_round[2].reshape(seq_rows, heads_local, HEAD)
    query_blocks = queries.reshape(blocks, block_rows, heads_local, HEAD)
    seg_blocks = segments.reshape(blocks, block_rows)

    def scores_of(query_rows, seg_rows):
        raw_scores = (
            jnp.einsum("bhe,she->hbs", query_rows, keys, preferred_element_type=jnp.float32)
            * score_scale
        )
        same_doc = (seg_rows[:, None] == segments[None, :])[None]
        return jnp.where(same_doc, raw_scores, -1e30)

    def forward_block(inputs):
        query_rows, seg_rows = inputs
        scores = scores_of(query_rows, seg_rows)
        row_top = jnp.max(scores, axis=-1, keepdims=True)
        weights = jnp.exp(scores - row_top)
        row_total = jnp.sum(weights, axis=-1, keepdims=True)
        attn_probs = (weights / row_total).astype(jnp.bfloat16)
        attn_mixed = jnp.einsum(
            "hbs,she->bhe", attn_probs, values, preferred_element_type=jnp.float32
        )
        return (attn_mixed, (row_top + jnp.log(row_total))[..., 0])

    attn_mixed, logsum = lax.map(forward_block, (query_blocks, seg_blocks))
    attended = attn_mixed.reshape(seq_rows, width_local).astype(jnp.bfloat16)
    low_attn = mixed_dot(attended, first_o)
    second_o_wide = second_o.astype(jnp.float32)
    row_part = attended
    low_part = low_attn
    attn_sum = lax.psum_scatter(
        mixed_dot(row_part, proj_full) + precise_dot(low_part, second_o_wide),
        "tp",
        scatter_dimension=0,
        tiled=True,
    )
    first_sum = hidden_in.astype(jnp.float32) + attn_sum + proj_bias.astype(jnp.float32)
    normed = layer_norm(first_sum, gains[0], shifts[0])
    normed_round = normed.astype(jnp.bfloat16)
    seq_normed = lax.all_gather(normed_round, "tp", axis=0, tiled=True)
    up_full, down_full = (
        lax.all_gather(up_weight, "fsdp", axis=0, tiled=True),
        lax.all_gather(down_weight, "fsdp", axis=1, tiled=True),
    )
    low_up = mixed_dot(seq_normed, first_u)
    pre_act = (
        mixed_dot(seq_normed, up_full)
        + precise_dot(low_up, second_u.astype(jnp.float32))
        + up_bias.astype(jnp.float32)
    )
    act_round = jax.nn.gelu(pre_act, approximate=True).astype(jnp.bfloat16)
    low_down = mixed_dot(act_round, first_d)
    second_d_wide = second_d.astype(jnp.float32)
    row_part = act_round
    low_part = low_down
    ffn_sum = lax.psum_scatter(
        mixed_dot(row_part, down_full) + precise_dot(low_part, second_d_wide),
        "tp",
        scatter_dimension=0,
        tiled=True,
    )
    second_sum = normed + ffn_sum + down_bias.astype(jnp.float32)
    layer_out = layer_norm(second_sum, gains[1], shifts[1])
    unused, norm_back = jax.vjp(
        lambda field_in: layer_norm(field_in, gains[1], shifts[1]), second_sum
    )
    grad_second = norm_back(cotangent.astype(jnp.float32))[0]
    grad_feed_round = grad_second.astype(jnp.bfloat16)
    seq_grad_feed = lax.all_gather(grad_feed_round, "tp", axis=0, tiled=True)
    up_back, down_back = (
        lax.all_gather(up_weight, "fsdp", axis=0, tiled=True),
        lax.all_gather(down_weight, "fsdp", axis=1, tiled=True),
    )
    grad_low_down = mixed_dot(seq_grad_feed, second_d.T)
    grad_act = jnp.einsum(
        "sd,fd->sf", seq_grad_feed, down_back, preferred_element_type=jnp.float32
    ) + precise_dot(grad_low_down, first_d.astype(jnp.float32).T)
    unused, gelu_back = jax.vjp(lambda field_in: jax.nn.gelu(field_in, approximate=True), pre_act)
    grad_pre_round = gelu_back(grad_act)[0].astype(jnp.bfloat16)
    grad_down_out_part = precise_dot(low_down.T, seq_grad_feed.astype(jnp.float32))
    grad_down_in_part = precise_dot(act_round.astype(jnp.float32).T, grad_low_down)
    grad_low_up = mixed_dot(grad_pre_round, second_u.T)
    grad_up_out_part = precise_dot(low_up.T, grad_pre_round.astype(jnp.float32))
    grad_up_in_part = precise_dot(seq_normed.astype(jnp.float32).T, grad_low_up)
    first_u_wide = first_u.astype(jnp.float32)
    row_part = grad_pre_round
    low_part = grad_low_up
    grad_normed = grad_second + lax.psum_scatter(
        jnp.einsum("sf,df->sd", row_part, up_back, preferred_element_type=jnp.float32)
        + precise_dot(low_part, first_u_wide.T),
        "tp",
        scatter_dimension=0,
        tiled=True,
    )
    unused, norm_front = jax.vjp(
        lambda field_in: layer_norm(field_in, gains[0], shifts[0]), first_sum
    )
    grad_first = norm_front(grad_normed)[0]
    grad_branch_round = grad_first.astype(jnp.bfloat16)
    seq_grad_branch = lax.all_gather(grad_branch_round, "tp", axis=0, tiled=True)
    qkv_back, proj_back = (
        lax.all_gather(qkv_weight, "fsdp", axis=1, tiled=True),
        lax.all_gather(proj_weight, "fsdp", axis=1, tiled=True),
    )
    grad_low_attn = mixed_dot(seq_grad_branch, second_o.T)
    grad_attended = jnp.einsum(
        "sd,cd->sc", seq_grad_branch, proj_back, preferred_element_type=jnp.float32
    ) + precise_dot(grad_low_attn, first_o.astype(jnp.float32).T)
    grad_attended_round = grad_attended.astype(jnp.bfloat16)
    grad_attn_out_part = precise_dot(low_attn.T, seq_grad_branch.astype(jnp.float32))
    grad_attn_in_part = precise_dot(attended.astype(jnp.float32).T, grad_low_attn)
    grad_blocks = grad_attended_round.reshape(blocks, block_rows, heads_local, HEAD)

    def backward_block(carry, inputs):
        grad_keys, grad_values = carry
        query_rows, seg_rows, lse_rows, grad_rows = inputs
        scores = scores_of(query_rows, seg_rows)
        attn_probs = jnp.exp(scores - lse_rows[..., None])
        grad_probs = jnp.einsum(
            "bhe,she->hbs", grad_rows, values, preferred_element_type=jnp.float32
        )
        centre = jnp.sum(grad_probs * attn_probs, axis=-1, keepdims=True)
        grad_scores = (attn_probs * (grad_probs - centre)).astype(jnp.bfloat16)
        grad_query = (
            jnp.einsum("hbs,she->bhe", grad_scores, keys, preferred_element_type=jnp.float32)
            * score_scale
        )
        grad_keys = (
            grad_keys
            + jnp.einsum(
                "hbs,bhe->she", grad_scores, query_rows, preferred_element_type=jnp.float32
            )
            * score_scale
        )
        grad_values = grad_values + jnp.einsum(
            "hbs,bhe->she",
            attn_probs.astype(jnp.bfloat16),
            grad_rows,
            preferred_element_type=jnp.float32,
        )
        return ((grad_keys, grad_values), grad_query)

    zero_state = jnp.zeros((seq_rows, heads_local, HEAD), jnp.float32)
    key_value_grads, grad_queries = lax.scan(
        backward_block, (zero_state, zero_state), (query_blocks, seg_blocks, logsum, grad_blocks)
    )
    grad_qkv_round = jnp.stack(
        [
            grad_queries.reshape(seq_rows, width_local),
            key_value_grads[0].reshape(seq_rows, width_local),
            key_value_grads[1].reshape(seq_rows, width_local),
        ]
    ).astype(jnp.bfloat16)
    grad_qkv_out_part = jnp.einsum(
        "jsr,jsc->jrc", low_in, grad_qkv_round.astype(jnp.float32), precision=lax.Precision.HIGHEST
    )
    grad_low_qkv = jnp.einsum(
        "jsc,jrc->jsr", grad_qkv_round, second_q, preferred_element_type=jnp.float32
    )
    grad_qkv_in_part = jnp.einsum(
        "sd,jsr->jdr", seq_hidden.astype(jnp.float32), grad_low_qkv, precision=lax.Precision.HIGHEST
    )
    first_q_wide = first_q.astype(jnp.float32)
    row_part = grad_qkv_round
    low_part = grad_low_qkv
    grad_input = grad_first + lax.psum_scatter(
        (
            jnp.einsum("jsc,jdc->sd", row_part, qkv_back, preferred_element_type=jnp.float32)
            + jnp.einsum("jsr,jdr->sd", low_part, first_q_wide, precision=lax.Precision.HIGHEST)
        ).astype(jnp.bfloat16),
        "tp",
        scatter_dimension=0,
        tiled=True,
    ).astype(jnp.float32)
    wide_grads = lax.psum(
        (
            place_set(grad_qkv_in_part, chosen, sets, 1),
            place_set(grad_attn_out_part, chosen, sets, 0),
            place_set(grad_up_in_part, chosen, sets, 0),
            place_set(grad_down_out_part, chosen, sets, 0),
        ),
        ("fsdp", "tp"),
    )
    split_grads = (
        lax.psum(place_set(grad_qkv_out_part, chosen, sets, 1).astype(jnp.bfloat16), "fsdp").astype(
            jnp.float32
        ),
        lax.psum(place_set(grad_attn_in_part, chosen, sets, 0).astype(jnp.bfloat16), "fsdp").astype(
            jnp.float32
        ),
        lax.psum(place_set(grad_up_out_part, chosen, sets, 0).astype(jnp.bfloat16), "fsdp").astype(
            jnp.float32
        ),
        lax.psum(place_set(grad_down_in_part, chosen, sets, 0).astype(jnp.bfloat16), "fsdp").astype(
            jnp.float32
        ),
    )
    return (
        layer_out,
        grad_input,
        wide_grads[0],
        split_grads[0],
        split_grads[1],
        wide_grads[1],
        wide_grads[2],
        split_grads[2],
        split_grads[3],
        wide_grads[3],
    )


def dot_nn(left, right):
    return jnp.dot(left, right, preferred_element_type=F32)


def dot_nt(left, right):
    return lax.dot_general(left, right, (((1,), (1,)), ((), ())), preferred_element_type=F32)


def flip(index, mask):
    out, bit = index, 1
    while bit <= mask:
        if mask & bit:
            out = out + bit - 2 * bit * lax.rem(lax.div(index, bit), 2)
        bit *= 2
    return out


def norm_parts(rows):
    centred = rows - jnp.mean(rows, axis=-1, keepdims=True)
    spread = jnp.mean(centred * centred, axis=-1, keepdims=True)
    rstd = lax.rsqrt(spread + 1e-05)
    return centred * rstd, rstd


def norm_pull(grad, unit, rstd):
    return rstd * (
        grad
        - jnp.mean(grad, axis=-1, keepdims=True)
        - unit * jnp.mean(grad * unit, axis=-1, keepdims=True)
    )


class Gather:
    def __init__(self, which, shard, whole, send, recv, fsdp, tp, count):
        self.which, self.shard, self.whole = which, shard, whole
        self.send, self.recv, self.fsdp, self.tp = send, recv, fsdp, tp
        bits = [1 << i for i in range(1, count.bit_length() - 1)]
        self.orders = [bits, bits[::-1]]
        self.steps = len(bits)
        self.held = [[0], [0]]
        self.sent = []
        self.count = count

    def copy(self, half, mask, bit):
        landed = mask ^ bit
        place = self.whole(flip(self.fsdp, mask), half)
        return pltpu.make_async_remote_copy(
            src_ref=self.shard(half) if mask == 0 else place,
            dst_ref=place,
            send_sem=self.send.at[self.which, half, landed],
            recv_sem=self.recv.at[self.which, half, landed],
            device_id=(flip(self.fsdp, bit), self.tp),
            device_id_type=MESH,
        )

    def launch(self, half, mask, bit):
        self.copy(half, mask, bit).start()
        self.sent.append((half, mask, bit))

    def await_block(self, half, mask, bit):
        place = self.whole(flip(self.fsdp, mask), half)
        pltpu.make_async_remote_copy(
            src_ref=place,
            dst_ref=place,
            send_sem=self.send.at[self.which, half, mask],
            recv_sem=self.recv.at[self.which, half, mask],
            device_id=(flip(self.fsdp, bit), self.tp),
            device_id_type=MESH,
        ).wait_recv()

    def stage(self, step):
        for half in range(2):
            fresh = [0]
            if step > 0:
                bit = self.orders[half][step - 1]
                fresh = [mask ^ bit for mask in self.held[half]]
                for mask in fresh:
                    self.await_block(half, mask, bit)
                self.held[half] = self.held[half] + fresh
            if step < self.steps:
                for mask in self.held[half]:
                    self.launch(half, mask, self.orders[half][step])
            for mask in fresh:
                self.launch(half, mask, 1)

    def finish(self):
        for half in range(2):
            for mask in self.held[half]:
                self.await_block(half, mask ^ 1, 1)

    def drain(self):
        for half, mask, bit in self.sent:
            self.copy(half, mask, bit).wait_send()


def layer_kernel(cfg, *refs):
    F, T, S, D, H, FL, C = (cfg[k] for k in ("F", "T", "S", "D", "H", "FL", "C"))
    Q, heads, block = S // T, H // HEAD, D // F
    R = Q // C
    M = T * R
    NT = math.gcd(FL, 512)
    (
        hidden_in, cotangent, segments, chosen, qkv_w, proj_w, up_w, down_w,
        proj_bias, down_bias, up_bias, qkv_bias, gains, shifts,
        q_in, q_out, o_in, o_out, u_in, u_out, d_in, d_out,
        layer_out, grad_input, feed_all, units_all, mix_all, heads_all,
        hidden, qkv_all, proj_all, up_all, down_all,
        qkv, probs, mixed, normed, act, slope, grad_feed, grad_branch, grad_mixed, grad_qkv,
        part, from_low, from_high, unit_one, rstd_one, grad_own,
        low_q, low_o, low_u, low_d, back_q, back_o, back_u, back_d,
        seg_row, seg_col, turned,
        wide_f, heads_f, units_f, wide_stage, heads_stage, units_stage,
        feed_part, feed_land, feed_full, mix_part, mix_land, mix_full, units_g, heads_g,
        stage_sem, deal_send, deal_recv,
        w_send, w_recv, up_send, up_recv, dn_send, dn_recv, g_up_send, g_up_recv, g_dn_send, g_dn_recv,
        own_sem,
    ) = refs
    grad_pre = slope
    f, z = lax.axis_index("fsdp"), lax.axis_index("tp")
    bits = [1 << i for i in range(F.bit_length() - 1)]

    barrier = pltpu.get_barrier_semaphore()
    for bit in bits:
        pl.semaphore_signal(barrier, inc=1, device_id=(flip(f, bit), z), device_id_type=MESH)

    turns = [lax.rem(z + k, T) for k in range(T)]
    for k in range(1, T):
        pl.semaphore_signal(barrier, inc=1, device_id=(f, turns[k]), device_id_type=MESH)
    pl.semaphore_wait(barrier, len(bits) + T - 1)

    rows_of = lambda total, half: pl.ds(half * (total // 2), total // 2)
    gathers = [
        Gather(0, lambda h: qkv_w.at[:, rows_of(block, h)], lambda g, h: qkv_all.at[:, g, rows_of(block, h)], w_send, w_recv, f, z, F),
        Gather(1, lambda h: proj_w.at[rows_of(H, h)], lambda g, h: proj_all.at[g, rows_of(H, h)], w_send, w_recv, f, z, F),
        Gather(2, lambda h: up_w.at[rows_of(block, h)], lambda g, h: up_all.at[g, rows_of(block, h)], w_send, w_recv, f, z, F),
    ]
    quarter = lambda part, h: pl.ds((2 * part + h) * (FL // 4), FL // 4)
    for part_of in range(2):
        shard = lambda h, p=part_of: down_w.at[quarter(p, h)]
        whole = lambda g, h, p=part_of: down_all.at[g, quarter(p, h)]
        gathers.append(Gather(3 + part_of, shard, whole, w_send, w_recv, f, z, F))
    pair = lambda ref, n: lambda h: ref.at[..., rows_of(n, h), :]
    pair_all = lambda ref, n: lambda g, h: ref.at[g, ..., rows_of(n, h), :]
    for k, (shard, whole) in enumerate(
        [(feed_full, feed_all), (units_g, units_all), (mix_full, mix_all), (heads_g, heads_all)]
    ):
        n = shard.shape[-2]
        gathers.append(Gather(5 + k, pair(shard, n), pair_all(whole, n), w_send, w_recv, f, z, F))
    K = gathers[0].steps
    own_copies = [
        pltpu.make_async_copy(hidden_in, hidden.at[:, z], own_sem.at[0]),
        pltpu.make_async_copy(qkv_w, qkv_all.at[:, f], own_sem.at[1]),
        pltpu.make_async_copy(proj_w, proj_all.at[f], own_sem.at[2]),
        pltpu.make_async_copy(up_w, up_all.at[f], own_sem.at[3]),
        pltpu.make_async_copy(down_w, down_all.at[f], own_sem.at[4]),
    ]
    own_grads = [
        pltpu.make_async_copy(feed_full, feed_all.at[f], own_sem.at[5]),
        pltpu.make_async_copy(units_g, units_all.at[f], own_sem.at[6]),
        pltpu.make_async_copy(mix_full, mix_all.at[f], own_sem.at[7]),
        pltpu.make_async_copy(heads_g, heads_all.at[f], own_sem.at[8]),
    ]

    def deal_copy(which, k):
        part_ref, land_ref = exchanges[which]
        return pltpu.make_async_remote_copy(
            src_ref=part_ref, dst_ref=land_ref.at[k - 1],
            send_sem=deal_send.at[which, k - 1], recv_sem=deal_recv.at[which, k - 1],
            device_id=(f, turns[k]), device_id_type=MESH,
        )

    exchanges = [(feed_part, feed_land), (mix_part, mix_land)]

    def deal(which):
        for k in range(1, T):
            deal_copy(which, k).start()

    def collect(which):
        part_ref, land_ref = exchanges[which]
        total = part_ref[...].astype(F32)
        for k in range(1, T):
            deal_copy(which, k).wait_recv()
            total += land_ref[k - 1].astype(F32)
        return total.astype(BF16)

    def pass_on(which):
        for k in (2 * which, 2 * which + 1):
            own_grads[k].start()
            gathers[5 + k].stage(0)

    def pass_drain(which):
        for k in range(1, T):
            deal_copy(which, k).wait_send()
        for k in (2 * which, 2 * which + 1):
            own_grads[k].wait()

    def line_copy(src, dst, send, recv, c, q, step):
        return pltpu.make_async_remote_copy(
            src_ref=src, dst_ref=dst, send_sem=send.at[c, q], recv_sem=recv.at[c, q],
            device_id=(f, z + step), device_id_type=MESH,
        )

    def rs_copy(c, q, step):
        landing, send, recv = (from_low, up_send, up_recv) if step > 0 else (from_high, dn_send, dn_recv)
        return line_copy(part.at[c, q], landing.at[c, q], send, recv, c, q, step)

    def rs_wait(c, q, step):
        landing, send, recv = (from_low, up_send, up_recv) if step > 0 else (from_high, dn_send, dn_recv)
        line_copy(landing.at[c, q], landing.at[c, q], send, recv, c, q, -step).wait_recv()

    def rs(c, t):
        def add(q, landing):
            part[c, q] = part[c, q] + landing[c, q]

        @pl.when(z <= t - 1)
        def _():
            q = T - t + z

            @pl.when(z > 0)
            def _():
                rs_wait(c, q, 1)
                add(q, from_low)

            rs_copy(c, q, 1).start()

        @pl.when(z >= T - t)
        def _():
            q = z - (T - t)

            @pl.when(z < T - 1)
            def _():
                rs_wait(c, q, -1)
                add(q, from_high)

            rs_copy(c, q, -1).start()

    def rs_end(c):
        @pl.when(z > 0)
        def _():
            rs_wait(c, z, 1)

        @pl.when(z < T - 1)
        def _():
            rs_wait(c, z, -1)

    def rs_sum(c, rows):
        terms = [ref[c, z, rows].astype(F32) for ref in (part, from_low, from_high)]
        return (terms[0] + terms[1]) + terms[2]

    def rs_drain(c):
        for q in range(T):
            if q > 0:

                @pl.when(z < q)
                def _(q=q):
                    rs_copy(c, q, 1).wait_send()

            if q < T - 1:

                @pl.when(z > q)
                def _(q=q):
                    rs_copy(c, q, -1).wait_send()

    def ag_copy(buffer, c, q, step):
        send, recv = (g_up_send, g_up_recv) if step > 0 else (g_dn_send, g_dn_recv)
        if c is None:
            return line_copy(buffer.at[:, q], buffer.at[:, q], send, recv, C, q, step)
        return line_copy(buffer.at[c, q], buffer.at[c, q], send, recv, c, q, step)

    def ag_wait(buffer, c, q, step):
        send, recv = (g_up_send, g_up_recv) if step > 0 else (g_dn_send, g_dn_recv)
        place = buffer.at[:, q] if c is None else buffer.at[c, q]
        line_copy(place, place, send, recv, C if c is None else c, q, -step).wait_recv()

    def ag(buffer, c, t):
        if t == 1:

            @pl.when(z < T - 1)
            def _():
                ag_copy(buffer, c, z, 1).start()

            @pl.when(z > 0)
            def _():
                ag_copy(buffer, c, z, -1).start()

            return

        @pl.when(z >= t - 1)
        def _():
            q = z - (t - 1)
            ag_wait(buffer, c, q, 1)

            @pl.when(z < T - 1)
            def _():
                ag_copy(buffer, c, q, 1).start()

        @pl.when(z <= T - t)
        def _():
            q = z + (t - 1)
            ag_wait(buffer, c, q, -1)

            @pl.when(z > 0)
            def _():
                ag_copy(buffer, c, q, -1).start()

    def ag_drain(buffer, c):
        for q in range(T):

            @pl.when((z >= q) & (z < T - 1))
            def _(q=q):
                ag_copy(buffer, c, q, 1).wait_send()

            @pl.when((z <= q) & (z > 0))
            def _(q=q):
                ag_copy(buffer, c, q, -1).wait_send()

    a_q = lambda j: wide_f.at[j]
    b_o, a_u, b_d = wide_f.at[3], wide_f.at[4], wide_f.at[5]
    b_q = lambda j: heads_f.at[j]
    a_o = heads_f.at[3]
    b_u, a_d = units_f.at[0], units_f.at[1]
    line = lambda ref, k: ref[pl.ds(k, 1)].astype(F32)
    flat = lambda ref: ref[...].reshape(1, ref.shape[0]).astype(F32)
    sets = q_in.shape[1]
    pick = (lax.broadcasted_iota(jnp.int32, (sets, 128), 0) == chosen[...]).astype(F32)

    def stage_copies(s):
        slot = s % 2
        pairs = [
            (q_in.at[:, s], wide_stage.at[slot, pl.ds(0, 3)]),
            (o_out.at[s], wide_stage.at[slot, 3]),
            (u_in.at[s], wide_stage.at[slot, 4]),
            (d_out.at[s], wide_stage.at[slot, 5]),
            (q_out.at[:, s], heads_stage.at[slot, pl.ds(0, 3)]),
            (o_in.at[s], heads_stage.at[slot, 3]),
            (u_out.at[s], units_stage.at[slot, 0]),
            (d_in.at[s], units_stage.at[slot, 1]),
        ]
        return [
            pltpu.make_async_copy(src, dst, stage_sem.at[slot, k])
            for k, (src, dst) in enumerate(pairs)
        ]

    def choose(s):
        for copy in stage_copies(s):
            copy.wait()
        weight = pick[s : s + 1, :1].astype(BF16)
        for stage, held in ((wide_stage, wide_f), (heads_stage, heads_f), (units_stage, units_f)):
            for k in range(held.shape[0]):
                term = stage[s % 2, k] * weight
                held[k] = term if s == 0 else held[k] + term
        if s + 2 < sets:
            for copy in stage_copies(s + 2):
                copy.start()

    def chunk(buffer, c, n, cols=slice(None)):
        rows = buffer[c : c + n, :, :, cols]
        return rows.reshape(n * M, rows.shape[-1])

    def cols_of(g, size):
        return pl.ds(pl.multiple_of(g * size, size), size)

    def project():
        width = math.gcd(H, 256)
        for j in range(3):
            low_j = dot_nt(hidden[...].reshape(S, D), a_q(j)[...]).astype(BF16)
            low_q[j] = low_j

            @pl.loop(0, H // width)
            def _(n, j=j, low_j=low_j):
                cols = cols_of(n, width)
                rows = dot_nn(hidden[...].reshape(S, D), qkv_all[j, :, :, cols].reshape(D, width))
                rows += dot_nn(low_j, b_q(j)[:, cols])
                if j != 1:
                    rows += qkv_bias[pl.ds(j // 2, 1), cols].astype(F32)
                qkv[j, :, cols] = rows.astype(BF16)

    scale = 1.0 / math.sqrt(HEAD)

    def mark_segments():
        row = segments[...].astype(F32)
        pieces = [row[:, q * Q + c * R : q * Q + c * R + R] for c in range(C) for q in range(T)]
        row = jnp.concatenate(pieces, axis=1)
        seg_row[...] = row
        seg_col[...] = jnp.broadcast_to(row, (128, S)).T

    def turn_heads(j):
        @pl.loop(0, heads)
        def _(h):
            turned[cols_of(h, HEAD)] = qkv[j, :, cols_of(h, HEAD)].T

    def attend(c):
        rows = pl.ds(c * M, M)

        @pl.loop(0, heads)
        def _(h):
            cols = cols_of(h, HEAD)
            scores = dot_nt(qkv[1, :, cols], qkv[0, rows, cols]) * scale
            scores = jnp.where(seg_col[:, :1] == seg_row[:, rows], scores, -1e30)
            weights = jnp.exp(scores - jnp.max(scores, axis=0, keepdims=True))
            low = (weights * (1.0 / jnp.sum(weights, axis=0, keepdims=True))).astype(BF16)
            probs[h, :, rows] = low
            mixed[rows, cols] = dot_nn(turned[cols], low).T.astype(BF16)

    def attend_back(c):
        rows = pl.ds(c * M, M)

        @pl.loop(0, heads)
        def _(h):
            cols = cols_of(h, HEAD)
            weights = probs[h, :, rows].astype(F32)
            grad = dot_nt(qkv[2, :, cols], grad_mixed[rows, cols])
            centre = jnp.sum(grad * weights, axis=0, keepdims=True)
            low = (weights * (grad - centre)).astype(BF16)
            grad_scores[:, pl.ds(pl.multiple_of(h * S + c * M, M), M)] = low
            grad_qkv[0, rows, cols] = (dot_nn(turned[cols], low).T * scale).astype(BF16)

    def attend_sums():
        @pl.loop(0, heads)
        def _(h):
            cols = cols_of(h, HEAD)
            low = grad_scores[:, cols_of(h, S)]
            grad_qkv[1, :, cols] = (dot_nn(low, qkv[0, :, cols]) * scale).astype(BF16)
            grad_qkv[2, :, cols] = dot_nn(probs[h], grad_mixed[:, cols]).astype(BF16)

    grad_scores = slope

    def span(c, n):
        return pl.ds(c * M, n * M)

    def put_part(c, n, cols, rows):
        part[c : c + n, :, :, cols] = rows.astype(BF16).reshape(n, T, R, rows.shape[-1])

    group = math.gcd(F, 2)

    def by_blocks(body):
        @pl.loop(0, F // group)
        def _(turn):
            for k in range(group):
                g = turn * group + k
                body(g, cols_of(g, block))

    def mix_out(c, n):
        low = dot_nt(mixed[span(c, n)], a_o[...]).astype(BF16)
        low_o[span(c, n)] = low

        @by_blocks
        def _(g, cols):
            put_part(c, n, cols, dot_nn(mixed[span(c, n)], proj_all[g]) + dot_nn(low, b_o[:, cols]))

    def feed_up(c, n):
        low = dot_nt(chunk(normed, c, n), a_u[...]).astype(BF16)
        low_u[span(c, n)] = low

        @pl.loop(0, FL // NT)
        def _(turn):
            cols = cols_of(turn, NT)
            pre = dot_nn(chunk(normed, c, n), up_all[:, :, cols].reshape(D, NT))
            pre += dot_nn(low, b_u[:, cols]) + up_bias[cols].reshape(1, NT).astype(F32)
            square = pre * pre
            bend = jnp.tanh(ROOT * (pre + 0.044715 * square * pre))
            half = 0.5 * (1.0 + bend)
            act[span(c, n), cols] = (pre * half).astype(BF16)
            rise = half + 0.5 * pre * (1.0 - bend * bend) * (ROOT * (1.0 + 3 * 0.044715 * square))
            slope[span(c, n), cols] = rise.astype(BF16)

    def feed_down(c, n):
        low = dot_nt(act[span(c, n)], a_d[...]).astype(BF16)
        low_d[span(c, n)] = low

        @by_blocks
        def _(g, cols):
            put_part(c, n, cols, dot_nn(act[span(c, n)], down_all[g]) + dot_nn(low, b_d[:, cols]))

    def back_down(c, n):
        low = dot_nt(chunk(grad_feed, c, n), b_d[...]).astype(BF16)
        back_d[span(c, n)] = low

        @pl.loop(0, FL // NT)
        def _(turn):
            cols = cols_of(turn, NT)
            total = dot_nn(low, a_d[:, cols])
            for g in range(F):
                total += dot_nt(chunk(grad_feed, c, n, pl.ds(g * block, block)), down_all[g, cols])
            grad_pre[span(c, n), cols] = (total * slope[span(c, n), cols].astype(F32)).astype(BF16)

    def back_up(c, n):
        low = dot_nt(grad_pre[span(c, n)], b_u[...]).astype(BF16)
        back_u[span(c, n)] = low

        @by_blocks
        def _(g, cols):
            put_part(c, n, cols, dot_nt(grad_pre[span(c, n)], up_all[g]) + dot_nn(low, a_u[:, cols]))

    def back_mix(c, n):
        low = dot_nt(chunk(grad_branch, c, n), b_o[...]).astype(BF16)
        back_o[span(c, n)] = low
        total = dot_nn(low, a_o[...])
        for g in range(F):
            total += dot_nt(chunk(grad_branch, c, n, pl.ds(g * block, block)), proj_all[g])
        grad_mixed[span(c, n)] = total.astype(BF16)

    def back_project(c, n):
        lows = [back_q[j, span(c, n)] for j in range(3)]

        @by_blocks
        def _(g, cols):
            total = dot_nn(lows[0], a_q(0)[:, cols])
            for j in range(3):
                if j:
                    total += dot_nn(lows[j], a_q(j)[:, cols])
                total += dot_nt(grad_qkv[j, span(c, n)], qkv_all[j, g])
            put_part(c, n, cols, total)

    def by_rows(body):
        def all_rows(c):
            rs_end(c)

            @pl.loop(0, R // 16)
            def _(k):
                body(c, cols_of(k, 16), pl.ds(pl.multiple_of(c * R + k * 16, 16), 16))

        return all_rows

    @by_rows
    def meet_one(c, rows, own):
        total = rs_sum(c, rows) + hidden[c, z, rows].astype(F32) + flat(proj_bias)
        unit, rstd = norm_parts(total)
        unit_one[own] = unit
        rstd_one[own] = jnp.broadcast_to(rstd, (16, 128))
        normed[c, z, rows] = (unit * line(gains, 0) + line(shifts, 0)).astype(BF16)

    @by_rows
    def meet_two(c, rows, own):
        total = rs_sum(c, rows) + unit_one[own] * line(gains, 0) + line(shifts, 0) + flat(down_bias)
        unit, rstd = norm_parts(total)
        layer_out[own] = unit * line(gains, 1) + line(shifts, 1)
        grad = norm_pull(cotangent[own].astype(F32) * line(gains, 1), unit, rstd)
        grad_own[own] = grad
        grad_feed[c, z, rows] = grad.astype(BF16)

    @by_rows
    def meet_three(c, rows, own):
        grad = (grad_own[own] + rs_sum(c, rows)) * line(gains, 0)
        grad = norm_pull(grad, unit_one[own], rstd_one[own][:, :1])
        grad_own[own] = grad
        grad_branch[c, z, rows] = grad.astype(BF16)

    @by_rows
    def meet_four(c, rows, own):
        grad_input[own] = grad_own[own] + rs_sum(c, rows)

    def turn_rows(low):
        return low.astype(F32).T.astype(BF16)

    def factor(low, right):
        return dot_nn(turn_rows(low[...]), right).astype(BF16)

    def by_columns(rows, right, place, row):
        count = rows.shape[0]

        @pl.loop(0, T)
        def _(q):
            cols = cols_of(q, H)
            place[pl.ds(row, count), cols] = dot_nn(rows, right[:, :, :, cols].reshape(S, H)).astype(BF16)

    def rows_feed():
        feed_part[pl.ds(0, 16)] = turn_rows(back_u[...])
        feed_part[pl.ds(16, 16)] = turn_rows(low_d[...])

    def units_feed():
        units_g[pl.ds(0, 16)] = factor(low_u, grad_pre[...])
        units_g[pl.ds(16, 16)] = factor(back_d, act[...])

    def wide_feed():
        rows = collect(0)
        by_columns(rows[:16], normed, feed_full, 0)
        by_columns(rows[16:], grad_feed, feed_full, 16)

    def rows_mix():
        for j in range(3):
            low = dot_nt(grad_qkv[j], b_q(j)[...]).astype(BF16)
            back_q[j] = low
            mix_part[pl.ds(16 * j, 16)] = turn_rows(low)
        mix_part[pl.ds(48, 16)] = turn_rows(low_o[...])

    def heads_mix():
        heads_g[pl.ds(48, 16)] = factor(back_o, mixed[...])
        for j in range(3):
            heads_g[pl.ds(16 * j, 16)] = factor(low_q.at[j], grad_qkv[j])
        marks = jnp.concatenate([pick[:, :1], jnp.zeros((32 - sets, 1), F32)])
        heads_g[pl.ds(64, 32)] = jnp.broadcast_to(marks, (32, H)).astype(BF16)

    def wide_mix():
        rows = collect(1)
        by_columns(rows[:48], hidden, mix_full, 0)
        by_columns(rows[48:], grad_branch, mix_full, 48)

    from_low[:, 0] = jnp.zeros((C, R, D), BF16)
    from_high[:, T - 1] = jnp.zeros((C, R, D), BF16)
    qkv_g = gathers[0]
    def own_hidden(step):
        return line_copy(hidden_in, hidden.at[:, z], g_up_send if step > 0 else g_dn_send, g_up_recv if step > 0 else g_dn_recv, C, z, step)

    @pl.when(z < T - 1)
    def _():
        own_hidden(1).start()

    @pl.when(z > 0)
    def _():
        own_hidden(-1).start()

    qkv_g.stage(0)
    for copy in own_copies + stage_copies(0) + stage_copies(1):
        copy.start()
    schedule(cfg, dict(locals()))


def schedule(cfg, env):
    T, C, K = cfg["T"], cfg["C"], env["K"]
    rs, ag, hidden = env["rs"], env["ag"], env["hidden"]
    qkv_g, proj_g, up_g, down_g, rest_g = env["gathers"][:5]
    env["mark_segments"]()
    for s in range(2):
        env["choose"](s)
    for step in range(1, K + 1):
        qkv_g.stage(step)
        if step == 1:
            proj_g.stage(0)
            ag(hidden, None, 2)
            for s in range(2, 5):
                env["choose"](s)
    if K == 0:
        proj_g.stage(0)
    if K >= 1:
        proj_g.stage(1)
    up_g.stage(0)
    if K < 1:
        ag(hidden, None, 2)
        for s in range(2, 5):
            env["choose"](s)
    for s in range(5, env["sets"]):
        env["choose"](s)
    for t in range(3, T + 1):
        ag(hidden, None, t)
    for step in range(2, K + 1):
        proj_g.stage(step)
    down_g.stage(0)
    rest_g.stage(0)
    qkv_g.finish()
    for copy in env["own_copies"]:
        copy.wait()
    env["project"]()
    env["turn_heads"](2)
    if K:
        up_g.stage(1)
    proj_g.finish()
    buffers = [env["normed"], env["grad_feed"], env["grad_branch"]]
    meets = [env["meet_one"], env["meet_two"], env["meet_three"], env["meet_four"]]

    def start_sum(chunks):
        for c in chunks:
            rs(c, 1)

    def work(kind, k, first, n):
        group = range(first, first + n)
        if kind == "up":
            if first == 0:
                up_g.finish()
            env["feed_up"](first, n)
            return
        if kind == "mix":
            env["back_mix"](first, n)
            for c in group:
                env["attend_back"](c)
            return
        if k > 0:
            for c in group:
                env["rs_drain"](c)
        if k == 0:
            for c in group:
                env["attend"](c)
            if first + n == C:
                env["turn_heads"](1)
            env["mix_out"](first, n)
        if k == 1:
            if first == 0:
                for gather in (down_g, rest_g):
                    for step in range(2, K + 1):
                        gather.stage(step)
                down_g.finish()
                rest_g.finish()
            env["feed_down"](first, n)
        if k == 2:
            env["back_down"](first, n)
            env["back_up"](first, n)
        if k == 3:
            env["back_project"](first, n)
        start_sum(group)
        if k == 2 and first + n == C:
            env["rows_feed"]()
            env["deal"](0)
            env["units_feed"]()

    def meet(k, c):
        meets[k](c)
        if k > 0:
            env["ag_drain"](buffers[k - 1], c)
        ag(buffers[k], c, 1)

    steps = []
    for k in range(3):
        steps += [("up", k, 0)] if k == 1 else []
        steps += [("work", k, 0)] + [("rs", k, t) for t in range(2, T)] + [("meet", k, 0)]
        steps += [("ag", k, t) for t in range(2, T + 1)]
    steps.append(("mix", 3, 0))
    groups, at, came, turn = cfg["groups"], [0] * C, {}, 0
    while min(at) < len(steps):
        if turn == 1 and K:
            down_g.stage(1)
            rest_g.stage(1)
        if turn == cfg["up_turn"]:
            for step in range(2, K + 1):
                up_g.stage(step)
        for c in range(C):
            if turn < cfg["lag"] * c or at[c] == len(steps):
                continue
            kind, k, t = steps[at[c]]
            if kind in ("up", "work", "mix"):
                n = groups[k]
                first = c // n * n
                came.setdefault((kind, k, first), set()).add(c)
                if len(came[kind, k, first]) < n:
                    continue
                work(kind, k, first, n)
                for member in range(first, first + n):
                    at[member] += 1
                continue
            if kind == "rs":
                rs(c, t)
            if kind == "meet":
                meet(k, c)
            if kind == "ag":
                ag(buffers[k], c, t)
            at[c] += 1
        turn += 1
    env["attend_sums"]()
    env["rows_mix"]()
    env["deal"](1)
    n, grads = groups[4], env["gathers"][5:]
    for c in range(0, C, n):
        work("work", 3, c, n)

    def shade(piece):
        if piece == 0:
            env["wide_feed"]()
            env["pass_on"](0)
        if piece == 1:
            env["heads_mix"]()
            env["wide_mix"]()
            env["pass_on"](1)
        if piece == 2 and K:
            for gather in grads:
                gather.stage(1)

    hops = [(c, t) for t in range(2, T) for c in range(C)]
    at_hop = [min(len(hops), share) for share in (C // 2, C, C + C // 2)]
    for i in range(len(hops) + 1):
        for piece in range(3):
            if at_hop[piece] == i:
                shade(piece)
        if i < len(hops):
            rs(*hops[i])
    for c in range(C):
        meets[3](c)
        if c == C // 2:
            for step in range(2, K + 1):
                for gather in grads:
                    gather.stage(step)
    for gather in grads:
        gather.finish()
    for c in range(C):
        env["rs_drain"](c)
        env["ag_drain"](buffers[2], c)
    env["ag_drain"](hidden, None)
    for which in range(2):
        env["pass_drain"](which)
    for gather in env["gathers"]:
        gather.drain()


def spread(mesh, body):
    placed = (
        P(("fsdp", "tp"), None),
        P(("fsdp", "tp"), None),
        P("fsdp", None),
        P("fsdp"),
        P(None, "fsdp", "tp"),
        P(None, "tp"),
        P("tp", "fsdp"),
        P(),
        P("fsdp", "tp"),
        P("tp"),
        P("tp", "fsdp"),
        P(),
        P(),
        P(),
        P(),
        P(None, None, None, "tp"),
        P(None, "tp", None),
        P(),
        P(),
        P(None, None, "tp"),
        P(None, "tp", None),
        P(),
    )
    return jax.shard_map(
        body,
        mesh=mesh,
        in_specs=placed,
        out_specs=(
            P(("fsdp", "tp"), None),
            P(("fsdp", "tp"), None),
            P(),
            P(None, None, None, "tp"),
            P(None, "tp", None),
            P(),
            P(),
            P(None, None, "tp"),
            P(None, "tp", None),
            P(),
        ),
        check_vma=False,
    )


def chunks_for(rows):
    return max(c for c in (1, 2, 4) if rows % (16 * c) == 0)


def place_kernel(layer_in, grad_in, feed_in, units_in, mix_in, heads_in, layer_out, grad_out, *refs):
    outs, tables = refs[:8], refs[8:16]
    feed_all, units_all, mix_all, heads_all, rows_a, rows_b, chosen, sems = refs[16:]
    F = feed_all.shape[0]
    sets = outs[2].shape[0]
    loads = [(heads_in, heads_all), (feed_in, feed_all), (units_in, units_all), (mix_in, mix_all)]
    loads += [(layer_in, rows_a), (grad_in, rows_b)]
    loads = [pltpu.make_async_copy(a, b, sems.at[k]) for k, (a, b) in enumerate(loads)]
    stores = list(zip(tables, outs)) + [(rows_a, layer_out), (rows_b, grad_out)]
    stores = [pltpu.make_async_copy(a, b, sems.at[6 + k]) for k, (a, b) in enumerate(stores)]
    for copy in loads:
        copy.start()
    order = lax.broadcasted_iota(jnp.int32, (32, 1), 0).astype(F32)
    q_in, q_out, o_in, o_out, u_in, u_out, d_in, d_out = range(8)
    loads[0].wait()
    for g in range(F):
        marks = heads_all[g, pl.ds(64, 32), pl.ds(0, 128)][:, :1].astype(F32)
        chosen[g] = jnp.clip(jnp.sum(marks * order).astype(jnp.int32), 0, sets - 1)

    def fill(which, rows_of):
        ref = tables[which]
        ref[...] = jnp.zeros_like(ref)

        @pl.loop(0, F)
        def _(g):
            rows_of(ref, g, chosen[g])

        stores[which].start()

    def whole(source, row):
        def add(ref, g, s):
            ref[s] += source[g, pl.ds(row, 16)].astype(F32)

        return add

    def trio(add_of):
        def add(ref, g, s):
            for j in range(3):
                add_of(16 * j)(ref.at[j], g, s)

        return add

    fill(q_out, trio(lambda row: whole(heads_all, row)))
    fill(o_in, whole(heads_all, 48))
    loads[1].wait()
    fill(u_in, whole(feed_all, 0))
    fill(d_out, whole(feed_all, 16))
    loads[2].wait()
    fill(u_out, whole(units_all, 0))
    fill(d_in, whole(units_all, 16))
    loads[3].wait()
    fill(o_out, whole(mix_all, 48))
    fill(q_in, trio(lambda row: whole(mix_all, row)))
    for copy in loads[4:]:
        copy.wait()
    for copy in stores[8:]:
        copy.start()
    for copy in stores:
        copy.wait()


def kernel_per_device(F, T):
    def per_device(
        hidden_in, cotangent, segment_ids, adapter_set, qkv_weight, qkv_bias, proj_weight, proj_bias,
        up_weight, up_bias, down_weight, down_bias, norm_gain, norm_bias, qkv_adapt_in, qkv_adapt_out,
        attn_adapt_in, attn_adapt_out, up_adapt_in, up_adapt_out, down_adapt_in, down_adapt_out,
    ):
        Q, D = hidden_in.shape
        H, FL = qkv_weight.shape[2], up_weight.shape[1]
        S, C, sets = Q * T, chunks_for(Q), qkv_adapt_in.shape[1]
        R, block = Q // C, D // F
        cfg = dict(F=F, T=T, S=S, D=D, H=H, FL=FL, C=C, lag=1, groups=(1, 1, 1, 1, 1), up_turn=T + 1)
        turn = lambda table: jnp.swapaxes(table, -1, -2)
        vmem, anywhere = pl.BlockSpec(memory_space=pltpu.VMEM), pl.BlockSpec(memory_space=pl.ANY)
        dma = pltpu.SemaphoreType.DMA
        bank = lambda *shape: pltpu.VMEM(shape, BF16)
        wide_bank = lambda *shape: pltpu.VMEM(shape, F32)
        scratch = (
            [bank(C, T, R, D), bank(3, F, block, H), bank(F, H, block), bank(F, block, FL), bank(F, FL, block)]
            + [bank(3, S, H), bank(H // HEAD, S, S), bank(S, H), bank(C, T, R, D), bank(S, FL), bank(S, FL)]
            + [bank(C, T, R, D), bank(C, T, R, D), bank(S, H), bank(3, S, H)]
            + [bank(C, T, R, D), bank(C, T, R, D), bank(C, T, R, D)]
            + [wide_bank(Q, D), wide_bank(Q, 128), wide_bank(Q, D)]
            + [bank(3, S, RANK), bank(S, RANK), bank(S, RANK), bank(S, RANK)] * 2
            + [wide_bank(1, S), wide_bank(S, 128), bank(H, S)]
            + [bank(6, RANK, D), bank(4, RANK, H), bank(2, RANK, FL)]
            + [bank(2, 6, RANK, D), bank(2, 4, RANK, H), bank(2, 2, RANK, FL)]
            + [bank(32, S), bank(T - 1, 32, S), bank(32, D)]
            + [bank(64, S), bank(T - 1, 64, S), bank(64, D)]
            + [bank(32, FL), bank(96, H)]
            + [dma((2, 8))] + [dma((2, T - 1))] * 2
            + [dma((9, 2, F)), dma((9, 2, F))]
            + [dma((C, T))] * 4
            + [dma((C + 1, T))] * 4
            + [dma((9,))]
        )
        flops = 2 * S * (4 * D * H + 2 * D * FL) * 2
        outs = pl.pallas_call(
            functools.partial(layer_kernel, cfg),
            out_shape=[
                jax.ShapeDtypeStruct((Q, D), F32),
                jax.ShapeDtypeStruct((Q, D), F32),
                jax.ShapeDtypeStruct((F, 32, D), BF16),
                jax.ShapeDtypeStruct((F, 32, FL), BF16),
                jax.ShapeDtypeStruct((F, 64, D), BF16),
                jax.ShapeDtypeStruct((F, 96, H), BF16),
            ],
            in_specs=[anywhere] + [vmem] * 3 + [anywhere] * 4 + [vmem] * 6 + [anywhere] * 8,
            out_specs=[vmem] * 2 + [anywhere] * 4,
            scratch_shapes=scratch,
            compiler_params=pltpu.CompilerParams(
                collective_id=0, has_side_effects=True, vmem_limit_bytes=62 * 1024 * 1024
            ),
            cost_estimate=pl.CostEstimate(flops=flops, bytes_accessed=30000000, transcendentals=0),
        )(
            hidden_in.reshape(C, R, D), cotangent, segment_ids, adapter_set[None, :],
            qkv_weight, proj_weight, up_weight, down_weight,
            proj_bias, down_bias, up_bias, qkv_bias, norm_gain, norm_bias,
            turn(qkv_adapt_in), qkv_adapt_out, turn(attn_adapt_in), attn_adapt_out,
            turn(up_adapt_in), up_adapt_out, turn(down_adapt_in), down_adapt_out,
        )
        shapes = [
            (3, sets, RANK, D), (3, sets, RANK, H), (sets, RANK, H), (sets, RANK, D),
            (sets, RANK, D), (sets, RANK, FL), (sets, RANK, FL), (sets, RANK, D),
        ]
        table = lambda *shape: jax.ShapeDtypeStruct(shape, F32)
        layer_out, grad_input, q_in, q_out, o_in, o_out, u_in, u_out, d_in, d_out = pl.pallas_call(
            place_kernel,
            out_shape=[table(Q, D), table(Q, D)] + [table(*shape) for shape in shapes],
            in_specs=[anywhere] * 6,
            out_specs=[anywhere] * 10,
            scratch_shapes=[wide_bank(*shape) for shape in shapes]
            + [bank(*out.shape) for out in outs[2:]]
            + [wide_bank(Q, D), wide_bank(Q, D), pltpu.SMEM((F,), jnp.int32), dma((16,))],
            compiler_params=pltpu.CompilerParams(vmem_limit_bytes=62 * 1024 * 1024),
        )(*outs)
        return (
            layer_out, grad_input, turn(q_in), q_out, turn(o_in), o_out, turn(u_in), u_out, turn(d_in), d_out,
        )

    return per_device


def solution(mesh):
    F, T = mesh.shape["fsdp"], mesh.shape["tp"]

    def whole(*args):
        width = args[0].shape[1]
        fits = F & (F - 1) == 0 and (width // F) % 128 == 0 and T > 1 and F > 1 and args[14].shape[1] <= 32 and width // T * args[2].shape[1] <= args[8].shape[1] // T * HEAD
        return spread(mesh, kernel_per_device(F, T) if fits else per_device)(*args)

    return whole
```

```python
import functools
import math

import jax
import jax.numpy as jnp
from jax import lax
from jax.experimental import pallas as pl
from jax.experimental.pallas import tpu as pltpu
from jax.sharding import PartitionSpec as P

HEAD = 128
RANK = 16
MESH = pl.DeviceIdType.MESH
F32 = jnp.float32
BF16 = jnp.bfloat16
ROOT = math.sqrt(2.0 / math.pi)


def layer_norm(field_in, gain_row, shift_row):
    centre = jnp.mean(field_in, axis=-1, keepdims=True)
    centred = field_in - centre
    spread = jnp.mean(centred * centred, axis=-1, keepdims=True)
    return centred * lax.rsqrt(spread + 1e-05) * gain_row + shift_row


def precise_dot(left, right):
    return jnp.dot(left, right, precision=lax.Precision.HIGHEST)


def mixed_dot(left, right):
    return jnp.dot(left, right, preferred_element_type=jnp.float32)


def choose_set(table, index, axis):
    return lax.dynamic_index_in_dim(table, index, axis, keepdims=False)


def place_set(grad, index, sets, axis):
    onehot = (jnp.arange(sets) == index).astype(jnp.float32)
    shape_list = [1] * (grad.ndim + 1)
    shape_list[axis] = sets
    return jnp.expand_dims(grad, axis) * onehot.reshape(shape_list)


def per_device(
    hidden_in,
    cotangent,
    segment_ids,
    adapter_set,
    qkv_weight,
    qkv_bias,
    proj_weight,
    proj_bias,
    up_weight,
    up_bias,
    down_weight,
    down_bias,
    norm_gain,
    norm_bias,
    qkv_adapt_in,
    qkv_adapt_out,
    attn_adapt_in,
    attn_adapt_out,
    up_adapt_in,
    up_adapt_out,
    down_adapt_in,
    down_adapt_out,
):
    width_local = qkv_weight.shape[2]
    heads_local = width_local // HEAD
    sets = qkv_adapt_in.shape[1]
    chosen = adapter_set[0]
    segments = segment_ids[0]
    seq_rows = segments.shape[0]
    block_rows = min(512, seq_rows)
    blocks = seq_rows // block_rows
    score_scale = 1.0 / math.sqrt(HEAD)
    gains = norm_gain.astype(jnp.float32)
    shifts = norm_bias.astype(jnp.float32)
    first_q = choose_set(qkv_adapt_in, chosen, 1)
    second_q = choose_set(qkv_adapt_out, chosen, 1)
    first_o = choose_set(attn_adapt_in, chosen, 0)
    second_o = choose_set(attn_adapt_out, chosen, 0)
    first_u = choose_set(up_adapt_in, chosen, 0)
    second_u = choose_set(up_adapt_out, chosen, 0)
    first_d = choose_set(down_adapt_in, chosen, 0)
    second_d = choose_set(down_adapt_out, chosen, 0)
    seq_hidden = lax.all_gather(hidden_in, "tp", axis=0, tiled=True)
    qkv_full, proj_full = (
        lax.all_gather(qkv_weight, "fsdp", axis=1, tiled=True),
        lax.all_gather(proj_weight, "fsdp", axis=1, tiled=True),
    )
    main_term = jnp.einsum("sd,jdc->jsc", seq_hidden, qkv_full, preferred_element_type=jnp.float32)
    low_in = jnp.einsum("sd,jdr->jsr", seq_hidden, first_q, preferred_element_type=jnp.float32)
    low_term = jnp.einsum(
        "jsr,jrc->jsc", low_in, second_q.astype(jnp.float32), precision=lax.Precision.HIGHEST
    )
    bias_rows = jnp.stack([qkv_bias[0], jnp.zeros_like(qkv_bias[0]), qkv_bias[1]]).astype(
        jnp.float32
    )[:, None, :]
    qkv_round = (main_term + low_term + bias_rows).astype(jnp.bfloat16)
    queries = qkv_round[0].reshape(seq_rows, heads_local, HEAD)
    keys = qkv_round[1].reshape(seq_rows, heads_local, HEAD)
    values = qkv_round[2].reshape(seq_rows, heads_local, HEAD)
    query_blocks = queries.reshape(blocks, block_rows, heads_local, HEAD)
    seg_blocks = segments.reshape(blocks, block_rows)

    def scores_of(query_rows, seg_rows):
        raw_scores = (
            jnp.einsum("bhe,she->hbs", query_rows, keys, preferred_element_type=jnp.float32)
            * score_scale
        )
        same_doc = (seg_rows[:, None] == segments[None, :])[None]
        return jnp.where(same_doc, raw_scores, -1e30)

    def forward_block(inputs):
        query_rows, seg_rows = inputs
        scores = scores_of(query_rows, seg_rows)
        row_top = jnp.max(scores, axis=-1, keepdims=True)
        weights = jnp.exp(scores - row_top)
        row_total = jnp.sum(weights, axis=-1, keepdims=True)
        attn_probs = (weights / row_total).astype(jnp.bfloat16)
        attn_mixed = jnp.einsum(
            "hbs,she->bhe", attn_probs, values, preferred_element_type=jnp.float32
        )
        return (attn_mixed, (row_top + jnp.log(row_total))[..., 0])

    attn_mixed, logsum = lax.map(forward_block, (query_blocks, seg_blocks))
    attended = attn_mixed.reshape(seq_rows, width_local).astype(jnp.bfloat16)
    low_attn = mixed_dot(attended, first_o)
    second_o_wide = second_o.astype(jnp.float32)
    row_part = attended
    low_part = low_attn
    attn_sum = lax.psum_scatter(
        mixed_dot(row_part, proj_full) + precise_dot(low_part, second_o_wide),
        "tp",
        scatter_dimension=0,
        tiled=True,
    )
    first_sum = hidden_in.astype(jnp.float32) + attn_sum + proj_bias.astype(jnp.float32)
    normed = layer_norm(first_sum, gains[0], shifts[0])
    normed_round = normed.astype(jnp.bfloat16)
    seq_normed = lax.all_gather(normed_round, "tp", axis=0, tiled=True)
    up_full, down_full = (
        lax.all_gather(up_weight, "fsdp", axis=0, tiled=True),
        lax.all_gather(down_weight, "fsdp", axis=1, tiled=True),
    )
    low_up = mixed_dot(seq_normed, first_u)
    pre_act = (
        mixed_dot(seq_normed, up_full)
        + precise_dot(low_up, second_u.astype(jnp.float32))
        + up_bias.astype(jnp.float32)
    )
    act_round = jax.nn.gelu(pre_act, approximate=True).astype(jnp.bfloat16)
    low_down = mixed_dot(act_round, first_d)
    second_d_wide = second_d.astype(jnp.float32)
    row_part = act_round
    low_part = low_down
    ffn_sum = lax.psum_scatter(
        mixed_dot(row_part, down_full) + precise_dot(low_part, second_d_wide),
        "tp",
        scatter_dimension=0,
        tiled=True,
    )
    second_sum = normed + ffn_sum + down_bias.astype(jnp.float32)
    layer_out = layer_norm(second_sum, gains[1], shifts[1])
    unused, norm_back = jax.vjp(
        lambda field_in: layer_norm(field_in, gains[1], shifts[1]), second_sum
    )
    grad_second = norm_back(cotangent.astype(jnp.float32))[0]
    grad_feed_round = grad_second.astype(jnp.bfloat16)
    seq_grad_feed = lax.all_gather(grad_feed_round, "tp", axis=0, tiled=True)
    up_back, down_back = (
        lax.all_gather(up_weight, "fsdp", axis=0, tiled=True),
        lax.all_gather(down_weight, "fsdp", axis=1, tiled=True),
    )
    grad_low_down = mixed_dot(seq_grad_feed, second_d.T)
    grad_act = jnp.einsum(
        "sd,fd->sf", seq_grad_feed, down_back, preferred_element_type=jnp.float32
    ) + precise_dot(grad_low_down, first_d.astype(jnp.float32).T)
    unused, gelu_back = jax.vjp(lambda field_in: jax.nn.gelu(field_in, approximate=True), pre_act)
    grad_pre_round = gelu_back(grad_act)[0].astype(jnp.bfloat16)
    grad_down_out_part = precise_dot(low_down.T, seq_grad_feed.astype(jnp.float32))
    grad_down_in_part = precise_dot(act_round.astype(jnp.float32).T, grad_low_down)
    grad_low_up = mixed_dot(grad_pre_round, second_u.T)
    grad_up_out_part = precise_dot(low_up.T, grad_pre_round.astype(jnp.float32))
    grad_up_in_part = precise_dot(seq_normed.astype(jnp.float32).T, grad_low_up)
    first_u_wide = first_u.astype(jnp.float32)
    row_part = grad_pre_round
    low_part = grad_low_up
    grad_normed = grad_second + lax.psum_scatter(
        jnp.einsum("sf,df->sd", row_part, up_back, preferred_element_type=jnp.float32)
        + precise_dot(low_part, first_u_wide.T),
        "tp",
        scatter_dimension=0,
        tiled=True,
    )
    unused, norm_front = jax.vjp(
        lambda field_in: layer_norm(field_in, gains[0], shifts[0]), first_sum
    )
    grad_first = norm_front(grad_normed)[0]
    grad_branch_round = grad_first.astype(jnp.bfloat16)
    seq_grad_branch = lax.all_gather(grad_branch_round, "tp", axis=0, tiled=True)
    qkv_back, proj_back = (
        lax.all_gather(qkv_weight, "fsdp", axis=1, tiled=True),
        lax.all_gather(proj_weight, "fsdp", axis=1, tiled=True),
    )
    grad_low_attn = mixed_dot(seq_grad_branch, second_o.T)
    grad_attended = jnp.einsum(
        "sd,cd->sc", seq_grad_branch, proj_back, preferred_element_type=jnp.float32
    ) + precise_dot(grad_low_attn, first_o.astype(jnp.float32).T)
    grad_attended_round = grad_attended.astype(jnp.bfloat16)
    grad_attn_out_part = precise_dot(low_attn.T, seq_grad_branch.astype(jnp.float32))
    grad_attn_in_part = precise_dot(attended.astype(jnp.float32).T, grad_low_attn)
    grad_blocks = grad_attended_round.reshape(blocks, block_rows, heads_local, HEAD)

    def backward_block(carry, inputs):
        grad_keys, grad_values = carry
        query_rows, seg_rows, lse_rows, grad_rows = inputs
        scores = scores_of(query_rows, seg_rows)
        attn_probs = jnp.exp(scores - lse_rows[..., None])
        grad_probs = jnp.einsum(
            "bhe,she->hbs", grad_rows, values, preferred_element_type=jnp.float32
        )
        centre = jnp.sum(grad_probs * attn_probs, axis=-1, keepdims=True)
        grad_scores = (attn_probs * (grad_probs - centre)).astype(jnp.bfloat16)
        grad_query = (
            jnp.einsum("hbs,she->bhe", grad_scores, keys, preferred_element_type=jnp.float32)
            * score_scale
        )
        grad_keys = (
            grad_keys
            + jnp.einsum(
                "hbs,bhe->she", grad_scores, query_rows, preferred_element_type=jnp.float32
            )
            * score_scale
        )
        grad_values = grad_values + jnp.einsum(
            "hbs,bhe->she",
            attn_probs.astype(jnp.bfloat16),
            grad_rows,
            preferred_element_type=jnp.float32,
        )
        return ((grad_keys, grad_values), grad_query)

    zero_state = jnp.zeros((seq_rows, heads_local, HEAD), jnp.float32)
    key_value_grads, grad_queries = lax.scan(
        backward_block, (zero_state, zero_state), (query_blocks, seg_blocks, logsum, grad_blocks)
    )
    grad_qkv_round = jnp.stack(
        [
            grad_queries.reshape(seq_rows, width_local),
            key_value_grads[0].reshape(seq_rows, width_local),
            key_value_grads[1].reshape(seq_rows, width_local),
        ]
    ).astype(jnp.bfloat16)
    grad_qkv_out_part = jnp.einsum(
        "jsr,jsc->jrc", low_in, grad_qkv_round.astype(jnp.float32), precision=lax.Precision.HIGHEST
    )
    grad_low_qkv = jnp.einsum(
        "jsc,jrc->jsr", grad_qkv_round, second_q, preferred_element_type=jnp.float32
    )
    grad_qkv_in_part = jnp.einsum(
        "sd,jsr->jdr", seq_hidden.astype(jnp.float32), grad_low_qkv, precision=lax.Precision.HIGHEST
    )
    first_q_wide = first_q.astype(jnp.float32)
    row_part = grad_qkv_round
    low_part = grad_low_qkv
    grad_input = grad_first + lax.psum_scatter(
        (
            jnp.einsum("jsc,jdc->sd", row_part, qkv_back, preferred_element_type=jnp.float32)
            + jnp.einsum("jsr,jdr->sd", low_part, first_q_wide, precision=lax.Precision.HIGHEST)
        ).astype(jnp.bfloat16),
        "tp",
        scatter_dimension=0,
        tiled=True,
    ).astype(jnp.float32)
    wide_grads = lax.psum(
        (
            place_set(grad_qkv_in_part, chosen, sets, 1),
            place_set(grad_attn_out_part, chosen, sets, 0),
            place_set(grad_up_in_part, chosen, sets, 0),
            place_set(grad_down_out_part, chosen, sets, 0),
        ),
        ("fsdp", "tp"),
    )
    split_grads = (
        lax.psum(place_set(grad_qkv_out_part, chosen, sets, 1).astype(jnp.bfloat16), "fsdp").astype(
            jnp.float32
        ),
        lax.psum(place_set(grad_attn_in_part, chosen, sets, 0).astype(jnp.bfloat16), "fsdp").astype(
            jnp.float32
        ),
        lax.psum(place_set(grad_up_out_part, chosen, sets, 0).astype(jnp.bfloat16), "fsdp").astype(
            jnp.float32
        ),
        lax.psum(place_set(grad_down_in_part, chosen, sets, 0).astype(jnp.bfloat16), "fsdp").astype(
            jnp.float32
        ),
    )
    return (
        layer_out,
        grad_input,
        wide_grads[0],
        split_grads[0],
        split_grads[1],
        wide_grads[1],
        wide_grads[2],
        split_grads[2],
        split_grads[3],
        wide_grads[3],
    )


def dot_nn(left, right):
    return jnp.dot(left, right, preferred_element_type=F32)


def dot_nt(left, right):
    return lax.dot_general(left, right, (((1,), (1,)), ((), ())), preferred_element_type=F32)


def flip(index, mask):
    out, bit = index, 1
    while bit <= mask:
        if mask & bit:
            out = out + bit - 2 * bit * lax.rem(lax.div(index, bit), 2)
        bit *= 2
    return out


def norm_parts(rows):
    centred = rows - jnp.mean(rows, axis=-1, keepdims=True)
    spread = jnp.mean(centred * centred, axis=-1, keepdims=True)
    rstd = lax.rsqrt(spread + 1e-05)
    return centred * rstd, rstd


def norm_pull(grad, unit, rstd):
    return rstd * (
        grad
        - jnp.mean(grad, axis=-1, keepdims=True)
        - unit * jnp.mean(grad * unit, axis=-1, keepdims=True)
    )


class Gather:
    def __init__(self, which, shard, whole, send, recv, fsdp, tp, count):
        self.which, self.shard, self.whole = which, shard, whole
        self.send, self.recv, self.fsdp, self.tp = send, recv, fsdp, tp
        bits = [1 << i for i in range(1, count.bit_length() - 1)]
        self.orders = [bits, bits[::-1]]
        self.steps = len(bits)
        self.held = [[0], [0]]
        self.sent = []
        self.count = count

    def copy(self, half, mask, bit):
        landed = mask ^ bit
        place = self.whole(flip(self.fsdp, mask), half)
        return pltpu.make_async_remote_copy(
            src_ref=self.shard(half) if mask == 0 else place,
            dst_ref=place,
            send_sem=self.send.at[self.which, half, landed],
            recv_sem=self.recv.at[self.which, half, landed],
            device_id=(flip(self.fsdp, bit), self.tp),
            device_id_type=MESH,
        )

    def launch(self, half, mask, bit):
        self.copy(half, mask, bit).start()
        self.sent.append((half, mask, bit))

    def await_block(self, half, mask, bit):
        place = self.whole(flip(self.fsdp, mask), half)
        pltpu.make_async_remote_copy(
            src_ref=place,
            dst_ref=place,
            send_sem=self.send.at[self.which, half, mask],
            recv_sem=self.recv.at[self.which, half, mask],
            device_id=(flip(self.fsdp, bit), self.tp),
            device_id_type=MESH,
        ).wait_recv()

    def stage(self, step):
        for half in range(2):
            fresh = [0]
            if step > 0:
                bit = self.orders[half][step - 1]
                fresh = [mask ^ bit for mask in self.held[half]]
                for mask in fresh:
                    self.await_block(half, mask, bit)
                self.held[half] = self.held[half] + fresh
            if step < self.steps:
                for mask in self.held[half]:
                    self.launch(half, mask, self.orders[half][step])
            for mask in fresh:
                self.launch(half, mask, 1)

    def finish(self):
        for half in range(2):
            for mask in self.held[half]:
                self.await_block(half, mask ^ 1, 1)

    def drain(self):
        for half, mask, bit in self.sent:
            self.copy(half, mask, bit).wait_send()


def layer_kernel(cfg, *refs):
    F, T, S, D, H, FL, C = (cfg[k] for k in ("F", "T", "S", "D", "H", "FL", "C"))
    Q, heads, block = S // T, H // HEAD, D // F
    R = Q // C
    M = T * R
    NT = math.gcd(FL, 512)
    (
        hidden_in, cotangent, segments, chosen, qkv_w, proj_w, up_w, down_w,
        proj_bias, down_bias, up_bias, qkv_bias, gains, shifts,
        q_in, q_out, o_in, o_out, u_in, u_out, d_in, d_out,
        layer_out, grad_input, feed_all, units_all, mix_all, heads_all,
        hidden, qkv_all, proj_all, up_all, down_all,
        qkv, probs, mixed, normed, act, slope, grad_feed, grad_branch, grad_mixed, grad_qkv,
        part, from_low, from_high, unit_one, rstd_one, grad_own,
        low_q, low_o, low_u, low_d, back_q, back_o, back_u, back_d,
        seg_row, seg_col, turned,
        wide_f, heads_f, units_f, wide_stage, heads_stage, units_stage,
        feed_part, feed_land, feed_full, mix_part, mix_land, mix_full, units_g, heads_g,
        stage_sem, deal_send, deal_recv,
        w_send, w_recv, up_send, up_recv, dn_send, dn_recv, g_up_send, g_up_recv, g_dn_send, g_dn_recv,
        own_sem,
    ) = refs
    grad_pre = slope
    f, z = lax.axis_index("fsdp"), lax.axis_index("tp")
    bits = [1 << i for i in range(F.bit_length() - 1)]

    barrier = pltpu.get_barrier_semaphore()
    for bit in bits:
        pl.semaphore_signal(barrier, inc=1, device_id=(flip(f, bit), z), device_id_type=MESH)

    turns = [lax.rem(z + k, T) for k in range(T)]
    for k in range(1, T):
        pl.semaphore_signal(barrier, inc=1, device_id=(f, turns[k]), device_id_type=MESH)
    pl.semaphore_wait(barrier, len(bits) + T - 1)

    rows_of = lambda total, half: pl.ds(half * (total // 2), total // 2)
    gathers = [
        Gather(0, lambda h: qkv_w.at[:, rows_of(block, h)], lambda g, h: qkv_all.at[:, g, rows_of(block, h)], w_send, w_recv, f, z, F),
        Gather(1, lambda h: proj_w.at[rows_of(H, h)], lambda g, h: proj_all.at[g, rows_of(H, h)], w_send, w_recv, f, z, F),
        Gather(2, lambda h: up_w.at[rows_of(block, h)], lambda g, h: up_all.at[g, rows_of(block, h)], w_send, w_recv, f, z, F),
    ]
    quarter = lambda part, h: pl.ds((2 * part + h) * (FL // 4), FL // 4)
    for part_of in range(2):
        shard = lambda h, p=part_of: down_w.at[quarter(p, h)]
        whole = lambda g, h, p=part_of: down_all.at[g, quarter(p, h)]
        gathers.append(Gather(3 + part_of, shard, whole, w_send, w_recv, f, z, F))
    pair = lambda ref, n: lambda h: ref.at[..., rows_of(n, h), :]
    pair_all = lambda ref, n: lambda g, h: ref.at[g, ..., rows_of(n, h), :]
    for k, (shard, whole) in enumerate(
        [(feed_full, feed_all), (units_g, units_all), (mix_full, mix_all), (heads_g, heads_all)]
    ):
        n = shard.shape[-2]
        gathers.append(Gather(5 + k, pair(shard, n), pair_all(whole, n), w_send, w_recv, f, z, F))
    K = gathers[0].steps
    own_copies = [
        pltpu.make_async_copy(hidden_in, hidden.at[:, z], own_sem.at[0]),
        pltpu.make_async_copy(qkv_w, qkv_all.at[:, f], own_sem.at[1]),
        pltpu.make_async_copy(proj_w, proj_all.at[f], own_sem.at[2]),
        pltpu.make_async_copy(up_w, up_all.at[f], own_sem.at[3]),
        pltpu.make_async_copy(down_w, down_all.at[f], own_sem.at[4]),
    ]
    own_grads = [
        pltpu.make_async_copy(feed_full, feed_all.at[f], own_sem.at[5]),
        pltpu.make_async_copy(units_g, units_all.at[f], own_sem.at[6]),
        pltpu.make_async_copy(mix_full, mix_all.at[f], own_sem.at[7]),
        pltpu.make_async_copy(heads_g, heads_all.at[f], own_sem.at[8]),
    ]

    def deal_copy(which, k):
        part_ref, land_ref = exchanges[which]
        return pltpu.make_async_remote_copy(
            src_ref=part_ref, dst_ref=land_ref.at[k - 1],
            send_sem=deal_send.at[which, k - 1], recv_sem=deal_recv.at[which, k - 1],
            device_id=(f, turns[k]), device_id_type=MESH,
        )

    exchanges = [(feed_part, feed_land), (mix_part, mix_land)]

    def deal(which):
        for k in range(1, T):
            deal_copy(which, k).start()

    def collect(which):
        part_ref, land_ref = exchanges[which]
        total = part_ref[...].astype(F32)
        for k in range(1, T):
            deal_copy(which, k).wait_recv()
            total += land_ref[k - 1].astype(F32)
        return total.astype(BF16)

    def pass_on(which):
        for k in (2 * which, 2 * which + 1):
            own_grads[k].start()
            gathers[5 + k].stage(0)

    def pass_drain(which):
        for k in range(1, T):
            deal_copy(which, k).wait_send()
        for k in (2 * which, 2 * which + 1):
            own_grads[k].wait()

    def line_copy(src, dst, send, recv, c, q, step):
        return pltpu.make_async_remote_copy(
            src_ref=src, dst_ref=dst, send_sem=send.at[c, q], recv_sem=recv.at[c, q],
            device_id=(f, z + step), device_id_type=MESH,
        )

    def rs_copy(c, q, step):
        landing, send, recv = (from_low, up_send, up_recv) if step > 0 else (from_high, dn_send, dn_recv)
        return line_copy(part.at[c, q], landing.at[c, q], send, recv, c, q, step)

    def rs_wait(c, q, step):
        landing, send, recv = (from_low, up_send, up_recv) if step > 0 else (from_high, dn_send, dn_recv)
        line_copy(landing.at[c, q], landing.at[c, q], send, recv, c, q, -step).wait_recv()

    def rs(c, t):
        def add(q, landing):
            part[c, q] = part[c, q] + landing[c, q]

        @pl.when(z <= t - 1)
        def _():
            q = T - t + z

            @pl.when(z > 0)
            def _():
                rs_wait(c, q, 1)
                add(q, from_low)

            rs_copy(c, q, 1).start()

        @pl.when(z >= T - t)
        def _():
            q = z - (T - t)

            @pl.when(z < T - 1)
            def _():
                rs_wait(c, q, -1)
                add(q, from_high)

            rs_copy(c, q, -1).start()

    def rs_end(c):
        @pl.when(z > 0)
        def _():
            rs_wait(c, z, 1)

        @pl.when(z < T - 1)
        def _():
            rs_wait(c, z, -1)

    def rs_sum(c, rows):
        terms = [ref[c, z, rows].astype(F32) for ref in (part, from_low, from_high)]
        return (terms[0] + terms[1]) + terms[2]

    def rs_drain(c):
        for q in range(T):
            if q > 0:

                @pl.when(z < q)
                def _(q=q):
                    rs_copy(c, q, 1).wait_send()

            if q < T - 1:

                @pl.when(z > q)
                def _(q=q):
                    rs_copy(c, q, -1).wait_send()

    def ag_copy(buffer, c, q, step):
        send, recv = (g_up_send, g_up_recv) if step > 0 else (g_dn_send, g_dn_recv)
        if c is None:
            return line_copy(buffer.at[:, q], buffer.at[:, q], send, recv, C, q, step)
        return line_copy(buffer.at[c, q], buffer.at[c, q], send, recv, c, q, step)

    def ag_wait(buffer, c, q, step):
        send, recv = (g_up_send, g_up_recv) if step > 0 else (g_dn_send, g_dn_recv)
        place = buffer.at[:, q] if c is None else buffer.at[c, q]
        line_copy(place, place, send, recv, C if c is None else c, q, -step).wait_recv()

    def ag(buffer, c, t):
        if t == 1:

            @pl.when(z < T - 1)
            def _():
                ag_copy(buffer, c, z, 1).start()

            @pl.when(z > 0)
            def _():
                ag_copy(buffer, c, z, -1).start()

            return

        @pl.when(z >= t - 1)
        def _():
            q = z - (t - 1)
            ag_wait(buffer, c, q, 1)

            @pl.when(z < T - 1)
            def _():
                ag_copy(buffer, c, q, 1).start()

        @pl.when(z <= T - t)
        def _():
            q = z + (t - 1)
            ag_wait(buffer, c, q, -1)

            @pl.when(z > 0)
            def _():
                ag_copy(buffer, c, q, -1).start()

    def ag_drain(buffer, c):
        for q in range(T):

            @pl.when((z >= q) & (z < T - 1))
            def _(q=q):
                ag_copy(buffer, c, q, 1).wait_send()

            @pl.when((z <= q) & (z > 0))
            def _(q=q):
                ag_copy(buffer, c, q, -1).wait_send()

    a_q = lambda j: wide_f.at[j]
    b_o, a_u, b_d = wide_f.at[3], wide_f.at[4], wide_f.at[5]
    b_q = lambda j: heads_f.at[j]
    a_o = heads_f.at[3]
    b_u, a_d = units_f.at[0], units_f.at[1]
    line = lambda ref, k: ref[pl.ds(k, 1)].astype(F32)
    flat = lambda ref: ref[...].reshape(1, ref.shape[0]).astype(F32)
    sets = q_in.shape[1]
    pick = (lax.broadcasted_iota(jnp.int32, (sets, 128), 0) == chosen[...]).astype(F32)

    def stage_copies(s):
        slot = s % 2
        pairs = [
            (q_in.at[:, s], wide_stage.at[slot, pl.ds(0, 3)]),
            (o_out.at[s], wide_stage.at[slot, 3]),
            (u_in.at[s], wide_stage.at[slot, 4]),
            (d_out.at[s], wide_stage.at[slot, 5]),
            (q_out.at[:, s], heads_stage.at[slot, pl.ds(0, 3)]),
            (o_in.at[s], heads_stage.at[slot, 3]),
            (u_out.at[s], units_stage.at[slot, 0]),
            (d_in.at[s], units_stage.at[slot, 1]),
        ]
        return [
            pltpu.make_async_copy(src, dst, stage_sem.at[slot, k])
            for k, (src, dst) in enumerate(pairs)
        ]

    def choose(s):
        for copy in stage_copies(s):
            copy.wait()
        weight = pick[s : s + 1, :1].astype(BF16)
        for stage, held in ((wide_stage, wide_f), (heads_stage, heads_f), (units_stage, units_f)):
            for k in range(held.shape[0]):
                term = stage[s % 2, k] * weight
                held[k] = term if s == 0 else held[k] + term
        if s + 2 < sets:
            for copy in stage_copies(s + 2):
                copy.start()

    def chunk(buffer, c, n, cols=slice(None)):
        rows = buffer[c : c + n, :, :, cols]
        return rows.reshape(n * M, rows.shape[-1])

    def cols_of(g, size):
        return pl.ds(pl.multiple_of(g * size, size), size)

    def project():
        width = math.gcd(H, 256)
        for j in range(3):
            low_j = dot_nt(hidden[...].reshape(S, D), a_q(j)[...]).astype(BF16)
            low_q[j] = low_j

            @pl.loop(0, H // width)
            def _(n, j=j, low_j=low_j):
                cols = cols_of(n, width)
                rows = dot_nn(hidden[...].reshape(S, D), qkv_all[j, :, :, cols].reshape(D, width))
                rows += dot_nn(low_j, b_q(j)[:, cols])
                if j != 1:
                    rows += qkv_bias[pl.ds(j // 2, 1), cols].astype(F32)
                qkv[j, :, cols] = rows.astype(BF16)

    scale = 1.0 / math.sqrt(HEAD)

    def mark_segments():
        row = segments[...].astype(F32)
        pieces = [row[:, q * Q + c * R : q * Q + c * R + R] for c in range(C) for q in range(T)]
        row = jnp.concatenate(pieces, axis=1)
        seg_row[...] = row
        seg_col[...] = jnp.broadcast_to(row, (128, S)).T

    def turn_heads(j):
        @pl.loop(0, heads)
        def _(h):
            turned[cols_of(h, HEAD)] = qkv[j, :, cols_of(h, HEAD)].T

    def attend(c):
        rows = pl.ds(c * M, M)

        @pl.loop(0, heads)
        def _(h):
            cols = cols_of(h, HEAD)
            scores = dot_nt(qkv[1, :, cols], qkv[0, rows, cols]) * scale
            scores = jnp.where(seg_col[:, :1] == seg_row[:, rows], scores, -1e30)
            weights = jnp.exp(scores - jnp.max(scores, axis=0, keepdims=True))
            low = (weights * (1.0 / jnp.sum(weights, axis=0, keepdims=True))).astype(BF16)
            probs[h, :, rows] = low
            mixed[rows, cols] = dot_nn(turned[cols], low).T.astype(BF16)

    def attend_back(c):
        rows = pl.ds(c * M, M)

        @pl.loop(0, heads)
        def _(h):
            cols = cols_of(h, HEAD)
            weights = probs[h, :, rows].astype(F32)
            grad = dot_nt(qkv[2, :, cols], grad_mixed[rows, cols])
            centre = jnp.sum(grad * weights, axis=0, keepdims=True)
            low = (weights * (grad - centre)).astype(BF16)
            grad_scores[:, pl.ds(pl.multiple_of(h * S + c * M, M), M)] = low
            grad_qkv[0, rows, cols] = (dot_nn(turned[cols], low).T * scale).astype(BF16)

    def attend_sums():
        @pl.loop(0, heads)
        def _(h):
            cols = cols_of(h, HEAD)
            low = grad_scores[:, cols_of(h, S)]
            grad_qkv[1, :, cols] = (dot_nn(low, qkv[0, :, cols]) * scale).astype(BF16)
            grad_qkv[2, :, cols] = dot_nn(probs[h], grad_mixed[:, cols]).astype(BF16)

    grad_scores = slope

    def span(c, n):
        return pl.ds(c * M, n * M)

    def put_part(c, n, cols, rows):
        part[c : c + n, :, :, cols] = rows.astype(BF16).reshape(n, T, R, rows.shape[-1])

    group = math.gcd(F, 2)

    def by_blocks(body):
        @pl.loop(0, F // group)
        def _(turn):
            for k in range(group):
                g = turn * group + k
                body(g, cols_of(g, block))

    def mix_out(c, n):
        low = dot_nt(mixed[span(c, n)], a_o[...]).astype(BF16)
        low_o[span(c, n)] = low

        @by_blocks
        def _(g, cols):
            put_part(c, n, cols, dot_nn(mixed[span(c, n)], proj_all[g]) + dot_nn(low, b_o[:, cols]))

    def feed_up(c, n):
        low = dot_nt(chunk(normed, c, n), a_u[...]).astype(BF16)
        low_u[span(c, n)] = low

        @pl.loop(0, FL // NT)
        def _(turn):
            cols = cols_of(turn, NT)
            pre = dot_nn(chunk(normed, c, n), up_all[:, :, cols].reshape(D, NT))
            pre += dot_nn(low, b_u[:, cols]) + up_bias[cols].reshape(1, NT).astype(F32)
            square = pre * pre
            bend = jnp.tanh(ROOT * (pre + 0.044715 * square * pre))
            half = 0.5 * (1.0 + bend)
            act[span(c, n), cols] = (pre * half).astype(BF16)
            rise = half + 0.5 * pre * (1.0 - bend * bend) * (ROOT * (1.0 + 3 * 0.044715 * square))
            slope[span(c, n), cols] = rise.astype(BF16)

    def feed_down(c, n):
        low = dot_nt(act[span(c, n)], a_d[...]).astype(BF16)
        low_d[span(c, n)] = low

        @by_blocks
        def _(g, cols):
            put_part(c, n, cols, dot_nn(act[span(c, n)], down_all[g]) + dot_nn(low, b_d[:, cols]))

    def back_down(c, n):
        low = dot_nt(chunk(grad_feed, c, n), b_d[...]).astype(BF16)
        back_d[span(c, n)] = low

        @pl.loop(0, FL // NT)
        def _(turn):
            cols = cols_of(turn, NT)
            total = dot_nn(low, a_d[:, cols])
            for g in range(F):
                total += dot_nt(chunk(grad_feed, c, n, pl.ds(g * block, block)), down_all[g, cols])
            grad_pre[span(c, n), cols] = (total * slope[span(c, n), cols].astype(F32)).astype(BF16)

    def back_up(c, n):
        low = dot_nt(grad_pre[span(c, n)], b_u[...]).astype(BF16)
        back_u[span(c, n)] = low

        @by_blocks
        def _(g, cols):
            put_part(c, n, cols, dot_nt(grad_pre[span(c, n)], up_all[g]) + dot_nn(low, a_u[:, cols]))

    def back_mix(c, n):
        low = dot_nt(chunk(grad_branch, c, n), b_o[...]).astype(BF16)
        back_o[span(c, n)] = low
        total = dot_nn(low, a_o[...])
        for g in range(F):
            total += dot_nt(chunk(grad_branch, c, n, pl.ds(g * block, block)), proj_all[g])
        grad_mixed[span(c, n)] = total.astype(BF16)

    def back_project(c, n):
        lows = [back_q[j, span(c, n)] for j in range(3)]

        @by_blocks
        def _(g, cols):
            total = dot_nn(lows[0], a_q(0)[:, cols])
            for j in range(3):
                if j:
                    total += dot_nn(lows[j], a_q(j)[:, cols])
                total += dot_nt(grad_qkv[j, span(c, n)], qkv_all[j, g])
            put_part(c, n, cols, total)

    def by_rows(body):
        def all_rows(c):
            rs_end(c)

            @pl.loop(0, R // 16)
            def _(k):
                body(c, cols_of(k, 16), pl.ds(pl.multiple_of(c * R + k * 16, 16), 16))

        return all_rows

    @by_rows
    def meet_one(c, rows, own):
        total = rs_sum(c, rows) + hidden[c, z, rows].astype(F32) + flat(proj_bias)
        unit, rstd = norm_parts(total)
        unit_one[own] = unit
        rstd_one[own] = jnp.broadcast_to(rstd, (16, 128))
        normed[c, z, rows] = (unit * line(gains, 0) + line(shifts, 0)).astype(BF16)

    @by_rows
    def meet_two(c, rows, own):
        total = rs_sum(c, rows) + unit_one[own] * line(gains, 0) + line(shifts, 0) + flat(down_bias)
        unit, rstd = norm_parts(total)
        layer_out[own] = unit * line(gains, 1) + line(shifts, 1)
        grad = norm_pull(cotangent[own].astype(F32) * line(gains, 1), unit, rstd)
        grad_own[own] = grad
        grad_feed[c, z, rows] = grad.astype(BF16)

    @by_rows
    def meet_three(c, rows, own):
        grad = (grad_own[own] + rs_sum(c, rows)) * line(gains, 0)
        grad = norm_pull(grad, unit_one[own], rstd_one[own][:, :1])
        grad_own[own] = grad
        grad_branch[c, z, rows] = grad.astype(BF16)

    @by_rows
    def meet_four(c, rows, own):
        grad_input[own] = grad_own[own] + rs_sum(c, rows)

    def turn_rows(low):
        return low.astype(F32).T.astype(BF16)

    def factor(low, right):
        return dot_nn(turn_rows(low[...]), right).astype(BF16)

    def by_columns(rows, right, place, row):
        count = rows.shape[0]

        @pl.loop(0, T)
        def _(q):
            cols = cols_of(q, H)
            place[pl.ds(row, count), cols] = dot_nn(rows, right[:, :, :, cols].reshape(S, H)).astype(BF16)

    def rows_feed():
        feed_part[pl.ds(0, 16)] = turn_rows(back_u[...])
        feed_part[pl.ds(16, 16)] = turn_rows(low_d[...])

    def units_feed():
        units_g[pl.ds(0, 16)] = factor(low_u, grad_pre[...])
        units_g[pl.ds(16, 16)] = factor(back_d, act[...])

    def wide_feed():
        rows = collect(0)
        by_columns(rows[:16], normed, feed_full, 0)
        by_columns(rows[16:], grad_feed, feed_full, 16)

    def rows_mix():
        for j in range(3):
            low = dot_nt(grad_qkv[j], b_q(j)[...]).astype(BF16)
            back_q[j] = low
            mix_part[pl.ds(16 * j, 16)] = turn_rows(low)
        mix_part[pl.ds(48, 16)] = turn_rows(low_o[...])

    def heads_mix():
        heads_g[pl.ds(48, 16)] = factor(back_o, mixed[...])
        for j in range(3):
            heads_g[pl.ds(16 * j, 16)] = factor(low_q.at[j], grad_qkv[j])
        marks = jnp.concatenate([pick[:, :1], jnp.zeros((32 - sets, 1), F32)])
        heads_g[pl.ds(64, 32)] = jnp.broadcast_to(marks, (32, H)).astype(BF16)

    def wide_mix():
        rows = collect(1)
        by_columns(rows[:48], hidden, mix_full, 0)
        by_columns(rows[48:], grad_branch, mix_full, 48)

    from_low[:, 0] = jnp.zeros((C, R, D), BF16)
    from_high[:, T - 1] = jnp.zeros((C, R, D), BF16)
    qkv_g = gathers[0]
    def own_hidden(step):
        return line_copy(hidden_in, hidden.at[:, z], g_up_send if step > 0 else g_dn_send, g_up_recv if step > 0 else g_dn_recv, C, z, step)

    @pl.when(z < T - 1)
    def _():
        own_hidden(1).start()

    @pl.when(z > 0)
    def _():
        own_hidden(-1).start()

    qkv_g.stage(0)
    for copy in own_copies + stage_copies(0) + stage_copies(1):
        copy.start()
    schedule(cfg, dict(locals()))


def schedule(cfg, env):
    T, C, K = cfg["T"], cfg["C"], env["K"]
    rs, ag, hidden = env["rs"], env["ag"], env["hidden"]
    qkv_g, proj_g, up_g, down_g, rest_g = env["gathers"][:5]
    env["mark_segments"]()
    for s in range(2):
        env["choose"](s)
    for step in range(1, K + 1):
        qkv_g.stage(step)
        if step == 1:
            proj_g.stage(0)
            ag(hidden, None, 2)
            for s in range(2, 5):
                env["choose"](s)
    if K == 0:
        proj_g.stage(0)
    if K >= 1:
        proj_g.stage(1)
    up_g.stage(0)
    if K < 1:
        ag(hidden, None, 2)
        for s in range(2, 5):
            env["choose"](s)
    for s in range(5, env["sets"]):
        env["choose"](s)
    for t in range(3, T + 1):
        ag(hidden, None, t)
    for step in range(2, K + 1):
        proj_g.stage(step)
    down_g.stage(0)
    rest_g.stage(0)
    qkv_g.finish()
    for copy in env["own_copies"]:
        copy.wait()
    env["project"]()
    env["turn_heads"](2)
    if K:
        up_g.stage(1)
    proj_g.finish()
    buffers = [env["normed"], env["grad_feed"], env["grad_branch"]]
    meets = [env["meet_one"], env["meet_two"], env["meet_three"], env["meet_four"]]

    def start_sum(chunks):
        for c in chunks:
            rs(c, 1)

    def work(kind, k, first, n):
        group = range(first, first + n)
        if kind == "mix" or k in (1, 2):
            for c in group:
                ag(buffers[k - 1], c, T)
        if kind == "mix":
            env["back_mix"](first, n)
            for c in group:
                env["attend_back"](c)
            return
        if k > 0:
            for c in group:
                env["rs_drain"](c)
        if k == 0:
            for c in group:
                env["attend"](c)
            if first + n == C:
                env["turn_heads"](1)
            env["mix_out"](first, n)
        if k == 1:
            if first == 0:
                up_g.finish()
            env["feed_up"](first, n)
            if first == 0:
                for gather in (down_g, rest_g):
                    for step in range(2, K + 1):
                        gather.stage(step)
                down_g.finish()
                rest_g.finish()
            env["feed_down"](first, n)
        if k == 2:
            env["back_down"](first, n)
            env["back_up"](first, n)
        if k == 3:
            env["back_project"](first, n)
        start_sum(group)
        if k == 2 and first + n == C:
            env["rows_feed"]()
            env["deal"](0)
            env["units_feed"]()

    def meet(k, c):
        meets[k](c)
        if k > 0:
            env["ag_drain"](buffers[k - 1], c)
        ag(buffers[k], c, 1)

    steps = []
    for k in range(3):
        steps += [("work", k, 0)] + [("rs", k, t) for t in range(2, T)] + [("meet", k, 0)]
        steps += [("ag", k, t) for t in range(2, T)]
    steps.append(("mix", 3, 0))
    groups, at, came, turn = cfg["groups"], [0] * C, {}, 0
    while min(at) < len(steps):
        if turn == 1 and K:
            down_g.stage(1)
            rest_g.stage(1)
        if turn == cfg["up_turn"]:
            for step in range(2, K + 1):
                up_g.stage(step)
        for c in range(C):
            if turn < cfg["lag"] * c or at[c] == len(steps):
                continue
            kind, k, t = steps[at[c]]
            if kind in ("work", "mix"):
                n = groups[k]
                first = c // n * n
                came.setdefault((kind, k, first), set()).add(c)
                if len(came[kind, k, first]) < n:
                    continue
                work(kind, k, first, n)
                for member in range(first, first + n):
                    at[member] += 1
                continue
            if kind == "rs":
                rs(c, t)
            if kind == "meet":
                meet(k, c)
            if kind == "ag":
                ag(buffers[k], c, t)
            at[c] += 1
        turn += 1
    env["attend_sums"]()
    env["rows_mix"]()
    env["deal"](1)
    n, grads = groups[4], env["gathers"][5:]
    for c in range(0, C, n):
        work("work", 3, c, n)

    def shade(piece):
        if piece == 0:
            env["wide_feed"]()
            env["pass_on"](0)
        if piece == 1:
            env["heads_mix"]()
            env["wide_mix"]()
            env["pass_on"](1)
        if piece == 2 and K:
            for gather in grads:
                gather.stage(1)

    hops = [(c, t) for t in range(2, T) for c in range(C)]
    at_hop = [min(len(hops), share) for share in (C // 2, C, C + C // 2)]
    for i in range(len(hops) + 1):
        for piece in range(3):
            if at_hop[piece] == i:
                shade(piece)
        if i < len(hops):
            rs(*hops[i])
    for c in range(C):
        meets[3](c)
        if c == C // 2:
            for step in range(2, K + 1):
                for gather in grads:
                    gather.stage(step)
    for gather in grads:
        gather.finish()
    for c in range(C):
        env["rs_drain"](c)
        env["ag_drain"](buffers[2], c)
    env["ag_drain"](hidden, None)
    for which in range(2):
        env["pass_drain"](which)
    for gather in env["gathers"]:
        gather.drain()


def spread(mesh, body):
    placed = (
        P(("fsdp", "tp"), None),
        P(("fsdp", "tp"), None),
        P("fsdp", None),
        P("fsdp"),
        P(None, "fsdp", "tp"),
        P(None, "tp"),
        P("tp", "fsdp"),
        P(),
        P("fsdp", "tp"),
        P("tp"),
        P("tp", "fsdp"),
        P(),
        P(),
        P(),
        P(),
        P(None, None, None, "tp"),
        P(None, "tp", None),
        P(),
        P(),
        P(None, None, "tp"),
        P(None, "tp", None),
        P(),
    )
    return jax.shard_map(
        body,
        mesh=mesh,
        in_specs=placed,
        out_specs=(
            P(("fsdp", "tp"), None),
            P(("fsdp", "tp"), None),
            P(),
            P(None, None, None, "tp"),
            P(None, "tp", None),
            P(),
            P(),
            P(None, None, "tp"),
            P(None, "tp", None),
            P(),
        ),
        check_vma=False,
    )


def chunks_for(rows):
    return max(c for c in (1, 2, 4) if rows % (16 * c) == 0)


def place_kernel(layer_in, grad_in, feed_in, units_in, mix_in, heads_in, layer_out, grad_out, *refs):
    outs, tables = refs[:8], refs[8:16]
    feed_all, units_all, mix_all, heads_all, rows_a, rows_b, chosen, sems = refs[16:]
    F = feed_all.shape[0]
    sets = outs[2].shape[0]
    loads = [(heads_in, heads_all), (feed_in, feed_all), (units_in, units_all), (mix_in, mix_all)]
    loads += [(layer_in, rows_a), (grad_in, rows_b)]
    loads = [pltpu.make_async_copy(a, b, sems.at[k]) for k, (a, b) in enumerate(loads)]
    stores = list(zip(tables, outs)) + [(rows_a, layer_out), (rows_b, grad_out)]
    stores = [pltpu.make_async_copy(a, b, sems.at[6 + k]) for k, (a, b) in enumerate(stores)]
    for copy in loads:
        copy.start()
    order = lax.broadcasted_iota(jnp.int32, (32, 1), 0).astype(F32)
    q_in, q_out, o_in, o_out, u_in, u_out, d_in, d_out = range(8)
    loads[0].wait()
    for g in range(F):
        marks = heads_all[g, pl.ds(64, 32), pl.ds(0, 128)][:, :1].astype(F32)
        chosen[g] = jnp.clip(jnp.sum(marks * order).astype(jnp.int32), 0, sets - 1)

    def fill(which, rows_of):
        ref = tables[which]
        ref[...] = jnp.zeros_like(ref)

        @pl.loop(0, F)
        def _(g):
            rows_of(ref, g, chosen[g])

        stores[which].start()

    def whole(source, row):
        def add(ref, g, s):
            ref[s] += source[g, pl.ds(row, 16)].astype(F32)

        return add

    def trio(add_of):
        def add(ref, g, s):
            for j in range(3):
                add_of(16 * j)(ref.at[j], g, s)

        return add

    fill(q_out, trio(lambda row: whole(heads_all, row)))
    fill(o_in, whole(heads_all, 48))
    loads[1].wait()
    fill(u_in, whole(feed_all, 0))
    fill(d_out, whole(feed_all, 16))
    loads[2].wait()
    fill(u_out, whole(units_all, 0))
    fill(d_in, whole(units_all, 16))
    loads[3].wait()
    fill(o_out, whole(mix_all, 48))
    fill(q_in, trio(lambda row: whole(mix_all, row)))
    for copy in loads[4:]:
        copy.wait()
    for copy in stores[8:]:
        copy.start()
    for copy in stores:
        copy.wait()


def kernel_per_device(F, T):
    def per_device(
        hidden_in, cotangent, segment_ids, adapter_set, qkv_weight, qkv_bias, proj_weight, proj_bias,
        up_weight, up_bias, down_weight, down_bias, norm_gain, norm_bias, qkv_adapt_in, qkv_adapt_out,
        attn_adapt_in, attn_adapt_out, up_adapt_in, up_adapt_out, down_adapt_in, down_adapt_out,
    ):
        Q, D = hidden_in.shape
        H, FL = qkv_weight.shape[2], up_weight.shape[1]
        S, C, sets = Q * T, chunks_for(Q), qkv_adapt_in.shape[1]
        R, block = Q // C, D // F
        cfg = dict(F=F, T=T, S=S, D=D, H=H, FL=FL, C=C, lag=1, groups=(1, 1, 1, 1, 1), up_turn=T + 1)
        turn = lambda table: jnp.swapaxes(table, -1, -2)
        vmem, anywhere = pl.BlockSpec(memory_space=pltpu.VMEM), pl.BlockSpec(memory_space=pl.ANY)
        dma = pltpu.SemaphoreType.DMA
        bank = lambda *shape: pltpu.VMEM(shape, BF16)
        wide_bank = lambda *shape: pltpu.VMEM(shape, F32)
        scratch = (
            [bank(C, T, R, D), bank(3, F, block, H), bank(F, H, block), bank(F, block, FL), bank(F, FL, block)]
            + [bank(3, S, H), bank(H // HEAD, S, S), bank(S, H), bank(C, T, R, D), bank(S, FL), bank(S, FL)]
            + [bank(C, T, R, D), bank(C, T, R, D), bank(S, H), bank(3, S, H)]
            + [bank(C, T, R, D), bank(C, T, R, D), bank(C, T, R, D)]
            + [wide_bank(Q, D), wide_bank(Q, 128), wide_bank(Q, D)]
            + [bank(3, S, RANK), bank(S, RANK), bank(S, RANK), bank(S, RANK)] * 2
            + [wide_bank(1, S), wide_bank(S, 128), bank(H, S)]
            + [bank(6, RANK, D), bank(4, RANK, H), bank(2, RANK, FL)]
            + [bank(2, 6, RANK, D), bank(2, 4, RANK, H), bank(2, 2, RANK, FL)]
            + [bank(32, S), bank(T - 1, 32, S), bank(32, D)]
            + [bank(64, S), bank(T - 1, 64, S), bank(64, D)]
            + [bank(32, FL), bank(96, H)]
            + [dma((2, 8))] + [dma((2, T - 1))] * 2
            + [dma((9, 2, F)), dma((9, 2, F))]
            + [dma((C, T))] * 4
            + [dma((C + 1, T))] * 4
            + [dma((9,))]
        )
        flops = 2 * S * (4 * D * H + 2 * D * FL) * 2
        outs = pl.pallas_call(
            functools.partial(layer_kernel, cfg),
            out_shape=[
                jax.ShapeDtypeStruct((Q, D), F32),
                jax.ShapeDtypeStruct((Q, D), F32),
                jax.ShapeDtypeStruct((F, 32, D), BF16),
                jax.ShapeDtypeStruct((F, 32, FL), BF16),
                jax.ShapeDtypeStruct((F, 64, D), BF16),
                jax.ShapeDtypeStruct((F, 96, H), BF16),
            ],
            in_specs=[anywhere] + [vmem] * 3 + [anywhere] * 4 + [vmem] * 6 + [anywhere] * 8,
            out_specs=[vmem] * 2 + [anywhere] * 4,
            scratch_shapes=scratch,
            compiler_params=pltpu.CompilerParams(
                collective_id=0, has_side_effects=True, vmem_limit_bytes=62 * 1024 * 1024
            ),
            cost_estimate=pl.CostEstimate(flops=flops, bytes_accessed=30000000, transcendentals=0),
        )(
            hidden_in.reshape(C, R, D), cotangent, segment_ids, adapter_set[None, :],
            qkv_weight, proj_weight, up_weight, down_weight,
            proj_bias, down_bias, up_bias, qkv_bias, norm_gain, norm_bias,
            turn(qkv_adapt_in), qkv_adapt_out, turn(attn_adapt_in), attn_adapt_out,
            turn(up_adapt_in), up_adapt_out, turn(down_adapt_in), down_adapt_out,
        )
        shapes = [
            (3, sets, RANK, D), (3, sets, RANK, H), (sets, RANK, H), (sets, RANK, D),
            (sets, RANK, D), (sets, RANK, FL), (sets, RANK, FL), (sets, RANK, D),
        ]
        table = lambda *shape: jax.ShapeDtypeStruct(shape, F32)
        layer_out, grad_input, q_in, q_out, o_in, o_out, u_in, u_out, d_in, d_out = pl.pallas_call(
            place_kernel,
            out_shape=[table(Q, D), table(Q, D)] + [table(*shape) for shape in shapes],
            in_specs=[anywhere] * 6,
            out_specs=[anywhere] * 10,
            scratch_shapes=[wide_bank(*shape) for shape in shapes]
            + [bank(*out.shape) for out in outs[2:]]
            + [wide_bank(Q, D), wide_bank(Q, D), pltpu.SMEM((F,), jnp.int32), dma((16,))],
            compiler_params=pltpu.CompilerParams(vmem_limit_bytes=62 * 1024 * 1024),
        )(*outs)
        return (
            layer_out, grad_input, turn(q_in), q_out, turn(o_in), o_out, turn(u_in), u_out, turn(d_in), d_out,
        )

    return per_device


def solution(mesh):
    F, T = mesh.shape["fsdp"], mesh.shape["tp"]

    def whole(*args):
        width = args[0].shape[1]
        fits = F & (F - 1) == 0 and (width // F) % 128 == 0 and T > 1 and F > 1 and args[14].shape[1] <= 32 and width // T * args[2].shape[1] <= args[8].shape[1] // T * HEAD
        return spread(mesh, kernel_per_device(F, T) if fits else per_device)(*args)

    return whole
```

```python
import functools
import math

import jax
import jax.numpy as jnp
from jax import lax
from jax.experimental import pallas as pl
from jax.experimental.pallas import tpu as pltpu
from jax.sharding import PartitionSpec as P

HEAD = 128
RANK = 16
MESH = pl.DeviceIdType.MESH
F32 = jnp.float32
BF16 = jnp.bfloat16
ROOT = math.sqrt(2.0 / math.pi)


def layer_norm(field_in, gain_row, shift_row):
    centre = jnp.mean(field_in, axis=-1, keepdims=True)
    centred = field_in - centre
    spread = jnp.mean(centred * centred, axis=-1, keepdims=True)
    return centred * lax.rsqrt(spread + 1e-05) * gain_row + shift_row


def precise_dot(left, right):
    return jnp.dot(left, right, precision=lax.Precision.HIGHEST)


def mixed_dot(left, right):
    return jnp.dot(left, right, preferred_element_type=jnp.float32)


def choose_set(table, index, axis):
    return lax.dynamic_index_in_dim(table, index, axis, keepdims=False)


def place_set(grad, index, sets, axis):
    onehot = (jnp.arange(sets) == index).astype(jnp.float32)
    shape_list = [1] * (grad.ndim + 1)
    shape_list[axis] = sets
    return jnp.expand_dims(grad, axis) * onehot.reshape(shape_list)


def per_device(
    hidden_in,
    cotangent,
    segment_ids,
    adapter_set,
    qkv_weight,
    qkv_bias,
    proj_weight,
    proj_bias,
    up_weight,
    up_bias,
    down_weight,
    down_bias,
    norm_gain,
    norm_bias,
    qkv_adapt_in,
    qkv_adapt_out,
    attn_adapt_in,
    attn_adapt_out,
    up_adapt_in,
    up_adapt_out,
    down_adapt_in,
    down_adapt_out,
):
    width_local = qkv_weight.shape[2]
    heads_local = width_local // HEAD
    sets = qkv_adapt_in.shape[1]
    chosen = adapter_set[0]
    segments = segment_ids[0]
    seq_rows = segments.shape[0]
    block_rows = min(512, seq_rows)
    blocks = seq_rows // block_rows
    score_scale = 1.0 / math.sqrt(HEAD)
    gains = norm_gain.astype(jnp.float32)
    shifts = norm_bias.astype(jnp.float32)
    first_q = choose_set(qkv_adapt_in, chosen, 1)
    second_q = choose_set(qkv_adapt_out, chosen, 1)
    first_o = choose_set(attn_adapt_in, chosen, 0)
    second_o = choose_set(attn_adapt_out, chosen, 0)
    first_u = choose_set(up_adapt_in, chosen, 0)
    second_u = choose_set(up_adapt_out, chosen, 0)
    first_d = choose_set(down_adapt_in, chosen, 0)
    second_d = choose_set(down_adapt_out, chosen, 0)
    seq_hidden = lax.all_gather(hidden_in, "tp", axis=0, tiled=True)
    qkv_full, proj_full = (
        lax.all_gather(qkv_weight, "fsdp", axis=1, tiled=True),
        lax.all_gather(proj_weight, "fsdp", axis=1, tiled=True),
    )
    main_term = jnp.einsum("sd,jdc->jsc", seq_hidden, qkv_full, preferred_element_type=jnp.float32)
    low_in = jnp.einsum("sd,jdr->jsr", seq_hidden, first_q, preferred_element_type=jnp.float32)
    low_term = jnp.einsum(
        "jsr,jrc->jsc", low_in, second_q.astype(jnp.float32), precision=lax.Precision.HIGHEST
    )
    bias_rows = jnp.stack([qkv_bias[0], jnp.zeros_like(qkv_bias[0]), qkv_bias[1]]).astype(
        jnp.float32
    )[:, None, :]
    qkv_round = (main_term + low_term + bias_rows).astype(jnp.bfloat16)
    queries = qkv_round[0].reshape(seq_rows, heads_local, HEAD)
    keys = qkv_round[1].reshape(seq_rows, heads_local, HEAD)
    values = qkv_round[2].reshape(seq_rows, heads_local, HEAD)
    query_blocks = queries.reshape(blocks, block_rows, heads_local, HEAD)
    seg_blocks = segments.reshape(blocks, block_rows)

    def scores_of(query_rows, seg_rows):
        raw_scores = (
            jnp.einsum("bhe,she->hbs", query_rows, keys, preferred_element_type=jnp.float32)
            * score_scale
        )
        same_doc = (seg_rows[:, None] == segments[None, :])[None]
        return jnp.where(same_doc, raw_scores, -1e30)

    def forward_block(inputs):
        query_rows, seg_rows = inputs
        scores = scores_of(query_rows, seg_rows)
        row_top = jnp.max(scores, axis=-1, keepdims=True)
        weights = jnp.exp(scores - row_top)
        row_total = jnp.sum(weights, axis=-1, keepdims=True)
        attn_probs = (weights / row_total).astype(jnp.bfloat16)
        attn_mixed = jnp.einsum(
            "hbs,she->bhe", attn_probs, values, preferred_element_type=jnp.float32
        )
        return (attn_mixed, (row_top + jnp.log(row_total))[..., 0])

    attn_mixed, logsum = lax.map(forward_block, (query_blocks, seg_blocks))
    attended = attn_mixed.reshape(seq_rows, width_local).astype(jnp.bfloat16)
    low_attn = mixed_dot(attended, first_o)
    second_o_wide = second_o.astype(jnp.float32)
    row_part = attended
    low_part = low_attn
    attn_sum = lax.psum_scatter(
        mixed_dot(row_part, proj_full) + precise_dot(low_part, second_o_wide),
        "tp",
        scatter_dimension=0,
        tiled=True,
    )
    first_sum = hidden_in.astype(jnp.float32) + attn_sum + proj_bias.astype(jnp.float32)
    normed = layer_norm(first_sum, gains[0], shifts[0])
    normed_round = normed.astype(jnp.bfloat16)
    seq_normed = lax.all_gather(normed_round, "tp", axis=0, tiled=True)
    up_full, down_full = (
        lax.all_gather(up_weight, "fsdp", axis=0, tiled=True),
        lax.all_gather(down_weight, "fsdp", axis=1, tiled=True),
    )
    low_up = mixed_dot(seq_normed, first_u)
    pre_act = (
        mixed_dot(seq_normed, up_full)
        + precise_dot(low_up, second_u.astype(jnp.float32))
        + up_bias.astype(jnp.float32)
    )
    act_round = jax.nn.gelu(pre_act, approximate=True).astype(jnp.bfloat16)
    low_down = mixed_dot(act_round, first_d)
    second_d_wide = second_d.astype(jnp.float32)
    row_part = act_round
    low_part = low_down
    ffn_sum = lax.psum_scatter(
        mixed_dot(row_part, down_full) + precise_dot(low_part, second_d_wide),
        "tp",
        scatter_dimension=0,
        tiled=True,
    )
    second_sum = normed + ffn_sum + down_bias.astype(jnp.float32)
    layer_out = layer_norm(second_sum, gains[1], shifts[1])
    unused, norm_back = jax.vjp(
        lambda field_in: layer_norm(field_in, gains[1], shifts[1]), second_sum
    )
    grad_second = norm_back(cotangent.astype(jnp.float32))[0]
    grad_feed_round = grad_second.astype(jnp.bfloat16)
    seq_grad_feed = lax.all_gather(grad_feed_round, "tp", axis=0, tiled=True)
    up_back, down_back = (
        lax.all_gather(up_weight, "fsdp", axis=0, tiled=True),
        lax.all_gather(down_weight, "fsdp", axis=1, tiled=True),
    )
    grad_low_down = mixed_dot(seq_grad_feed, second_d.T)
    grad_act = jnp.einsum(
        "sd,fd->sf", seq_grad_feed, down_back, preferred_element_type=jnp.float32
    ) + precise_dot(grad_low_down, first_d.astype(jnp.float32).T)
    unused, gelu_back = jax.vjp(lambda field_in: jax.nn.gelu(field_in, approximate=True), pre_act)
    grad_pre_round = gelu_back(grad_act)[0].astype(jnp.bfloat16)
    grad_down_out_part = precise_dot(low_down.T, seq_grad_feed.astype(jnp.float32))
    grad_down_in_part = precise_dot(act_round.astype(jnp.float32).T, grad_low_down)
    grad_low_up = mixed_dot(grad_pre_round, second_u.T)
    grad_up_out_part = precise_dot(low_up.T, grad_pre_round.astype(jnp.float32))
    grad_up_in_part = precise_dot(seq_normed.astype(jnp.float32).T, grad_low_up)
    first_u_wide = first_u.astype(jnp.float32)
    row_part = grad_pre_round
    low_part = grad_low_up
    grad_normed = grad_second + lax.psum_scatter(
        jnp.einsum("sf,df->sd", row_part, up_back, preferred_element_type=jnp.float32)
        + precise_dot(low_part, first_u_wide.T),
        "tp",
        scatter_dimension=0,
        tiled=True,
    )
    unused, norm_front = jax.vjp(
        lambda field_in: layer_norm(field_in, gains[0], shifts[0]), first_sum
    )
    grad_first = norm_front(grad_normed)[0]
    grad_branch_round = grad_first.astype(jnp.bfloat16)
    seq_grad_branch = lax.all_gather(grad_branch_round, "tp", axis=0, tiled=True)
    qkv_back, proj_back = (
        lax.all_gather(qkv_weight, "fsdp", axis=1, tiled=True),
        lax.all_gather(proj_weight, "fsdp", axis=1, tiled=True),
    )
    grad_low_attn = mixed_dot(seq_grad_branch, second_o.T)
    grad_attended = jnp.einsum(
        "sd,cd->sc", seq_grad_branch, proj_back, preferred_element_type=jnp.float32
    ) + precise_dot(grad_low_attn, first_o.astype(jnp.float32).T)
    grad_attended_round = grad_attended.astype(jnp.bfloat16)
    grad_attn_out_part = precise_dot(low_attn.T, seq_grad_branch.astype(jnp.float32))
    grad_attn_in_part = precise_dot(attended.astype(jnp.float32).T, grad_low_attn)
    grad_blocks = grad_attended_round.reshape(blocks, block_rows, heads_local, HEAD)

    def backward_block(carry, inputs):
        grad_keys, grad_values = carry
        query_rows, seg_rows, lse_rows, grad_rows = inputs
        scores = scores_of(query_rows, seg_rows)
        attn_probs = jnp.exp(scores - lse_rows[..., None])
        grad_probs = jnp.einsum(
            "bhe,she->hbs", grad_rows, values, preferred_element_type=jnp.float32
        )
        centre = jnp.sum(grad_probs * attn_probs, axis=-1, keepdims=True)
        grad_scores = (attn_probs * (grad_probs - centre)).astype(jnp.bfloat16)
        grad_query = (
            jnp.einsum("hbs,she->bhe", grad_scores, keys, preferred_element_type=jnp.float32)
            * score_scale
        )
        grad_keys = (
            grad_keys
            + jnp.einsum(
                "hbs,bhe->she", grad_scores, query_rows, preferred_element_type=jnp.float32
            )
            * score_scale
        )
        grad_values = grad_values + jnp.einsum(
            "hbs,bhe->she",
            attn_probs.astype(jnp.bfloat16),
            grad_rows,
            preferred_element_type=jnp.float32,
        )
        return ((grad_keys, grad_values), grad_query)

    zero_state = jnp.zeros((seq_rows, heads_local, HEAD), jnp.float32)
    key_value_grads, grad_queries = lax.scan(
        backward_block, (zero_state, zero_state), (query_blocks, seg_blocks, logsum, grad_blocks)
    )
    grad_qkv_round = jnp.stack(
        [
            grad_queries.reshape(seq_rows, width_local),
            key_value_grads[0].reshape(seq_rows, width_local),
            key_value_grads[1].reshape(seq_rows, width_local),
        ]
    ).astype(jnp.bfloat16)
    grad_qkv_out_part = jnp.einsum(
        "jsr,jsc->jrc", low_in, grad_qkv_round.astype(jnp.float32), precision=lax.Precision.HIGHEST
    )
    grad_low_qkv = jnp.einsum(
        "jsc,jrc->jsr", grad_qkv_round, second_q, preferred_element_type=jnp.float32
    )
    grad_qkv_in_part = jnp.einsum(
        "sd,jsr->jdr", seq_hidden.astype(jnp.float32), grad_low_qkv, precision=lax.Precision.HIGHEST
    )
    first_q_wide = first_q.astype(jnp.float32)
    row_part = grad_qkv_round
    low_part = grad_low_qkv
    grad_input = grad_first + lax.psum_scatter(
        (
            jnp.einsum("jsc,jdc->sd", row_part, qkv_back, preferred_element_type=jnp.float32)
            + jnp.einsum("jsr,jdr->sd", low_part, first_q_wide, precision=lax.Precision.HIGHEST)
        ).astype(jnp.bfloat16),
        "tp",
        scatter_dimension=0,
        tiled=True,
    ).astype(jnp.float32)
    wide_grads = lax.psum(
        (
            place_set(grad_qkv_in_part, chosen, sets, 1),
            place_set(grad_attn_out_part, chosen, sets, 0),
            place_set(grad_up_in_part, chosen, sets, 0),
            place_set(grad_down_out_part, chosen, sets, 0),
        ),
        ("fsdp", "tp"),
    )
    split_grads = (
        lax.psum(place_set(grad_qkv_out_part, chosen, sets, 1).astype(jnp.bfloat16), "fsdp").astype(
            jnp.float32
        ),
        lax.psum(place_set(grad_attn_in_part, chosen, sets, 0).astype(jnp.bfloat16), "fsdp").astype(
            jnp.float32
        ),
        lax.psum(place_set(grad_up_out_part, chosen, sets, 0).astype(jnp.bfloat16), "fsdp").astype(
            jnp.float32
        ),
        lax.psum(place_set(grad_down_in_part, chosen, sets, 0).astype(jnp.bfloat16), "fsdp").astype(
            jnp.float32
        ),
    )
    return (
        layer_out,
        grad_input,
        wide_grads[0],
        split_grads[0],
        split_grads[1],
        wide_grads[1],
        wide_grads[2],
        split_grads[2],
        split_grads[3],
        wide_grads[3],
    )


def dot_nn(left, right):
    return jnp.dot(left, right, preferred_element_type=F32)


def dot_nt(left, right):
    return lax.dot_general(left, right, (((1,), (1,)), ((), ())), preferred_element_type=F32)


def flip(index, mask):
    out, bit = index, 1
    while bit <= mask:
        if mask & bit:
            out = out + bit - 2 * bit * lax.rem(lax.div(index, bit), 2)
        bit *= 2
    return out


def norm_parts(rows):
    centred = rows - jnp.mean(rows, axis=-1, keepdims=True)
    spread = jnp.mean(centred * centred, axis=-1, keepdims=True)
    rstd = lax.rsqrt(spread + 1e-05)
    return centred * rstd, rstd


def norm_pull(grad, unit, rstd):
    return rstd * (
        grad
        - jnp.mean(grad, axis=-1, keepdims=True)
        - unit * jnp.mean(grad * unit, axis=-1, keepdims=True)
    )


class Gather:
    def __init__(self, which, shard, whole, send, recv, fsdp, tp, count):
        self.which, self.shard, self.whole = which, shard, whole
        self.send, self.recv, self.fsdp, self.tp = send, recv, fsdp, tp
        bits = [1 << i for i in range(1, count.bit_length() - 1)]
        self.orders = [bits, bits[::-1]]
        self.steps = len(bits)
        self.held = [[0], [0]]
        self.sent = []
        self.count = count

    def copy(self, half, mask, bit):
        landed = mask ^ bit
        place = self.whole(flip(self.fsdp, mask), half)
        return pltpu.make_async_remote_copy(
            src_ref=self.shard(half) if mask == 0 else place,
            dst_ref=place,
            send_sem=self.send.at[self.which, half, landed],
            recv_sem=self.recv.at[self.which, half, landed],
            device_id=(flip(self.fsdp, bit), self.tp),
            device_id_type=MESH,
        )

    def launch(self, half, mask, bit):
        self.copy(half, mask, bit).start()
        self.sent.append((half, mask, bit))

    def await_block(self, half, mask, bit):
        place = self.whole(flip(self.fsdp, mask), half)
        pltpu.make_async_remote_copy(
            src_ref=place,
            dst_ref=place,
            send_sem=self.send.at[self.which, half, mask],
            recv_sem=self.recv.at[self.which, half, mask],
            device_id=(flip(self.fsdp, bit), self.tp),
            device_id_type=MESH,
        ).wait_recv()

    def stage(self, step):
        for half in range(2):
            fresh = [0]
            if step > 0:
                bit = self.orders[half][step - 1]
                fresh = [mask ^ bit for mask in self.held[half]]
                for mask in fresh:
                    self.await_block(half, mask, bit)
                self.held[half] = self.held[half] + fresh
            if step < self.steps:
                for mask in self.held[half]:
                    self.launch(half, mask, self.orders[half][step])
            for mask in fresh:
                self.launch(half, mask, 1)

    def finish(self):
        for half in range(2):
            for mask in self.held[half]:
                self.await_block(half, mask ^ 1, 1)

    def drain(self):
        for half, mask, bit in self.sent:
            self.copy(half, mask, bit).wait_send()


def layer_kernel(cfg, *refs):
    F, T, S, D, H, FL, C = (cfg[k] for k in ("F", "T", "S", "D", "H", "FL", "C"))
    Q, heads, block = S // T, H // HEAD, D // F
    R = Q // C
    M = T * R
    NT = math.gcd(FL, 512)
    (
        hidden_in, cotangent, segments, chosen, qkv_w, proj_w, up_w, down_w,
        proj_bias, down_bias, up_bias, qkv_bias, gains, shifts,
        q_in, q_out, o_in, o_out, u_in, u_out, d_in, d_out,
        layer_out, grad_input, feed_all, units_all, mix_all, heads_all,
        hidden, qkv_all, proj_all, up_all, down_all,
        qkv, probs, mixed, normed, act, slope, grad_feed, grad_branch, grad_mixed, grad_qkv,
        part, from_low, from_high, unit_one, rstd_one, grad_own,
        low_q, low_o, low_u, low_d, back_q, back_o, back_u, back_d,
        seg_row, seg_col, turned,
        wide_f, heads_f, units_f, wide_stage, heads_stage, units_stage,
        feed_part, feed_land, feed_full, mix_part, mix_land, mix_full, units_g, heads_g,
        stage_sem, deal_send, deal_recv,
        w_send, w_recv, up_send, up_recv, dn_send, dn_recv, g_up_send, g_up_recv, g_dn_send, g_dn_recv,
        own_sem,
    ) = refs
    grad_pre = slope
    f, z = lax.axis_index("fsdp"), lax.axis_index("tp")
    bits = [1 << i for i in range(F.bit_length() - 1)]

    barrier = pltpu.get_barrier_semaphore()
    for bit in bits:
        pl.semaphore_signal(barrier, inc=1, device_id=(flip(f, bit), z), device_id_type=MESH)

    turns = [lax.rem(z + k, T) for k in range(T)]
    for k in range(1, T):
        pl.semaphore_signal(barrier, inc=1, device_id=(f, turns[k]), device_id_type=MESH)
    pl.semaphore_wait(barrier, len(bits) + T - 1)

    rows_of = lambda total, half: pl.ds(half * (total // 2), total // 2)
    gathers = [
        Gather(0, lambda h: qkv_w.at[:, rows_of(block, h)], lambda g, h: qkv_all.at[:, g, rows_of(block, h)], w_send, w_recv, f, z, F),
        Gather(1, lambda h: proj_w.at[rows_of(H, h)], lambda g, h: proj_all.at[g, rows_of(H, h)], w_send, w_recv, f, z, F),
        Gather(2, lambda h: up_w.at[rows_of(block, h)], lambda g, h: up_all.at[g, rows_of(block, h)], w_send, w_recv, f, z, F),
    ]
    quarter = lambda part, h: pl.ds((2 * part + h) * (FL // 4), FL // 4)
    for part_of in range(2):
        shard = lambda h, p=part_of: down_w.at[quarter(p, h)]
        whole = lambda g, h, p=part_of: down_all.at[g, quarter(p, h)]
        gathers.append(Gather(3 + part_of, shard, whole, w_send, w_recv, f, z, F))
    pair = lambda ref, n: lambda h: ref.at[..., rows_of(n, h), :]
    pair_all = lambda ref, n: lambda g, h: ref.at[g, ..., rows_of(n, h), :]
    for k, (shard, whole) in enumerate(
        [(feed_full, feed_all), (units_g, units_all), (mix_full, mix_all), (heads_g, heads_all)]
    ):
        n = shard.shape[-2]
        gathers.append(Gather(5 + k, pair(shard, n), pair_all(whole, n), w_send, w_recv, f, z, F))
    K = gathers[0].steps
    own_copies = [
        pltpu.make_async_copy(hidden_in, hidden.at[:, z], own_sem.at[0]),
        pltpu.make_async_copy(qkv_w, qkv_all.at[:, f], own_sem.at[1]),
        pltpu.make_async_copy(proj_w, proj_all.at[f], own_sem.at[2]),
        pltpu.make_async_copy(up_w, up_all.at[f], own_sem.at[3]),
        pltpu.make_async_copy(down_w, down_all.at[f], own_sem.at[4]),
    ]
    own_grads = [
        pltpu.make_async_copy(feed_full, feed_all.at[f], own_sem.at[5]),
        pltpu.make_async_copy(units_g, units_all.at[f], own_sem.at[6]),
        pltpu.make_async_copy(mix_full, mix_all.at[f], own_sem.at[7]),
        pltpu.make_async_copy(heads_g, heads_all.at[f], own_sem.at[8]),
    ]

    def deal_copy(which, k):
        part_ref, land_ref = exchanges[which]
        return pltpu.make_async_remote_copy(
            src_ref=part_ref, dst_ref=land_ref.at[k - 1],
            send_sem=deal_send.at[which, k - 1], recv_sem=deal_recv.at[which, k - 1],
            device_id=(f, turns[k]), device_id_type=MESH,
        )

    exchanges = [(feed_part, feed_land), (mix_part, mix_land)]

    def deal(which):
        for k in range(1, T):
            deal_copy(which, k).start()

    def collect(which):
        part_ref, land_ref = exchanges[which]
        total = part_ref[...].astype(F32)
        for k in range(1, T):
            deal_copy(which, k).wait_recv()
            total += land_ref[k - 1].astype(F32)
        return total.astype(BF16)

    def pass_on(which):
        for k in (2 * which, 2 * which + 1):
            own_grads[k].start()
            gathers[5 + k].stage(0)

    def pass_drain(which):
        for k in range(1, T):
            deal_copy(which, k).wait_send()
        for k in (2 * which, 2 * which + 1):
            own_grads[k].wait()

    def line_copy(src, dst, send, recv, c, q, step):
        return pltpu.make_async_remote_copy(
            src_ref=src, dst_ref=dst, send_sem=send.at[c, q], recv_sem=recv.at[c, q],
            device_id=(f, z + step), device_id_type=MESH,
        )

    def rs_copy(c, q, step):
        landing, send, recv = (from_low, up_send, up_recv) if step > 0 else (from_high, dn_send, dn_recv)
        return line_copy(part.at[c, q], landing.at[c, q], send, recv, c, q, step)

    def rs_wait(c, q, step):
        landing, send, recv = (from_low, up_send, up_recv) if step > 0 else (from_high, dn_send, dn_recv)
        line_copy(landing.at[c, q], landing.at[c, q], send, recv, c, q, -step).wait_recv()

    def rs(c, t):
        def add(q, landing):
            part[c, q] = part[c, q] + landing[c, q]

        @pl.when(z <= t - 1)
        def _():
            q = T - t + z

            @pl.when(z > 0)
            def _():
                rs_wait(c, q, 1)
                add(q, from_low)

            rs_copy(c, q, 1).start()

        @pl.when(z >= T - t)
        def _():
            q = z - (T - t)

            @pl.when(z < T - 1)
            def _():
                rs_wait(c, q, -1)
                add(q, from_high)

            rs_copy(c, q, -1).start()

    def rs_end(c):
        @pl.when(z > 0)
        def _():
            rs_wait(c, z, 1)

        @pl.when(z < T - 1)
        def _():
            rs_wait(c, z, -1)

    def rs_sum(c, rows):
        terms = [ref[c, z, rows].astype(F32) for ref in (part, from_low, from_high)]
        return (terms[0] + terms[1]) + terms[2]

    def rs_drain(c):
        for q in range(T):
            if q > 0:

                @pl.when(z < q)
                def _(q=q):
                    rs_copy(c, q, 1).wait_send()

            if q < T - 1:

                @pl.when(z > q)
                def _(q=q):
                    rs_copy(c, q, -1).wait_send()

    def ag_copy(buffer, c, q, step):
        send, recv = (g_up_send, g_up_recv) if step > 0 else (g_dn_send, g_dn_recv)
        if c is None:
            return line_copy(buffer.at[:, q], buffer.at[:, q], send, recv, C, q, step)
        return line_copy(buffer.at[c, q], buffer.at[c, q], send, recv, c, q, step)

    def ag_wait(buffer, c, q, step):
        send, recv = (g_up_send, g_up_recv) if step > 0 else (g_dn_send, g_dn_recv)
        place = buffer.at[:, q] if c is None else buffer.at[c, q]
        line_copy(place, place, send, recv, C if c is None else c, q, -step).wait_recv()

    def ag(buffer, c, t):
        if t == 1:

            @pl.when(z < T - 1)
            def _():
                ag_copy(buffer, c, z, 1).start()

            @pl.when(z > 0)
            def _():
                ag_copy(buffer, c, z, -1).start()

            return

        @pl.when(z >= t - 1)
        def _():
            q = z - (t - 1)
            ag_wait(buffer, c, q, 1)

            @pl.when(z < T - 1)
            def _():
                ag_copy(buffer, c, q, 1).start()

        @pl.when(z <= T - t)
        def _():
            q = z + (t - 1)
            ag_wait(buffer, c, q, -1)

            @pl.when(z > 0)
            def _():
                ag_copy(buffer, c, q, -1).start()

    def ag_drain(buffer, c):
        for q in range(T):

            @pl.when((z >= q) & (z < T - 1))
            def _(q=q):
                ag_copy(buffer, c, q, 1).wait_send()

            @pl.when((z <= q) & (z > 0))
            def _(q=q):
                ag_copy(buffer, c, q, -1).wait_send()

    a_q = lambda j: wide_f.at[j]
    b_o, a_u, b_d = wide_f.at[3], wide_f.at[4], wide_f.at[5]
    b_q = lambda j: heads_f.at[j]
    a_o = heads_f.at[3]
    b_u, a_d = units_f.at[0], units_f.at[1]
    line = lambda ref, k: ref[pl.ds(k, 1)].astype(F32)
    flat = lambda ref: ref[...].reshape(1, ref.shape[0]).astype(F32)
    sets = q_in.shape[1]
    pick = (lax.broadcasted_iota(jnp.int32, (sets, 128), 0) == chosen[...]).astype(F32)

    def stage_copies(s):
        slot = s % 2
        pairs = [
            (q_in.at[:, s], wide_stage.at[slot, pl.ds(0, 3)]),
            (o_out.at[s], wide_stage.at[slot, 3]),
            (u_in.at[s], wide_stage.at[slot, 4]),
            (d_out.at[s], wide_stage.at[slot, 5]),
            (q_out.at[:, s], heads_stage.at[slot, pl.ds(0, 3)]),
            (o_in.at[s], heads_stage.at[slot, 3]),
            (u_out.at[s], units_stage.at[slot, 0]),
            (d_in.at[s], units_stage.at[slot, 1]),
        ]
        return [
            pltpu.make_async_copy(src, dst, stage_sem.at[slot, k])
            for k, (src, dst) in enumerate(pairs)
        ]

    def choose(s):
        for copy in stage_copies(s):
            copy.wait()
        weight = pick[s : s + 1, :1].astype(BF16)
        for stage, held in ((wide_stage, wide_f), (heads_stage, heads_f), (units_stage, units_f)):
            for k in range(held.shape[0]):
                term = stage[s % 2, k] * weight
                held[k] = term if s == 0 else held[k] + term
        if s + 2 < sets:
            for copy in stage_copies(s + 2):
                copy.start()

    def chunk(buffer, c, n, cols=slice(None)):
        rows = buffer[c : c + n, :, :, cols]
        return rows.reshape(n * M, rows.shape[-1])

    def cols_of(g, size):
        return pl.ds(pl.multiple_of(g * size, size), size)

    def project():
        width = math.gcd(H, 256)
        for j in range(3):
            low_j = dot_nt(hidden[...].reshape(S, D), a_q(j)[...]).astype(BF16)
            low_q[j] = low_j

            @pl.loop(0, H // width)
            def _(n, j=j, low_j=low_j):
                cols = cols_of(n, width)
                rows = dot_nn(hidden[...].reshape(S, D), qkv_all[j, :, :, cols].reshape(D, width))
                rows += dot_nn(low_j, b_q(j)[:, cols])
                if j != 1:
                    rows += qkv_bias[pl.ds(j // 2, 1), cols].astype(F32)
                qkv[j, :, cols] = rows.astype(BF16)

    scale = 1.0 / math.sqrt(HEAD)

    def mark_segments():
        row = segments[...].astype(F32)
        pieces = [row[:, q * Q + c * R : q * Q + c * R + R] for c in range(C) for q in range(T)]
        row = jnp.concatenate(pieces, axis=1)
        seg_row[...] = row
        seg_col[...] = jnp.broadcast_to(row, (128, S)).T

    def turn_heads(j):
        @pl.loop(0, heads)
        def _(h):
            turned[cols_of(h, HEAD)] = qkv[j, :, cols_of(h, HEAD)].T

    def attend(c):
        rows = pl.ds(c * M, M)

        @pl.loop(0, heads)
        def _(h):
            cols = cols_of(h, HEAD)
            scores = dot_nt(qkv[1, :, cols], qkv[0, rows, cols]) * scale
            scores = jnp.where(seg_col[:, :1] == seg_row[:, rows], scores, -1e30)
            weights = jnp.exp(scores - jnp.max(scores, axis=0, keepdims=True))
            low = (weights * (1.0 / jnp.sum(weights, axis=0, keepdims=True))).astype(BF16)
            probs[h, :, rows] = low
            mixed[rows, cols] = dot_nn(turned[cols], low).T.astype(BF16)

    def attend_back(c):
        rows = pl.ds(c * M, M)

        @pl.loop(0, heads)
        def _(h):
            cols = cols_of(h, HEAD)
            weights = probs[h, :, rows].astype(F32)
            grad = dot_nt(qkv[2, :, cols], grad_mixed[rows, cols])
            centre = jnp.sum(grad * weights, axis=0, keepdims=True)
            low = (weights * (grad - centre)).astype(BF16)
            grad_scores[:, pl.ds(pl.multiple_of(h * S + c * M, M), M)] = low
            grad_qkv[0, rows, cols] = (dot_nn(turned[cols], low).T * scale).astype(BF16)

    def attend_sums():
        @pl.loop(0, heads)
        def _(h):
            cols = cols_of(h, HEAD)
            low = grad_scores[:, cols_of(h, S)]
            grad_qkv[1, :, cols] = (dot_nn(low, qkv[0, :, cols]) * scale).astype(BF16)
            grad_qkv[2, :, cols] = dot_nn(probs[h], grad_mixed[:, cols]).astype(BF16)

    grad_scores = slope

    def span(c, n):
        return pl.ds(c * M, n * M)

    def put_part(c, n, cols, rows):
        part[c : c + n, :, :, cols] = rows.astype(BF16).reshape(n, T, R, rows.shape[-1])

    group = math.gcd(F, 2)

    def by_blocks(body):
        @pl.loop(0, F // group)
        def _(turn):
            for k in range(group):
                g = turn * group + k
                body(g, cols_of(g, block))

    def mix_out(c, n):
        low = dot_nt(mixed[span(c, n)], a_o[...]).astype(BF16)
        low_o[span(c, n)] = low

        @by_blocks
        def _(g, cols):
            put_part(c, n, cols, dot_nn(mixed[span(c, n)], proj_all[g]) + dot_nn(low, b_o[:, cols]))

    def feed_up(c, n):
        low = dot_nt(chunk(normed, c, n), a_u[...]).astype(BF16)
        low_u[span(c, n)] = low

        @pl.loop(0, FL // NT)
        def _(turn):
            cols = cols_of(turn, NT)
            pre = dot_nn(chunk(normed, c, n), up_all[:, :, cols].reshape(D, NT))
            pre += dot_nn(low, b_u[:, cols]) + up_bias[cols].reshape(1, NT).astype(F32)
            square = pre * pre
            bend = jnp.tanh(ROOT * (pre + 0.044715 * square * pre))
            half = 0.5 * (1.0 + bend)
            act[span(c, n), cols] = (pre * half).astype(BF16)
            rise = half + 0.5 * pre * (1.0 - bend * bend) * (ROOT * (1.0 + 3 * 0.044715 * square))
            slope[span(c, n), cols] = rise.astype(BF16)

    def feed_down(c, n):
        low = dot_nt(act[span(c, n)], a_d[...]).astype(BF16)
        low_d[span(c, n)] = low

        @by_blocks
        def _(g, cols):
            put_part(c, n, cols, dot_nn(act[span(c, n)], down_all[g]) + dot_nn(low, b_d[:, cols]))

    def back_down(c, n):
        low = dot_nt(chunk(grad_feed, c, n), b_d[...]).astype(BF16)
        back_d[span(c, n)] = low

        @pl.loop(0, FL // NT)
        def _(turn):
            cols = cols_of(turn, NT)
            total = dot_nn(low, a_d[:, cols])
            for g in range(F):
                total += dot_nt(chunk(grad_feed, c, n, pl.ds(g * block, block)), down_all[g, cols])
            grad_pre[span(c, n), cols] = (total * slope[span(c, n), cols].astype(F32)).astype(BF16)

    def back_up(c, n):
        low = dot_nt(grad_pre[span(c, n)], b_u[...]).astype(BF16)
        back_u[span(c, n)] = low

        @by_blocks
        def _(g, cols):
            put_part(c, n, cols, dot_nt(grad_pre[span(c, n)], up_all[g]) + dot_nn(low, a_u[:, cols]))

    def back_mix(c, n):
        low = dot_nt(chunk(grad_branch, c, n), b_o[...]).astype(BF16)
        back_o[span(c, n)] = low
        total = dot_nn(low, a_o[...])
        for g in range(F):
            total += dot_nt(chunk(grad_branch, c, n, pl.ds(g * block, block)), proj_all[g])
        grad_mixed[span(c, n)] = total.astype(BF16)

    def back_project(c, n):
        lows = [back_q[j, span(c, n)] for j in range(3)]

        @by_blocks
        def _(g, cols):
            total = dot_nn(lows[0], a_q(0)[:, cols])
            for j in range(3):
                if j:
                    total += dot_nn(lows[j], a_q(j)[:, cols])
                total += dot_nt(grad_qkv[j, span(c, n)], qkv_all[j, g])
            put_part(c, n, cols, total)

    def by_rows(body):
        def all_rows(c):
            rs_end(c)

            @pl.loop(0, R // 16)
            def _(k):
                body(c, cols_of(k, 16), pl.ds(pl.multiple_of(c * R + k * 16, 16), 16))

        return all_rows

    @by_rows
    def meet_one(c, rows, own):
        total = rs_sum(c, rows) + hidden[c, z, rows].astype(F32) + flat(proj_bias)
        unit, rstd = norm_parts(total)
        unit_one[own] = unit
        rstd_one[own] = jnp.broadcast_to(rstd, (16, 128))
        normed[c, z, rows] = (unit * line(gains, 0) + line(shifts, 0)).astype(BF16)

    @by_rows
    def meet_two(c, rows, own):
        total = rs_sum(c, rows) + unit_one[own] * line(gains, 0) + line(shifts, 0) + flat(down_bias)
        unit, rstd = norm_parts(total)
        layer_out[own] = unit * line(gains, 1) + line(shifts, 1)
        grad = norm_pull(cotangent[own].astype(F32) * line(gains, 1), unit, rstd)
        grad_own[own] = grad
        grad_feed[c, z, rows] = grad.astype(BF16)

    @by_rows
    def meet_three(c, rows, own):
        grad = (grad_own[own] + rs_sum(c, rows)) * line(gains, 0)
        grad = norm_pull(grad, unit_one[own], rstd_one[own][:, :1])
        grad_own[own] = grad
        grad_branch[c, z, rows] = grad.astype(BF16)

    @by_rows
    def meet_four(c, rows, own):
        grad_input[own] = grad_own[own] + rs_sum(c, rows)

    def turn_rows(low):
        return low.astype(F32).T.astype(BF16)

    def factor(low, right):
        return dot_nn(turn_rows(low[...]), right).astype(BF16)

    def by_columns(rows, right, place, row):
        count = rows.shape[0]

        @pl.loop(0, T)
        def _(q):
            cols = cols_of(q, H)
            place[pl.ds(row, count), cols] = dot_nn(rows, right[:, :, :, cols].reshape(S, H)).astype(BF16)

    def rows_feed():
        feed_part[pl.ds(0, 16)] = turn_rows(back_u[...])
        feed_part[pl.ds(16, 16)] = turn_rows(low_d[...])

    def units_feed():
        units_g[pl.ds(0, 16)] = factor(low_u, grad_pre[...])
        units_g[pl.ds(16, 16)] = factor(back_d, act[...])

    def wide_feed():
        rows = collect(0)
        by_columns(rows[:16], normed, feed_full, 0)
        by_columns(rows[16:], grad_feed, feed_full, 16)

    def rows_mix():
        for j in range(3):
            low = dot_nt(grad_qkv[j], b_q(j)[...]).astype(BF16)
            back_q[j] = low
            mix_part[pl.ds(16 * j, 16)] = turn_rows(low)
        mix_part[pl.ds(48, 16)] = turn_rows(low_o[...])

    def heads_mix():
        heads_g[pl.ds(48, 16)] = factor(back_o, mixed[...])
        for j in range(3):
            heads_g[pl.ds(16 * j, 16)] = factor(low_q.at[j], grad_qkv[j])
        marks = jnp.concatenate([pick[:, :1], jnp.zeros((32 - sets, 1), F32)])
        heads_g[pl.ds(64, 32)] = jnp.broadcast_to(marks, (32, H)).astype(BF16)

    def wide_mix():
        rows = collect(1)
        by_columns(rows[:48], hidden, mix_full, 0)
        by_columns(rows[48:], grad_branch, mix_full, 48)

    from_low[:, 0] = jnp.zeros((C, R, D), BF16)
    from_high[:, T - 1] = jnp.zeros((C, R, D), BF16)
    qkv_g = gathers[0]
    def own_hidden(step):
        return line_copy(hidden_in, hidden.at[:, z], g_up_send if step > 0 else g_dn_send, g_up_recv if step > 0 else g_dn_recv, C, z, step)

    @pl.when(z < T - 1)
    def _():
        own_hidden(1).start()

    @pl.when(z > 0)
    def _():
        own_hidden(-1).start()

    qkv_g.stage(0)
    for copy in own_copies + stage_copies(0) + stage_copies(1):
        copy.start()
    schedule(cfg, dict(locals()))


def schedule(cfg, env):
    T, C, K = cfg["T"], cfg["C"], env["K"]
    rs, ag, hidden = env["rs"], env["ag"], env["hidden"]
    qkv_g, proj_g, up_g, down_g, rest_g = env["gathers"][:5]
    env["mark_segments"]()
    for s in range(2):
        env["choose"](s)
    for step in range(1, K + 1):
        qkv_g.stage(step)
        if step == 1:
            proj_g.stage(0)
            ag(hidden, None, 2)
            for s in range(2, 5):
                env["choose"](s)
    if K == 0:
        proj_g.stage(0)
    if K >= 1:
        proj_g.stage(1)
    up_g.stage(0)
    if K < 1:
        ag(hidden, None, 2)
        for s in range(2, 5):
            env["choose"](s)
    for s in range(5, env["sets"]):
        env["choose"](s)
    for t in range(3, T + 1):
        ag(hidden, None, t)
    for step in range(2, K + 1):
        proj_g.stage(step)
    down_g.stage(0)
    rest_g.stage(0)
    qkv_g.finish()
    for copy in env["own_copies"]:
        copy.wait()
    env["project"]()
    env["turn_heads"](2)
    if K:
        up_g.stage(1)
    proj_g.finish()
    buffers = [env["normed"], env["grad_feed"], env["grad_branch"]]
    meets = [env["meet_one"], env["meet_two"], env["meet_three"], env["meet_four"]]

    def start_sum(chunks):
        for c in chunks:
            rs(c, 1)

    def work(kind, k, first, n):
        group = range(first, first + n)
        if kind == "mix" or k in (1, 2):
            for c in group:
                ag(buffers[k - 1], c, T)
        if kind == "mix":
            env["back_mix"](first, n)
            for c in group:
                env["attend_back"](c)
            return
        if k > 0:
            for c in group:
                env["rs_drain"](c)
        if k == 0:
            for c in group:
                env["attend"](c)
            if first + n == C:
                env["turn_heads"](1)
            env["mix_out"](first, n)
        if k == 1:
            if first == 0:
                up_g.finish()
            env["feed_up"](first, n)
            if first == 0:
                for gather in (down_g, rest_g):
                    for step in range(2, K + 1):
                        gather.stage(step)
                down_g.finish()
                rest_g.finish()
            env["feed_down"](first, n)
        if k == 2:
            env["back_down"](first, n)
            env["back_up"](first, n)
        if k == 3:
            env["back_project"](first, n)
        start_sum(group)
        if k == 2 and first + n == C:
            env["rows_feed"]()
            env["deal"](0)
            env["units_feed"]()

    def meet(k, c):
        if T > 2:
            rs(c, T - 1)
        meets[k](c)
        if k > 0:
            env["ag_drain"](buffers[k - 1], c)
        ag(buffers[k], c, 1)

    steps = []
    for k in range(3):
        steps += [("work", k, 0)] + [("rs", k, t) for t in range(2, T - 1)] + [("meet", k, 0)]
        steps += [("ag", k, t) for t in range(2, T)]
    steps.append(("mix", 3, 0))
    groups, at, came, turn = cfg["groups"], [0] * C, {}, 0
    while min(at) < len(steps):
        if turn == 1 and K:
            down_g.stage(1)
            rest_g.stage(1)
        if turn == cfg["up_turn"]:
            for step in range(2, K + 1):
                up_g.stage(step)
        for c in range(C):
            if turn < cfg["lag"] * c or at[c] == len(steps):
                continue
            kind, k, t = steps[at[c]]
            if kind in ("work", "mix"):
                n = groups[k]
                first = c // n * n
                came.setdefault((kind, k, first), set()).add(c)
                if len(came[kind, k, first]) < n:
                    continue
                work(kind, k, first, n)
                for member in range(first, first + n):
                    at[member] += 1
                continue
            if kind == "rs":
                rs(c, t)
            if kind == "meet":
                meet(k, c)
            if kind == "ag":
                ag(buffers[k], c, t)
            at[c] += 1
        turn += 1
    env["attend_sums"]()
    env["rows_mix"]()
    env["deal"](1)
    n, grads = groups[4], env["gathers"][5:]
    for c in range(0, C, n):
        work("work", 3, c, n)

    def shade(piece):
        if piece == 0:
            env["wide_feed"]()
            env["pass_on"](0)
        if piece == 1:
            env["heads_mix"]()
            env["wide_mix"]()
            env["pass_on"](1)
        if piece == 2 and K:
            for gather in grads:
                gather.stage(1)

    hops = [(c, t) for t in range(2, T) for c in range(C)]
    at_hop = [min(len(hops), share) for share in (C // 2, C, C + C // 2)]
    for i in range(len(hops) + 1):
        for piece in range(3):
            if at_hop[piece] == i:
                shade(piece)
        if i < len(hops):
            rs(*hops[i])
    for c in range(C):
        meets[3](c)
        if c == C // 2:
            for step in range(2, K + 1):
                for gather in grads:
                    gather.stage(step)
    for gather in grads:
        gather.finish()
    for c in range(C):
        env["rs_drain"](c)
        env["ag_drain"](buffers[2], c)
    env["ag_drain"](hidden, None)
    for which in range(2):
        env["pass_drain"](which)
    for gather in env["gathers"]:
        gather.drain()


def spread(mesh, body):
    placed = (
        P(("fsdp", "tp"), None),
        P(("fsdp", "tp"), None),
        P("fsdp", None),
        P("fsdp"),
        P(None, "fsdp", "tp"),
        P(None, "tp"),
        P("tp", "fsdp"),
        P(),
        P("fsdp", "tp"),
        P("tp"),
        P("tp", "fsdp"),
        P(),
        P(),
        P(),
        P(),
        P(None, None, None, "tp"),
        P(None, "tp", None),
        P(),
        P(),
        P(None, None, "tp"),
        P(None, "tp", None),
        P(),
    )
    return jax.shard_map(
        body,
        mesh=mesh,
        in_specs=placed,
        out_specs=(
            P(("fsdp", "tp"), None),
            P(("fsdp", "tp"), None),
            P(),
            P(None, None, None, "tp"),
            P(None, "tp", None),
            P(),
            P(),
            P(None, None, "tp"),
            P(None, "tp", None),
            P(),
        ),
        check_vma=False,
    )


def chunks_for(rows):
    return max(c for c in (1, 2, 4) if rows % (16 * c) == 0)


def place_kernel(layer_in, grad_in, feed_in, units_in, mix_in, heads_in, layer_out, grad_out, *refs):
    outs, tables = refs[:8], refs[8:16]
    feed_all, units_all, mix_all, heads_all, rows_a, rows_b, chosen, sems = refs[16:]
    F = feed_all.shape[0]
    sets = outs[2].shape[0]
    loads = [(heads_in, heads_all), (feed_in, feed_all), (units_in, units_all), (mix_in, mix_all)]
    loads += [(layer_in, rows_a), (grad_in, rows_b)]
    loads = [pltpu.make_async_copy(a, b, sems.at[k]) for k, (a, b) in enumerate(loads)]
    stores = list(zip(tables, outs)) + [(rows_a, layer_out), (rows_b, grad_out)]
    stores = [pltpu.make_async_copy(a, b, sems.at[6 + k]) for k, (a, b) in enumerate(stores)]
    for copy in loads:
        copy.start()
    order = lax.broadcasted_iota(jnp.int32, (32, 1), 0).astype(F32)
    q_in, q_out, o_in, o_out, u_in, u_out, d_in, d_out = range(8)
    loads[0].wait()
    for g in range(F):
        marks = heads_all[g, pl.ds(64, 32), pl.ds(0, 128)][:, :1].astype(F32)
        chosen[g] = jnp.clip(jnp.sum(marks * order).astype(jnp.int32), 0, sets - 1)

    def fill(which, rows_of):
        ref = tables[which]
        ref[...] = jnp.zeros_like(ref)

        @pl.loop(0, F)
        def _(g):
            rows_of(ref, g, chosen[g])

        stores[which].start()

    def whole(source, row):
        def add(ref, g, s):
            ref[s] += source[g, pl.ds(row, 16)].astype(F32)

        return add

    def trio(add_of):
        def add(ref, g, s):
            for j in range(3):
                add_of(16 * j)(ref.at[j], g, s)

        return add

    fill(q_out, trio(lambda row: whole(heads_all, row)))
    fill(o_in, whole(heads_all, 48))
    loads[1].wait()
    fill(u_in, whole(feed_all, 0))
    fill(d_out, whole(feed_all, 16))
    loads[2].wait()
    fill(u_out, whole(units_all, 0))
    fill(d_in, whole(units_all, 16))
    loads[3].wait()
    fill(o_out, whole(mix_all, 48))
    fill(q_in, trio(lambda row: whole(mix_all, row)))
    for copy in loads[4:]:
        copy.wait()
    for copy in stores[8:]:
        copy.start()
    for copy in stores:
        copy.wait()


def kernel_per_device(F, T):
    def per_device(
        hidden_in, cotangent, segment_ids, adapter_set, qkv_weight, qkv_bias, proj_weight, proj_bias,
        up_weight, up_bias, down_weight, down_bias, norm_gain, norm_bias, qkv_adapt_in, qkv_adapt_out,
        attn_adapt_in, attn_adapt_out, up_adapt_in, up_adapt_out, down_adapt_in, down_adapt_out,
    ):
        Q, D = hidden_in.shape
        H, FL = qkv_weight.shape[2], up_weight.shape[1]
        S, C, sets = Q * T, chunks_for(Q), qkv_adapt_in.shape[1]
        R, block = Q // C, D // F
        cfg = dict(F=F, T=T, S=S, D=D, H=H, FL=FL, C=C, lag=1, groups=(1, 1, 1, 1, 1), up_turn=T + 1)
        turn = lambda table: jnp.swapaxes(table, -1, -2)
        vmem, anywhere = pl.BlockSpec(memory_space=pltpu.VMEM), pl.BlockSpec(memory_space=pl.ANY)
        dma = pltpu.SemaphoreType.DMA
        bank = lambda *shape: pltpu.VMEM(shape, BF16)
        wide_bank = lambda *shape: pltpu.VMEM(shape, F32)
        scratch = (
            [bank(C, T, R, D), bank(3, F, block, H), bank(F, H, block), bank(F, block, FL), bank(F, FL, block)]
            + [bank(3, S, H), bank(H // HEAD, S, S), bank(S, H), bank(C, T, R, D), bank(S, FL), bank(S, FL)]
            + [bank(C, T, R, D), bank(C, T, R, D), bank(S, H), bank(3, S, H)]
            + [bank(C, T, R, D), bank(C, T, R, D), bank(C, T, R, D)]
            + [wide_bank(Q, D), wide_bank(Q, 128), wide_bank(Q, D)]
            + [bank(3, S, RANK), bank(S, RANK), bank(S, RANK), bank(S, RANK)] * 2
            + [wide_bank(1, S), wide_bank(S, 128), bank(H, S)]
            + [bank(6, RANK, D), bank(4, RANK, H), bank(2, RANK, FL)]
            + [bank(2, 6, RANK, D), bank(2, 4, RANK, H), bank(2, 2, RANK, FL)]
            + [bank(32, S), bank(T - 1, 32, S), bank(32, D)]
            + [bank(64, S), bank(T - 1, 64, S), bank(64, D)]
            + [bank(32, FL), bank(96, H)]
            + [dma((2, 8))] + [dma((2, T - 1))] * 2
            + [dma((9, 2, F)), dma((9, 2, F))]
            + [dma((C, T))] * 4
            + [dma((C + 1, T))] * 4
            + [dma((9,))]
        )
        flops = 2 * S * (4 * D * H + 2 * D * FL) * 2
        outs = pl.pallas_call(
            functools.partial(layer_kernel, cfg),
            out_shape=[
                jax.ShapeDtypeStruct((Q, D), F32),
                jax.ShapeDtypeStruct((Q, D), F32),
                jax.ShapeDtypeStruct((F, 32, D), BF16),
                jax.ShapeDtypeStruct((F, 32, FL), BF16),
                jax.ShapeDtypeStruct((F, 64, D), BF16),
                jax.ShapeDtypeStruct((F, 96, H), BF16),
            ],
            in_specs=[anywhere] + [vmem] * 3 + [anywhere] * 4 + [vmem] * 6 + [anywhere] * 8,
            out_specs=[vmem] * 2 + [anywhere] * 4,
            scratch_shapes=scratch,
            compiler_params=pltpu.CompilerParams(
                collective_id=0, has_side_effects=True, vmem_limit_bytes=62 * 1024 * 1024
            ),
            cost_estimate=pl.CostEstimate(flops=flops, bytes_accessed=30000000, transcendentals=0),
        )(
            hidden_in.reshape(C, R, D), cotangent, segment_ids, adapter_set[None, :],
            qkv_weight, proj_weight, up_weight, down_weight,
            proj_bias, down_bias, up_bias, qkv_bias, norm_gain, norm_bias,
            turn(qkv_adapt_in), qkv_adapt_out, turn(attn_adapt_in), attn_adapt_out,
            turn(up_adapt_in), up_adapt_out, turn(down_adapt_in), down_adapt_out,
        )
        shapes = [
            (3, sets, RANK, D), (3, sets, RANK, H), (sets, RANK, H), (sets, RANK, D),
            (sets, RANK, D), (sets, RANK, FL), (sets, RANK, FL), (sets, RANK, D),
        ]
        table = lambda *shape: jax.ShapeDtypeStruct(shape, F32)
        layer_out, grad_input, q_in, q_out, o_in, o_out, u_in, u_out, d_in, d_out = pl.pallas_call(
            place_kernel,
            out_shape=[table(Q, D), table(Q, D)] + [table(*shape) for shape in shapes],
            in_specs=[anywhere] * 6,
            out_specs=[anywhere] * 10,
            scratch_shapes=[wide_bank(*shape) for shape in shapes]
            + [bank(*out.shape) for out in outs[2:]]
            + [wide_bank(Q, D), wide_bank(Q, D), pltpu.SMEM((F,), jnp.int32), dma((16,))],
            compiler_params=pltpu.CompilerParams(vmem_limit_bytes=62 * 1024 * 1024),
        )(*outs)
        return (
            layer_out, grad_input, turn(q_in), q_out, turn(o_in), o_out, turn(u_in), u_out, turn(d_in), d_out,
        )

    return per_device


def solution(mesh):
    F, T = mesh.shape["fsdp"], mesh.shape["tp"]

    def whole(*args):
        width = args[0].shape[1]
        fits = F & (F - 1) == 0 and (width // F) % 128 == 0 and T > 1 and F > 1 and args[14].shape[1] <= 32 and width // T * args[2].shape[1] <= args[8].shape[1] // T * HEAD
        return spread(mesh, kernel_per_device(F, T) if fits else per_device)(*args)

    return whole
```
